32 devices in a mesh: req: 8 (over z, y), exp: 4 (over x, core).
Axes of the slice: x: 2, y: 2, z: 4, core: 2. Of those that a mesh axis runs over, the one named last changes fastest.
Arguments:
- hidden_in: bfloat16 [2048, 2048], P(('req', 'exp')), may hold values from -6 to 6
- query_in: bfloat16 [2048, 2048], P('req', 'exp'), may hold values from -6 to 6
- key_in: bfloat16 [2048, 2048], P('req', 'exp'), may hold values from -6 to 6
- value_in: bfloat16 [2048, 2048], P('req', 'exp'), may hold values from -24 to 24
- query_gain: float32 [128], replicated, may hold values from 0.5 to 2.5
- key_gain: float32 [128], replicated, may hold values from 0.5 to 2.5
- cache_keys: bfloat16 [16, 32, 2048], P('req', None, 'exp'), may hold values from -400 to 400
- cache_values: bfloat16 [16, 32, 2048], P('req', None, 'exp'), may hold values from -24 to 24
- cache_block: int32 [32], replicated, may hold values from -1 to 15, as said below
- request_lengths: int32 [8, 4], P('req'), may hold values from 1 to 128, 256 in all within a row
- out_proj: bfloat16 [2048, 2048], P('exp'), may hold values from -0.125 to 0.125
- norm_gain: float32 [2048], replicated, may hold values from 0.25 to 1.75
- expert_ids: int32 [2048, 8], P(('req', 'exp')), may hold values from 0 to 15, all different within a row; in each aligned block of 64 rows (0 to 63, 64 to 127, ...) at most 40 rows name the same one
- gate_values: float32 [2048, 8], P(('req', 'exp')), may hold values from 0.4 to 1.6
- old_slots: int32 [16], replicated, may hold values from 0 to 15, each once
- new_replicas: int32 [8], replicated, may hold values from 0 to 15
- slot_weights: bfloat16 [16, 3, 2048, 1024], P('req', None, None, 'exp'), may hold values from -0.125 to 0.125
Outputs:
- layer_out: bfloat16 [2048, 2048], P(('req', 'exp'))
- replica_weights: bfloat16 [8, 3, 2048, 1024], P('req', None, None, 'exp')
The draws below stay inside these ranges and needn't reach their ends.
Inputs may be any that keep to these rules, and one draw needn't show every extreme that they name: `cache_block`: each index of req has exactly 2 of its 4 requests with a block; every block serves exactly one request. `expert_ids`: in each aligned block of 64 rows (the rows of one device) no expert is named by more than 40 rows, a bound that some block reaches; the 8 experts of a row differ. `old_slots`: every expert is in exactly one slot. `request_lengths`: the lengths of each index of req sum to 256.
All inputs are finite; a program needn't handle non-finite values.
Results may differ from the reference program's by a relative error of at most 0.025.
Values may be sent and summed in bfloat16 or wider, within the bound.
No kernel may reach another device: no remote copies, remote signals or barrier semaphores. Data moves between devices by JAX's collectives and lax.ppermute only.
A program may use at most 128 MiB of HBM per device.

```python
import math
import jax
import jax.numpy as jnp
import numpy as np
from jax import lax

D = 2048
HEADS = 16
HEAD_DIM = 128
FF = 1024
TOPK = 8
REQ_GRP = 4
CACHE_DEV = 2
PRE = 32
TOK_DEV = 64
TOK_GRP = 256
TOKENS = 2048
EXPERTS = 16
MOST = 40
N_REQ = 8
N_EXP = 4


def draw_cache_block(key, part):
    first_key, second_key = jax.random.split(jax.random.fold_in(key, 17))
    orders = jax.vmap(lambda one_key: jax.random.permutation(one_key, REQ_GRP))(jax.random.split(first_key, N_REQ))
    cached = (orders < CACHE_DEV).reshape(-1)
    rank = jnp.cumsum(cached.astype(jnp.int32)) - 1
    blocks = jax.random.permutation(second_key, N_REQ * CACHE_DEV).astype(jnp.int32)
    chosen = jnp.take(blocks, jnp.maximum(rank, 0))
    return jnp.where(cached, chosen, -1).astype(jnp.int32)


def draw_cache_keys(key, part):
    first_key, second_key, third_key, fourth_key = jax.random.split(jax.random.fold_in(key, 29), 4)
    block_count = N_REQ * CACHE_DEV
    block_shape = (block_count, PRE, HEADS * HEAD_DIM)
    background = 1.5 * jax.random.truncated_normal(first_key, -6.0, 6.0, block_shape, jnp.float32)
    strength = jnp.exp(jax.random.uniform(second_key, (block_count, 1, 1), jnp.float32, math.log(20.0), math.log(60.0)))
    leading = strength * jax.random.truncated_normal(third_key, -4.0, 4.0, (block_count, 1, HEADS * HEAD_DIM), jnp.float32)
    nudging = 1.5 * jax.random.truncated_normal(fourth_key, -4.0, 4.0, (block_count, 1, HEADS * HEAD_DIM), jnp.float32)
    row_index = jnp.arange(PRE, dtype=jnp.int32)[None, :, None]
    planted = jnp.where(row_index == 0, leading, jnp.where(row_index == 1, leading + nudging, background))
    return jnp.clip(planted, -400.0, 400.0).astype(jnp.bfloat16)


def with_ends(drawn, rng, least, high):
    dims = drawn.shape
    spot = [jax.random.randint(jax.random.fold_in(rng, axis), (), 0, dims[axis]) for axis in range(len(dims))]
    drawn = drawn.at[tuple(spot)].set(least)
    longest = dims.index(max(dims))
    spot[longest] = (spot[longest] + 1) % dims[longest]
    return drawn.at[tuple(spot)].set(high)


def shard_levels(key, shape, cuts, low, largest):
    loudness = 1.0
    for dim, blocks in cuts:
        heights = jax.random.uniform(jax.random.fold_in(jax.random.fold_in(key, 6), dim), (blocks,), jnp.float32, low / len(cuts), largest / len(cuts))
        loudness = loudness * jnp.repeat(jnp.exp(heights), shape[dim] // blocks).reshape((-1,) + (1,) * (len(shape) - 1 - dim))
    return loudness


def profile(number_of, total, bound, slope):
    loads = [(1 << 20) // math.isqrt(standing ** slope) + 1 for standing in range(2, number_of + 1)]
    surplus, given = total - bound - (number_of - 1), [1] * (number_of - 1)
    while surplus > 0:
        candidates = [i for i in range(number_of - 1) if given[i] < bound]
        mass, budget = sum([loads[i] for i in candidates]), surplus
        for i in candidates:
            more = min(bound - given[i], max(1, budget * loads[i] // mass), surplus)
            given[i] = given[i] + more
            surplus = surplus - more
    return np.array([bound] + given)


def ragged_sizes(rng, amount, total, limit, skew):
    if amount == 2:
        one = jax.random.randint(rng, (), max(1, total - limit), min(limit, total - 1) + 1)
        return jnp.stack([one, total - one])
    sizes = jnp.asarray(profile(amount, total, limit, skew), jnp.int32)
    couples = (amount - 1) // 2
    giver, receiver = sizes[1:1 + 2 * couples:2], sizes[2:2 + 2 * couples:2]
    margin = jnp.minimum(giver - 1, limit - receiver)
    moved = jax.random.randint(jax.random.fold_in(rng, 1), (couples,), 0, 1 << 20) % (margin + 1)
    sizes = sizes.at[1:1 + 2 * couples:2].set(giver - moved).at[2:2 + 2 * couples:2].set(receiver + moved)
    return sizes[jax.random.permutation(jax.random.fold_in(rng, 2), amount)]


def assign_block(key, own, number, rows, amount, top, limit, slope):
    ranking = jax.random.permutation(key, amount)
    heavy_load, usual = load_shares(amount, rows * top, limit, slope, True), load_shares(amount, rows * top, limit, slope, False)
    places = jnp.arange(amount)

    def named(sizes, offset_by):
        used = int((sizes > 0).sum())
        fixed = max(1, used // 4)
        moved = fixed + (places - fixed + offset_by * (used - fixed)) % max(1, amount - fixed)
        return jnp.zeros((amount,), jnp.int32).at[ranking[jnp.where(places < fixed, places, moved)]].set(jnp.asarray(sizes, jnp.int32))

    sizes = jnp.where(number % 4 == 0, named(heavy_load, number // 4), named(usual, number - number // 4 - 1))
    mixed = jax.random.permutation(jax.random.fold_in(own, 3), amount)
    giver, receiver = mixed[0:amount // 2 * 2:2], mixed[1:amount // 2 * 2:2]
    room = jnp.minimum(sizes[giver] - 1, limit - sizes[receiver]) // 2
    room = jnp.where((giver == ranking[0]) | (receiver == ranking[0]) | (sizes[receiver] == 0), 0, jnp.maximum(room, 0))
    moved = jax.random.randint(jax.random.fold_in(own, 4), (amount // 2,), 0, 1 << 20) % (room + 1)
    sizes = sizes.at[giver].add(-moved).at[receiver].add(moved)
    members = jnp.searchsorted(jnp.cumsum(sizes), jnp.arange(rows * top), side="right").astype(jnp.int32)
    listing = members.reshape(top, rows).T
    listing = listing[jax.random.permutation(jax.random.fold_in(own, 1), rows)]
    offset_by = jax.random.randint(jax.random.fold_in(own, 2), (rows, 1), 0, top)
    return jnp.take_along_axis(listing, (jnp.arange(top)[None, :] + offset_by) % top, axis=1)


def load_shares(amount, total, most, lean, full):
    portions = [(1 << 20) // math.isqrt(grade ** lean) + 1 for grade in range(1, amount + 1)]
    largest = most if full else min(most, max(-(-total // amount), total * portions[0] // sum(portions)))
    least = 1 if total - largest >= amount - 1 else 0
    given, spare = [largest] + [least] * (amount - 1), total - largest - least * (amount - 1)
    while spare > 0:
        movable = [i for i in range(1, amount) if given[i] < largest] or [i for i in range(1, amount) if given[i] < most]
        mass, left = sum([portions[i] for i in movable]), spare
        for i in movable:
            extra = min(most - given[i], max(1, left * portions[i] // mass), spare)
            given[i] = given[i] + extra
            spare = spare - extra
    return np.array(given)


def gaussian(rng, extent, scale, bound, shards=(), kind=jnp.bfloat16):
    result = scale * jax.random.normal(rng, extent, jnp.float32)
    if shards:
        result = result * shard_levels(rng, extent, shards, -0.22, 0.18)
    return jnp.clip(result, -bound, bound).astype(kind)


def setup_inputs(seed: int = 0) -> dict:
    key_of = jax.random.split(jax.random.key(seed), 18)
    hidden_in = gaussian(key_of[0], (TOKENS, D), 1.0, 6.0, ((0, 32),))
    query_in = gaussian(key_of[1], (TOKENS, HEADS * HEAD_DIM), 1.0, 6.0, ((0, 8), (1, 4)))
    key_in = gaussian(key_of[2], (TOKENS, HEADS * HEAD_DIM), 1.0, 6.0, ((0, 8), (1, 4)))
    value_in = gaussian(key_of[3], (TOKENS, HEADS * HEAD_DIM), 4.0, 24.0, ((0, 8), (1, 4)))
    query_gain = jnp.clip(jnp.exp(jax.random.uniform(key_of[4], (HEAD_DIM,), jnp.float32, math.log(0.5), math.log(2.5))), 0.5, 2.5)
    key_gain = jnp.clip(jnp.exp(jax.random.uniform(key_of[5], (HEAD_DIM,), jnp.float32, math.log(0.5), math.log(2.5))), 0.5, 2.5)
    cache_keys = draw_cache_keys(jax.random.fold_in(key_of[17], 71), 0)
    cache_values = gaussian(key_of[7], (N_REQ * CACHE_DEV, PRE, HEADS * HEAD_DIM), 4.0, 24.0, ((0, 8), (2, 4)))
    cache_block = draw_cache_block(jax.random.fold_in(key_of[17], 71), 0)
    request_lengths = jax.vmap(lambda own: ragged_sizes(own, REQ_GRP, TOK_GRP, TOK_GRP // 2, 2))(jax.random.split(key_of[9], N_REQ)).reshape((N_REQ, REQ_GRP)).astype(jnp.int32)
    out_proj = gaussian(key_of[10], (HEADS * HEAD_DIM, D), (HEADS * HEAD_DIM) ** -0.5, 0.125, ((0, 4),))
    norm_gain = jnp.clip(1.0 + 0.15 * jax.random.normal(key_of[11], (D,), jnp.float32), 0.25, 1.75)
    expert_ids_keys = jax.random.split(jax.random.fold_in(key_of[12], 1), TOKENS // TOK_DEV)
    expert_ids_turns = jax.random.permutation(jax.random.fold_in(key_of[12], 3), TOKENS // TOK_DEV)
    expert_ids = jax.vmap(lambda own, number: assign_block(jax.random.fold_in(key_of[12], 2), own, number, TOK_DEV, EXPERTS, TOPK, MOST, 1))(expert_ids_keys, expert_ids_turns).reshape((TOKENS, TOPK))
    gate_values = jnp.clip(0.4 + 1.2 * jax.random.uniform(key_of[13], (TOKENS, TOPK), jnp.float32) ** shard_levels(key_of[13], (TOKENS, TOPK), ((0, 32),), -0.2, 0.2), 0.4, 1.6)
    old_slots = jax.random.permutation(key_of[14], EXPERTS).astype(jnp.int32)
    new_replicas = with_ends(jax.random.randint(key_of[15], (N_REQ,), 0, EXPERTS), jax.random.fold_in(key_of[15], 1), 0, EXPERTS - 1).astype(jnp.int32)
    slot_weights = gaussian(key_of[16], (EXPERTS, 3, D, FF), D ** -0.5, 0.125, ((0, 8), (3, 4)))
    return dict(hidden_in=hidden_in, query_in=query_in, key_in=key_in, value_in=value_in, query_gain=query_gain, key_gain=key_gain, cache_keys=cache_keys, cache_values=cache_values, cache_block=cache_block, request_lengths=request_lengths, out_proj=out_proj, norm_gain=norm_gain, expert_ids=expert_ids, gate_values=gate_values, old_slots=old_slots, new_replicas=new_replicas, slot_weights=slot_weights)


def prepare(values, gain, position):
    vector = values.astype(jnp.float32)
    scaled = vector * lax.rsqrt(lax.optimization_barrier(jnp.mean(vector * vector, axis=-1, keepdims=True)) + 1e-06) * gain
    half_size = scaled.shape[-1] // 2
    frequency = 10000.0 ** (-(jnp.arange(half_size, dtype=jnp.float32) * 2.0 / scaled.shape[-1]))
    angles = position[:, None] * frequency[None, :]
    cosine = jnp.cos(angles)[:, None, :]
    sine_part = jnp.sin(angles)[:, None, :]
    lower_half = scaled[..., :half_size]
    upper_half = scaled[..., half_size:]
    rotated = jnp.concatenate([lower_half * cosine - upper_half * sine_part, upper_half * cosine + lower_half * sine_part], axis=-1)
    return rotated.astype(jnp.bfloat16)

def run_expert(in_rows, weights):
    gate_act = jnp.dot(in_rows, weights[0], preferred_element_type=jnp.float32)
    up_act = jnp.dot(in_rows, weights[1], preferred_element_type=jnp.float32)
    hidden = (jax.nn.silu(gate_act) * up_act).astype(jnp.bfloat16)
    row_count = in_rows.shape[0]
    quarter = FF // N_EXP
    blocks = hidden.reshape(row_count, N_EXP, quarter).astype(jnp.float32)
    down_rows = weights[2].reshape(D, N_EXP, quarter).astype(jnp.float32)
    parts = jnp.einsum('cqf,dqf->qcd', blocks, down_rows)
    return lax.optimization_barrier(jnp.sum(parts.astype(jnp.bfloat16).astype(jnp.float32), axis=0))

def reference(hidden_in, query_in, key_in, value_in, query_gain, key_gain, cache_keys, cache_values, cache_block, request_lengths, out_proj, norm_gain, expert_ids, gate_values, old_slots, new_replicas, slot_weights):
    scale = 1.0 / math.sqrt(HEAD_DIM)
    query_groups = query_in.reshape(N_REQ, TOK_GRP, HEADS, HEAD_DIM)
    key_groups = key_in.reshape(N_REQ, TOK_GRP, HEADS, HEAD_DIM)
    value_groups = value_in.reshape(N_REQ, TOK_GRP, HEADS, HEAD_DIM)
    block_groups = cache_block.reshape(N_REQ, REQ_GRP)

    def attend_group(inputs):
        query_here, key_here, value_here, lengths, blocks = inputs
        req_ends = jnp.cumsum(lengths).astype(jnp.int32)
        starts = (req_ends - lengths).astype(jnp.int32)
        places = jnp.arange(TOK_GRP, dtype=jnp.int32)
        member = (places[:, None] >= starts[None, :]) & (places[:, None] < req_ends[None, :])
        request_idx = jnp.arange(REQ_GRP, dtype=jnp.int32)
        segment = lax.optimization_barrier(jnp.sum(jnp.where(member, request_idx[None, :], 0), axis=1)).astype(jnp.int32)
        offset = places - lax.optimization_barrier(jnp.sum(jnp.where(member, starts[None, :], 0), axis=1)).astype(jnp.int32)
        has_cache = blocks >= 0
        token_cached = lax.optimization_barrier(jnp.sum(jnp.where(member & has_cache[None, :], 1, 0), axis=1)) > 0
        position = (offset + jnp.where(token_cached, PRE, 0)).astype(jnp.float32)
        query_n = prepare(query_here, query_gain, position)
        key_n = prepare(key_here, key_gain, position)
        safe_blocks = jnp.maximum(blocks, 0).astype(jnp.int32)
        far_keys = jnp.take(cache_keys, safe_blocks, axis=0).reshape(REQ_GRP * PRE, HEADS, HEAD_DIM)
        far_values = jnp.take(cache_values, safe_blocks, axis=0).reshape(REQ_GRP * PRE, HEADS, HEAD_DIM)
        keyset = jnp.concatenate([key_n, far_keys], axis=0)
        valueset = jnp.concatenate([value_here, far_values], axis=0)
        key_request = jnp.concatenate([segment, jnp.repeat(request_idx, PRE)])
        key_live = jnp.concatenate([jnp.ones((TOK_GRP,), dtype=bool), jnp.repeat(has_cache, PRE)])
        allowed = (segment[:, None] == key_request[None, :]) & key_live[None, :]
        scores = jnp.einsum('qhd,khd->hqk', query_n.astype(jnp.float32), keyset.astype(jnp.float32)) * scale
        scores = jnp.where(allowed[None], scores, -1e+30)
        peak = lax.optimization_barrier(jnp.max(scores, axis=-1, keepdims=True))
        expos = jnp.exp(scores - peak)
        weights = (expos / lax.optimization_barrier(jnp.sum(expos, axis=-1, keepdims=True))).astype(jnp.bfloat16)
        attended = jnp.einsum('hqk,khd->qhd', weights.astype(jnp.float32), valueset.astype(jnp.float32))
        return attended.astype(jnp.bfloat16).reshape(TOK_GRP, HEADS * HEAD_DIM)
    attended = lax.map(attend_group, (query_groups, key_groups, value_groups, request_lengths, block_groups))
    attended = attended.reshape(TOKENS, HEADS * HEAD_DIM)
    attn_out = jnp.dot(attended, out_proj, preferred_element_type=jnp.float32)
    residual = hidden_in.astype(jnp.float32) + attn_out
    normed = (residual * lax.rsqrt(lax.optimization_barrier(jnp.mean(residual * residual, axis=-1, keepdims=True)) + 1e-06) * norm_gain).astype(jnp.bfloat16)
    flat_ids = expert_ids.reshape(-1).astype(jnp.int32)
    order = jnp.argsort(flat_ids, stable=True).astype(jnp.int32)
    expert_range = jnp.arange(EXPERTS, dtype=jnp.int32)
    counts = lax.optimization_barrier(jnp.sum((flat_ids[None, :] == expert_range[:, None]).astype(jnp.int32), axis=1)).astype(jnp.int32)
    firsts = (jnp.cumsum(counts) - counts).astype(jnp.int32)
    capacity_all = TOKENS // TOK_DEV * MOST
    token_sorted = jnp.concatenate([(order // TOPK).astype(jnp.int32), jnp.zeros((capacity_all,), jnp.int32)])
    gate_sorted = jnp.concatenate([jnp.take(gate_values.reshape(-1), order), jnp.zeros((capacity_all,), gate_values.dtype)])
    slot_of = jnp.argsort(old_slots).astype(jnp.int32)

    def expert_step(total, expert):
        begin = firsts[expert]
        picked = lax.dynamic_slice_in_dim(token_sorted, begin, capacity_all)
        gates_here = lax.dynamic_slice_in_dim(gate_sorted, begin, capacity_all)
        live = jnp.arange(capacity_all, dtype=jnp.int32) < counts[expert]
        weights = lax.dynamic_index_in_dim(slot_weights, slot_of[expert], 0, keepdims=False)
        output = run_expert(jnp.take(normed, picked, axis=0), weights)
        factor = jnp.where(live, gates_here, 0.0)
        return (total.at[picked].add(output * factor[:, None]), None)
    mixture, _ = lax.scan(expert_step, jnp.zeros((TOKENS, D), jnp.float32), expert_range)
    layer_out = (residual + mixture).astype(jnp.bfloat16)
    replica_weights = jnp.take(slot_weights, jnp.take(slot_of, new_replicas), axis=0)
    return (layer_out, replica_weights)
```

```python
import math

import jax
import jax.numpy as jnp
from jax import lax
from jax.experimental import pallas as pl
from jax.experimental.pallas import tpu as pltpu
from jax.sharding import PartitionSpec as P


def prepare(values, gain, position):
    vector = values.astype(jnp.float32)
    scaled = vector * lax.rsqrt(jnp.mean(vector * vector, axis=-1, keepdims=True) + 1e-06) * gain
    half_size = scaled.shape[-1] // 2
    frequency = 10000.0 ** (-(jnp.arange(half_size, dtype=jnp.float32) * 2.0 / scaled.shape[-1]))
    angles = position[:, None] * frequency[None, :]
    cosine = jnp.cos(angles)[:, None, :]
    sine_part = jnp.sin(angles)[:, None, :]
    lower_half = scaled[..., :half_size]
    upper_half = scaled[..., half_size:]
    rotated = jnp.concatenate(
        [
            lower_half * cosine - upper_half * sine_part,
            upper_half * cosine + lower_half * sine_part,
        ],
        axis=-1,
    )
    return rotated.astype(jnp.bfloat16)


def compact(block_rows, slots_wanted):
    live = block_rows >= 0
    ranks = jnp.cumsum(live.astype(jnp.int32), axis=1) - 1
    request_idx = jnp.arange(block_rows.shape[1], dtype=jnp.int32)[None, :]
    chosen_blocks = []
    chosen_requests = []
    for slot_num in range(slots_wanted):
        picked = live & (ranks == slot_num)
        chosen_blocks.append(jnp.sum(jnp.where(picked, block_rows, 0), axis=1))
        chosen_requests.append(jnp.sum(jnp.where(picked, request_idx, 0), axis=1))
    return (jnp.stack(chosen_blocks, axis=1), jnp.stack(chosen_requests, axis=1))


def experts_kernel(tok_ref, gate_ref, weights_ref, out_ref):
    rows = tok_ref[...]
    slot_count = weights_ref.shape[0]
    total = None
    for slot_num in range(slot_count):
        gate_act = jnp.dot(rows, weights_ref[slot_num, 0], preferred_element_type=jnp.float32)
        up_act = jnp.dot(rows, weights_ref[slot_num, 1], preferred_element_type=jnp.float32)
        factor = gate_ref[:, slot_num : slot_num + 1]
        hidden = gate_act / (1.0 + jnp.exp(-gate_act)) * up_act
        hidden = (hidden * factor).astype(jnp.bfloat16)
        part = lax.dot_general(
            hidden,
            weights_ref[slot_num, 2],
            (((1,), (1,)), ((), ())),
            preferred_element_type=jnp.float32,
        )
        total = part if total is None else total + part
    out_ref[...] = total.astype(out_ref.dtype)


def run_experts(tokens, gates, slot_weights, block):
    count, width = tokens.shape
    slots_here, mats, _, hidden_size = slot_weights.shape
    return pl.pallas_call(
        experts_kernel,
        out_shape=jax.ShapeDtypeStruct((count, width), jnp.bfloat16),
        grid=(count // block,),
        in_specs=[
            pl.BlockSpec((block, width), lambda i: (i, 0)),
            pl.BlockSpec((block, slots_here), lambda i: (i, 0)),
            pl.BlockSpec((slots_here, mats, width, hidden_size), lambda i: (0, 0, 0, 0)),
        ],
        out_specs=pl.BlockSpec((block, width), lambda i: (i, 0)),
        compiler_params=pltpu.CompilerParams(vmem_limit_bytes=40 * 1024 * 1024),
        cost_estimate=pl.CostEstimate(
            flops=2 * count * width * hidden_size * mats * slots_here,
            bytes_accessed=4 * count * width + 2 * slot_weights.size,
            transcendentals=count * hidden_size * slots_here,
        ),
    )(tokens, gates, slot_weights)


def body(
    hidden_in,
    query_in,
    key_in,
    value_in,
    query_gain,
    key_gain,
    cache_keys,
    cache_values,
    cache_block,
    request_lengths,
    out_proj,
    norm_gain,
    expert_ids,
    gate_values,
    old_slots,
    new_replicas,
    slot_weights,
):
    req_count = lax.axis_size("req")
    exp_count = lax.axis_size("exp")
    group_idx = lax.axis_index("req")
    tok_grp, width_q = query_in.shape
    tok_dev, model_width = hidden_in.shape
    head_size = query_gain.shape[0]
    head_count = width_q // head_size
    cache_dev = cache_keys.shape[0]
    pre_len = cache_keys.shape[1]
    req_grp = request_lengths.shape[1]
    lengths = request_lengths[0]
    req_ends = jnp.cumsum(lengths)
    starts = req_ends - lengths
    places = jnp.arange(tok_grp, dtype=jnp.int32)
    member = (places[:, None] >= starts[None, :]) & (places[:, None] < req_ends[None, :])
    request_idx = jnp.arange(req_grp, dtype=jnp.int32)
    segment = jnp.sum(jnp.where(member, request_idx[None, :], 0), axis=1)
    offset = places - jnp.sum(jnp.where(member, starts[None, :], 0), axis=1)
    block_rows = cache_block.reshape(req_count, req_grp)
    my_blocks = lax.dynamic_index_in_dim(block_rows, group_idx, 0, keepdims=False)
    has_cache = my_blocks >= 0
    token_cached = jnp.sum(jnp.where(member & has_cache[None, :], 1, 0), axis=1) > 0
    position = (offset + jnp.where(token_cached, pre_len, 0)).astype(jnp.float32)
    need_blocks, need_requests = compact(block_rows, cache_dev)
    my_requests = lax.dynamic_index_in_dim(need_requests, group_idx, 0, keepdims=False)
    every_cache = lax.all_gather(jnp.stack([cache_keys, cache_values]), "req", axis=1, tiled=True)
    wanted = lax.dynamic_index_in_dim(need_blocks, group_idx, 0, keepdims=False)
    far_cache = jnp.take(every_cache, wanted, axis=1)
    far_keys, far_values = far_cache[0], far_cache[1]
    query_n = prepare(query_in.reshape(tok_grp, head_count, head_size), query_gain, position)
    key_n = prepare(key_in.reshape(tok_grp, head_count, head_size), key_gain, position)
    keyset = jnp.concatenate(
        [key_n, far_keys.reshape(cache_dev * pre_len, head_count, head_size)], axis=0
    )
    valueset = jnp.concatenate(
        [
            value_in.reshape(tok_grp, head_count, head_size),
            far_values.reshape(cache_dev * pre_len, head_count, head_size),
        ],
        axis=0,
    )
    key_request = jnp.concatenate([segment, jnp.repeat(my_requests, pre_len)])
    allowed = segment[:, None] == key_request[None, :]
    scores = jnp.einsum("qhd,khd->hqk", query_n, keyset, preferred_element_type=jnp.float32) * (
        1.0 / math.sqrt(head_size)
    )
    scores = jnp.where(allowed[None], scores, -1e30)
    peak = jnp.max(scores, axis=-1, keepdims=True)
    expos = jnp.exp(scores - peak)
    weights = (expos / jnp.sum(expos, axis=-1, keepdims=True)).astype(jnp.bfloat16)
    attended = jnp.einsum("hqk,khd->qhd", weights, valueset, preferred_element_type=jnp.float32)
    attended = attended.astype(jnp.bfloat16).reshape(tok_grp, width_q)
    attn_out = lax.psum_scatter(
        jnp.dot(attended, out_proj, preferred_element_type=jnp.float32),
        "exp",
        scatter_dimension=0,
        tiled=True,
    )
    residual = hidden_in.astype(jnp.float32) + attn_out
    normed = (
        residual
        * lax.rsqrt(jnp.mean(residual * residual, axis=-1, keepdims=True) + 1e-06)
        * norm_gain
    ).astype(jnp.bfloat16)
    slot_total = old_slots.shape[0]
    slots_here = slot_weights.shape[0]
    slot_range = jnp.arange(slot_total, dtype=jnp.int32)
    slot_of = jnp.sum(
        jnp.where(old_slots[None, :] == slot_range[:, None], slot_range[None, :], 0), axis=1
    )
    dense_gates = jnp.sum(
        jnp.where(expert_ids[:, :, None] == old_slots[None, None, :], gate_values[:, :, None], 0.0),
        axis=1,
    )
    every_gates = lax.all_gather(dense_gates, ("req", "exp"), axis=0, tiled=True)
    my_gates = lax.dynamic_slice_in_dim(every_gates, group_idx * slots_here, slots_here, axis=1)
    tokens = lax.all_gather(normed, ("req", "exp"), axis=0, tiled=True)
    mixed = run_experts(tokens, my_gates, slot_weights, tok_grp)
    mixture = lax.psum_scatter(mixed, ("req", "exp"), scatter_dimension=0, tiled=True)
    layer_out = (residual + mixture.astype(jnp.float32)).astype(jnp.bfloat16)
    spread_slots = lax.all_to_all(slot_weights, "req", split_axis=2, concat_axis=0, tiled=True)
    replica_onehot = new_replicas[:, None] == slot_range[None, :]
    source_slot = jnp.sum(jnp.where(replica_onehot, slot_of[None, :], 0), axis=1)
    chosen_pieces = jnp.take(spread_slots, source_slot, axis=0)
    replica_weights = lax.all_to_all(chosen_pieces, "req", split_axis=0, concat_axis=2, tiled=True)
    return (layer_out, replica_weights)


def solution(mesh):
    in_specs = (
        P(("req", "exp"), None),
        P("req", "exp"),
        P("req", "exp"),
        P("req", "exp"),
        P(),
        P(),
        P("req", None, "exp"),
        P("req", None, "exp"),
        P(),
        P("req", None),
        P("exp", None),
        P(),
        P(("req", "exp"), None),
        P(("req", "exp"), None),
        P(),
        P(),
        P("req", None, None, "exp"),
    )
    out_specs = (P(("req", "exp"), None), P("req", None, None, "exp"))
    return jax.shard_map(body, mesh=mesh, in_specs=in_specs, out_specs=out_specs, check_vma=False)
```

```python
import math

import jax
import jax.numpy as jnp
from jax import lax
from jax.experimental import pallas as pl
from jax.experimental.pallas import tpu as pltpu
from jax.sharding import PartitionSpec as P


def prepare(values, gain, position):
    vector = values.astype(jnp.float32)
    scaled = vector * lax.rsqrt(jnp.mean(vector * vector, axis=-1, keepdims=True) + 1e-06) * gain
    half_size = scaled.shape[-1] // 2
    frequency = 10000.0 ** (-(jnp.arange(half_size, dtype=jnp.float32) * 2.0 / scaled.shape[-1]))
    angles = position[:, None] * frequency[None, :]
    cosine = jnp.cos(angles)[:, None, :]
    sine_part = jnp.sin(angles)[:, None, :]
    lower_half = scaled[..., :half_size]
    upper_half = scaled[..., half_size:]
    rotated = jnp.concatenate(
        [
            lower_half * cosine - upper_half * sine_part,
            upper_half * cosine + lower_half * sine_part,
        ],
        axis=-1,
    )
    return rotated.astype(jnp.bfloat16)


def compact(block_rows, slots_wanted):
    live = block_rows >= 0
    ranks = jnp.cumsum(live.astype(jnp.int32), axis=1) - 1
    request_idx = jnp.arange(block_rows.shape[1], dtype=jnp.int32)[None, :]
    chosen_blocks = []
    chosen_requests = []
    for slot_num in range(slots_wanted):
        picked = live & (ranks == slot_num)
        chosen_blocks.append(jnp.sum(jnp.where(picked, block_rows, 0), axis=1))
        chosen_requests.append(jnp.sum(jnp.where(picked, request_idx, 0), axis=1))
    return (jnp.stack(chosen_blocks, axis=1), jnp.stack(chosen_requests, axis=1))


def experts_kernel(first_slot_ref, tok_ref, weights_ref, out_ref):
    slot_count, _, model_width, _ = weights_ref.shape
    rows = tok_ref[:, :model_width]
    codes = tok_ref[:, model_width:].astype(jnp.float32)
    half_codes = codes.shape[1] // 2
    lane = lax.broadcasted_iota(jnp.int32, codes.shape, 1)
    total = None
    for slot_num in range(slot_count):
        wanted = first_slot_ref[0] + slot_num
        picked = (lane == wanted) | (lane == wanted + half_codes)
        factor = jnp.sum(jnp.where(picked, codes, 0.0), axis=1, keepdims=True)
        gate_act = jnp.dot(rows, weights_ref[slot_num, 0], preferred_element_type=jnp.float32)
        up_act = jnp.dot(rows, weights_ref[slot_num, 1], preferred_element_type=jnp.float32)
        hidden = gate_act / (1.0 + jnp.exp(-gate_act)) * up_act
        hidden = (hidden * factor).astype(jnp.bfloat16)
        part = lax.dot_general(
            hidden,
            weights_ref[slot_num, 2],
            (((1,), (1,)), ((), ())),
            preferred_element_type=jnp.float32,
        )
        total = part if total is None else total + part
    out_ref[...] = total.astype(out_ref.dtype)


def run_experts(first_slot, tokens, slot_weights, block):
    count, ext_width = tokens.shape
    slots_here, mats, width, hidden_size = slot_weights.shape
    return pl.pallas_call(
        experts_kernel,
        out_shape=jax.ShapeDtypeStruct((count, width), jnp.bfloat16),
        grid=(count // block,),
        in_specs=[
            pl.BlockSpec(memory_space=pltpu.SMEM),
            pl.BlockSpec((block, ext_width), lambda i: (i, 0)),
            pl.BlockSpec((slots_here, mats, width, hidden_size), lambda i: (0, 0, 0, 0)),
        ],
        out_specs=pl.BlockSpec((block, width), lambda i: (i, 0)),
        compiler_params=pltpu.CompilerParams(vmem_limit_bytes=40 * 1024 * 1024),
        cost_estimate=pl.CostEstimate(
            flops=2 * count * width * hidden_size * mats * slots_here,
            bytes_accessed=4 * count * width + 2 * slot_weights.size,
            transcendentals=count * hidden_size * slots_here,
        ),
    )(first_slot, tokens, slot_weights)


def turn_pairs(value, step):
    count = lax.axis_size("req")
    return lax.ppermute(value, "req", [(i, (i + 2 * step) % count) for i in range(count)])


def turn(value, step):
    count = lax.axis_size("req")
    return lax.ppermute(value, "req", [(i, (i + step) % count) for i in range(count)])


def flip_pair(value):
    count = lax.axis_size("req")
    return lax.ppermute(value, "req", [(i, i ^ 1) for i in range(count)])


def flip_chip(value):
    count = lax.axis_size("exp")
    return lax.ppermute(value, "exp", [(i, i ^ 2) for i in range(count)])


def flip_core(value):
    count = lax.axis_size("exp")
    return lax.ppermute(value, "exp", [(i, i ^ 1) for i in range(count)])


def pick(value, index, axis):
    return lax.dynamic_index_in_dim(value, index, axis, keepdims=False)


def add(first, second):
    return (first.astype(jnp.float32) + second.astype(jnp.float32)).astype(jnp.bfloat16)


def fetch_cache(cache_keys, cache_values, need_blocks):
    me = lax.axis_index("req")
    pair_count = lax.axis_size("req") // 2
    cache_dev = cache_keys.shape[0]
    mine = jnp.stack([cache_keys, cache_values], axis=1)
    column = jnp.stack([mine] + [turn_pairs(mine, step) for step in range(1, pair_count)])
    column = column.reshape((pair_count * cache_dev,) + mine.shape[1:])

    def rows_for(wanted):
        holder = wanted // cache_dev
        back = (me // 2 - holder // 2) % pair_count
        index = back * cache_dev + wanted % cache_dev
        return jnp.stack([pick(column, index[k], 0) for k in range(cache_dev)])

    mine_wanted = pick(need_blocks, me, 0)
    from_pair = flip_pair(rows_for(pick(need_blocks, me ^ 1, 0)))
    here = ((mine_wanted // cache_dev) ^ me) & 1
    return jnp.where((here == 0)[:, None, None, None], rows_for(mine_wanted), from_pair)


def sum_heads(partial_value):
    me = lax.axis_index("exp")
    rows, width = partial_value.shape
    grid = partial_value.reshape(2, 2, rows // 4, width)
    core, chip = me % 2, me // 2
    got = flip_core(pick(grid, 1 - core, 1).astype(jnp.bfloat16))
    level = pick(grid, core, 1) + got.astype(jnp.float32)
    got = flip_chip(pick(level, 1 - chip, 0).astype(jnp.bfloat16))
    return pick(level, chip, 0) + got.astype(jnp.float32)


def spread_tokens(pieces):
    width = pieces[0].shape[1]
    stacked = jnp.stack(pieces)
    cut = stacked.shape[1] // 2
    first, second = stacked[:, :cut], stacked[:, cut:]
    first = jnp.stack([first, flip_pair(first)])
    second = jnp.stack([second, flip_chip(second)])
    first_far, second_far = flip_chip(first), flip_pair(second)
    parts = [first, first_far, second, second_far]
    return jnp.concatenate([part.reshape(-1, width) for part in parts])


def gather_sums(total, piece_count):
    rows, width = total.shape
    cut = rows // (8 * piece_count)
    first, second = total.reshape(2, 2, 2, piece_count, cut, width)
    first = add(first[0], flip_chip(first[1]))
    second = add(second[0], flip_pair(second[1]))
    first = add(first[0], flip_pair(first[1]))
    second = add(second[0], flip_chip(second[1]))
    return jnp.concatenate([first, second], axis=1)


def mix(normed, codes, slot_weights):
    pair_count = lax.axis_size("req") // 2
    first_slot = (lax.axis_index("req") * slot_weights.shape[0]).astype(jnp.int32).reshape(1)
    ext = jnp.concatenate([normed, codes], axis=1)
    pieces = [ext] + [turn_pairs(ext, step) for step in range(1, pair_count)]
    total = None
    for begin in range(0, pair_count, 2):
        here = spread_tokens(pieces[begin : begin + 2])
        there = flip_core(here)
        back = flip_core(run_experts(first_slot, there, slot_weights, 256))
        sums = gather_sums(add(run_experts(first_slot, here, slot_weights, 256), back), 2)
        for offset in range(2):
            step = begin + offset
            part = sums[offset] if step == 0 else turn_pairs(sums[offset], -step)
            part = part.astype(jnp.float32)
            total = part if total is None else total + part
    return total


def move_replicas(slot_weights, source_slot):
    me = lax.axis_index("req")
    count = lax.axis_size("req")
    slots_here = slot_weights.shape[0]
    last = slot_weights.shape[-1]
    chunks = slot_weights.reshape(slots_here, count, -1, last)
    held = [pick(chunks, me, 1)]
    for step in range(1, count):
        held.append(turn(pick(chunks, (me + step) % count, 1), step))
    held = jnp.concatenate(held)
    result = jnp.zeros(chunks.shape[1:], slot_weights.dtype)
    for step in range(count):
        slot = pick(source_slot, (me + step) % count, 0)
        index = ((me - slot // slots_here) % count) * slots_here + slot % slots_here
        piece = pick(held, index, 0)
        piece = piece if step == 0 else turn(piece, step)
        result = lax.dynamic_update_index_in_dim(result, piece, (me - step) % count, 0)
    return result.reshape((1,) + slot_weights.shape[1:])


def body(
    hidden_in,
    query_in,
    key_in,
    value_in,
    query_gain,
    key_gain,
    cache_keys,
    cache_values,
    cache_block,
    request_lengths,
    out_proj,
    norm_gain,
    expert_ids,
    gate_values,
    old_slots,
    new_replicas,
    slot_weights,
):
    req_count = lax.axis_size("req")
    exp_count = lax.axis_size("exp")
    group_idx = lax.axis_index("req")
    tok_grp, width_q = query_in.shape
    tok_dev, model_width = hidden_in.shape
    head_size = query_gain.shape[0]
    head_count = width_q // head_size
    cache_dev = cache_keys.shape[0]
    pre_len = cache_keys.shape[1]
    req_grp = request_lengths.shape[1]
    lengths = request_lengths[0]
    req_ends = jnp.cumsum(lengths)
    starts = req_ends - lengths
    places = jnp.arange(tok_grp, dtype=jnp.int32)
    member = (places[:, None] >= starts[None, :]) & (places[:, None] < req_ends[None, :])
    request_idx = jnp.arange(req_grp, dtype=jnp.int32)
    segment = jnp.sum(jnp.where(member, request_idx[None, :], 0), axis=1)
    offset = places - jnp.sum(jnp.where(member, starts[None, :], 0), axis=1)
    block_rows = cache_block.reshape(req_count, req_grp)
    my_blocks = lax.dynamic_index_in_dim(block_rows, group_idx, 0, keepdims=False)
    has_cache = my_blocks >= 0
    token_cached = jnp.sum(jnp.where(member & has_cache[None, :], 1, 0), axis=1) > 0
    position = (offset + jnp.where(token_cached, pre_len, 0)).astype(jnp.float32)
    need_blocks, need_requests = compact(block_rows, cache_dev)
    my_requests = lax.dynamic_index_in_dim(need_requests, group_idx, 0, keepdims=False)
    far_cache = fetch_cache(cache_keys, cache_values, need_blocks)
    far_keys, far_values = far_cache[:, 0], far_cache[:, 1]
    far_keys, far_values, slot_weights_later = lax.optimization_barrier(
        (far_keys, far_values, slot_weights)
    )
    query_n = prepare(query_in.reshape(tok_grp, head_count, head_size), query_gain, position)
    key_n = prepare(key_in.reshape(tok_grp, head_count, head_size), key_gain, position)
    keyset = jnp.concatenate(
        [key_n, far_keys.reshape(cache_dev * pre_len, head_count, head_size)], axis=0
    )
    valueset = jnp.concatenate(
        [
            value_in.reshape(tok_grp, head_count, head_size),
            far_values.reshape(cache_dev * pre_len, head_count, head_size),
        ],
        axis=0,
    )
    key_request = jnp.concatenate([segment, jnp.repeat(my_requests, pre_len)])
    allowed = segment[:, None] == key_request[None, :]
    scores = jnp.einsum("qhd,khd->hqk", query_n, keyset, preferred_element_type=jnp.float32) * (
        1.0 / math.sqrt(head_size)
    )
    scores = jnp.where(allowed[None], scores, -1e30)
    peak = jnp.max(scores, axis=-1, keepdims=True)
    expos = jnp.exp(scores - peak)
    weights = (expos / jnp.sum(expos, axis=-1, keepdims=True)).astype(jnp.bfloat16)
    attended = jnp.einsum("hqk,khd->qhd", weights, valueset, preferred_element_type=jnp.float32)
    attended = attended.astype(jnp.bfloat16).reshape(tok_grp, width_q)
    attn_out = sum_heads(jnp.dot(attended, out_proj, preferred_element_type=jnp.float32))
    residual = hidden_in.astype(jnp.float32) + attn_out
    normed = (
        residual
        * lax.rsqrt(jnp.mean(residual * residual, axis=-1, keepdims=True) + 1e-06)
        * norm_gain
    ).astype(jnp.bfloat16)
    slot_total = old_slots.shape[0]
    slot_range = jnp.arange(slot_total, dtype=jnp.int32)
    slot_of = jnp.sum(
        jnp.where(old_slots[None, :] == slot_range[:, None], slot_range[None, :], 0), axis=1
    )
    dense_gates = jnp.sum(
        jnp.where(expert_ids[:, :, None] == old_slots[None, None, :], gate_values[:, :, None], 0.0),
        axis=1,
    )
    high_part = dense_gates.astype(jnp.bfloat16)
    low_part = (dense_gates - high_part.astype(jnp.float32)).astype(jnp.bfloat16)
    lanes = max(64, slot_total)
    gap = ((0, 0), (0, lanes - slot_total))
    codes = jnp.concatenate([jnp.pad(high_part, gap), jnp.pad(low_part, gap)], axis=1)
    mixture = mix(normed, codes, slot_weights)
    layer_out = (residual + mixture).astype(jnp.bfloat16)
    replica_onehot = new_replicas[:, None] == slot_range[None, :]
    source_slot = jnp.sum(jnp.where(replica_onehot, slot_of[None, :], 0), axis=1)
    replica_weights = move_replicas(slot_weights_later, source_slot)
    return (layer_out, replica_weights)


def solution(mesh):
    in_specs = (
        P(("req", "exp"), None),
        P("req", "exp"),
        P("req", "exp"),
        P("req", "exp"),
        P(),
        P(),
        P("req", None, "exp"),
        P("req", None, "exp"),
        P(),
        P("req", None),
        P("exp", None),
        P(),
        P(("req", "exp"), None),
        P(("req", "exp"), None),
        P(),
        P(),
        P("req", None, None, "exp"),
    )
    out_specs = (P(("req", "exp"), None), P("req", None, None, "exp"))
    return jax.shard_map(body, mesh=mesh, in_specs=in_specs, out_specs=out_specs, check_vma=False)
```

```python
import math

import jax
import jax.numpy as jnp
from jax import lax
from jax.experimental import pallas as pl
from jax.experimental.pallas import tpu as pltpu
from jax.sharding import PartitionSpec as P


def prepare(values, gain, position):
    vector = values.astype(jnp.float32)
    scaled = vector * lax.rsqrt(jnp.mean(vector * vector, axis=-1, keepdims=True) + 1e-06) * gain
    half_size = scaled.shape[-1] // 2
    frequency = 10000.0 ** (-(jnp.arange(half_size, dtype=jnp.float32) * 2.0 / scaled.shape[-1]))
    angles = position[:, None] * frequency[None, :]
    cosine = jnp.cos(angles)[:, None, :]
    sine_part = jnp.sin(angles)[:, None, :]
    lower_half = scaled[..., :half_size]
    upper_half = scaled[..., half_size:]
    rotated = jnp.concatenate(
        [
            lower_half * cosine - upper_half * sine_part,
            upper_half * cosine + lower_half * sine_part,
        ],
        axis=-1,
    )
    return rotated.astype(jnp.bfloat16)


def compact(block_rows, slots_wanted):
    live = block_rows >= 0
    ranks = jnp.cumsum(live.astype(jnp.int32), axis=1) - 1
    request_idx = jnp.arange(block_rows.shape[1], dtype=jnp.int32)[None, :]
    chosen_blocks = []
    chosen_requests = []
    for slot_num in range(slots_wanted):
        picked = live & (ranks == slot_num)
        chosen_blocks.append(jnp.sum(jnp.where(picked, block_rows, 0), axis=1))
        chosen_requests.append(jnp.sum(jnp.where(picked, request_idx, 0), axis=1))
    return (jnp.stack(chosen_blocks, axis=1), jnp.stack(chosen_requests, axis=1))


def experts_kernel(first_slot_ref, tok_ref, weights_ref, out_ref):
    slot_count, _, model_width, _ = weights_ref.shape
    rows = tok_ref[:, :model_width]
    codes = tok_ref[:, model_width:].astype(jnp.float32)
    half_codes = codes.shape[1] // 2
    lane = lax.broadcasted_iota(jnp.int32, codes.shape, 1)
    total = None
    for slot_num in range(slot_count):
        wanted = first_slot_ref[0] + slot_num
        picked = (lane == wanted) | (lane == wanted + half_codes)
        factor = jnp.sum(jnp.where(picked, codes, 0.0), axis=1, keepdims=True)
        gate_act = jnp.dot(rows, weights_ref[slot_num, 0], preferred_element_type=jnp.float32)
        up_act = jnp.dot(rows, weights_ref[slot_num, 1], preferred_element_type=jnp.float32)
        hidden = gate_act / (1.0 + jnp.exp(-gate_act)) * up_act
        hidden = (hidden * factor).astype(jnp.bfloat16)
        part = lax.dot_general(
            hidden,
            weights_ref[slot_num, 2],
            (((1,), (1,)), ((), ())),
            preferred_element_type=jnp.float32,
        )
        total = part if total is None else total + part
    out_ref[...] = total.astype(out_ref.dtype)


def run_experts(first_slot, tokens, slot_weights, block):
    count, ext_width = tokens.shape
    slots_here, mats, width, hidden_size = slot_weights.shape
    return pl.pallas_call(
        experts_kernel,
        out_shape=jax.ShapeDtypeStruct((count, width), jnp.bfloat16),
        grid=(count // block,),
        in_specs=[
            pl.BlockSpec(memory_space=pltpu.SMEM),
            pl.BlockSpec((block, ext_width), lambda i: (i, 0)),
            pl.BlockSpec((slots_here, mats, width, hidden_size), lambda i: (0, 0, 0, 0)),
        ],
        out_specs=pl.BlockSpec((block, width), lambda i: (i, 0)),
        compiler_params=pltpu.CompilerParams(vmem_limit_bytes=40 * 1024 * 1024),
        cost_estimate=pl.CostEstimate(
            flops=2 * count * width * hidden_size * mats * slots_here,
            bytes_accessed=4 * count * width + 2 * slot_weights.size,
            transcendentals=count * hidden_size * slots_here,
        ),
    )(first_slot, tokens, slot_weights)


def turn_pairs(value, step):
    count = lax.axis_size("req")
    return lax.ppermute(value, "req", [(i, (i + 2 * step) % count) for i in range(count)])


def flip_pair(value):
    count = lax.axis_size("req")
    return lax.ppermute(value, "req", [(i, i ^ 1) for i in range(count)])


def flip_chip(value):
    count = lax.axis_size("exp")
    return lax.ppermute(value, "exp", [(i, i ^ 2) for i in range(count)])


def flip_core(value):
    count = lax.axis_size("exp")
    return lax.ppermute(value, "exp", [(i, i ^ 1) for i in range(count)])


def pick(value, index, axis):
    return lax.dynamic_index_in_dim(value, index, axis, keepdims=False)


def add(first, second):
    return (first.astype(jnp.float32) + second.astype(jnp.float32)).astype(jnp.bfloat16)


def fetch_cache(cache_keys, cache_values, need_blocks):
    me = lax.axis_index("req")
    pair_count = lax.axis_size("req") // 2
    cache_dev = cache_keys.shape[0]
    mine = jnp.stack([cache_keys, cache_values], axis=1)
    column = jnp.stack([mine] + [turn_pairs(mine, step) for step in range(1, pair_count)])
    column = column.reshape((pair_count * cache_dev,) + mine.shape[1:])

    def rows_for(wanted):
        holder = wanted // cache_dev
        back = (me // 2 - holder // 2) % pair_count
        index = back * cache_dev + wanted % cache_dev
        return jnp.stack([pick(column, index[k], 0) for k in range(cache_dev)])

    mine_wanted = pick(need_blocks, me, 0)
    from_pair = flip_pair(rows_for(pick(need_blocks, me ^ 1, 0)))
    here = ((mine_wanted // cache_dev) ^ me) & 1
    return jnp.where((here == 0)[:, None, None, None], rows_for(mine_wanted), from_pair)


def sum_heads(partial_value):
    me = lax.axis_index("exp")
    rows, width = partial_value.shape
    grid = partial_value.reshape(2, 2, rows // 4, width)
    core, chip = me % 2, me // 2
    got = flip_core(pick(grid, 1 - core, 1).astype(jnp.bfloat16))
    level = pick(grid, core, 1) + got.astype(jnp.float32)
    got = flip_chip(pick(level, 1 - chip, 0).astype(jnp.bfloat16))
    return pick(level, chip, 0) + got.astype(jnp.float32)


def spread_tokens(pieces):
    width = pieces[0].shape[1]
    stacked = jnp.stack(pieces)
    cut = stacked.shape[1] // 2
    first, second = stacked[:, :cut], stacked[:, cut:]
    first = jnp.stack([first, flip_pair(first)])
    second = jnp.stack([second, flip_chip(second)])
    first_far, second_far = flip_chip(first), flip_pair(second)
    parts = [first, first_far, second, second_far]
    return jnp.concatenate([part.reshape(-1, width) for part in parts])


def gather_sums(total, piece_count):
    rows, width = total.shape
    cut = rows // (8 * piece_count)
    first, second = total.reshape(2, 2, 2, piece_count, cut, width)
    first = add(first[0], flip_chip(first[1]))
    second = add(second[0], flip_pair(second[1]))
    first = add(first[0], flip_pair(first[1]))
    second = add(second[0], flip_chip(second[1]))
    return jnp.concatenate([first, second], axis=1)


def mix(normed, codes, slot_weights, later):
    pair_count = lax.axis_size("req") // 2
    first_slot = (lax.axis_index("req") * slot_weights.shape[0]).astype(jnp.int32).reshape(1)
    ext = jnp.concatenate([normed, codes], axis=1)
    pieces = [ext] + [turn_pairs(ext, step) for step in range(1, pair_count)]
    total = None
    for begin in range(0, pair_count, 2):
        here = spread_tokens(pieces[begin : begin + 2])
        there = flip_core(here)
        back = flip_core(run_experts(first_slot, there, slot_weights, 256))
        mixed = run_experts(first_slot, here, slot_weights, 256)
        if begin + 2 >= pair_count:
            mixed, later = lax.optimization_barrier((mixed, later))
        sums = gather_sums(add(mixed, back), 2)
        for offset in range(2):
            step = begin + offset
            part = sums[offset] if step == 0 else turn_pairs(sums[offset], -step)
            part = part.astype(jnp.float32)
            total = part if total is None else total + part
    return total, later


def spread_weights(slot_weights):
    count = lax.axis_size("req")
    slots_here = slot_weights.shape[0]
    chunks = slot_weights.reshape(slots_here, count, -1, slot_weights.shape[-1])
    spread = lax.all_to_all(
        jnp.swapaxes(chunks, 0, 1), "req", split_axis=0, concat_axis=0, tiled=True
    )
    return spread.reshape((count * slots_here,) + chunks.shape[2:])


def collect_replicas(spread, source_slot, shape):
    pieces = jnp.stack([pick(spread, source_slot[k], 0) for k in range(source_slot.shape[0])])
    result = lax.all_to_all(pieces, "req", split_axis=0, concat_axis=0, tiled=True)
    return result.reshape(shape)


def body(
    hidden_in,
    query_in,
    key_in,
    value_in,
    query_gain,
    key_gain,
    cache_keys,
    cache_values,
    cache_block,
    request_lengths,
    out_proj,
    norm_gain,
    expert_ids,
    gate_values,
    old_slots,
    new_replicas,
    slot_weights,
):
    req_count = lax.axis_size("req")
    exp_count = lax.axis_size("exp")
    group_idx = lax.axis_index("req")
    tok_grp, width_q = query_in.shape
    tok_dev, model_width = hidden_in.shape
    head_size = query_gain.shape[0]
    head_count = width_q // head_size
    cache_dev = cache_keys.shape[0]
    pre_len = cache_keys.shape[1]
    req_grp = request_lengths.shape[1]
    lengths = request_lengths[0]
    req_ends = jnp.cumsum(lengths)
    starts = req_ends - lengths
    places = jnp.arange(tok_grp, dtype=jnp.int32)
    member = (places[:, None] >= starts[None, :]) & (places[:, None] < req_ends[None, :])
    request_idx = jnp.arange(req_grp, dtype=jnp.int32)
    segment = jnp.sum(jnp.where(member, request_idx[None, :], 0), axis=1)
    offset = places - jnp.sum(jnp.where(member, starts[None, :], 0), axis=1)
    block_rows = cache_block.reshape(req_count, req_grp)
    my_blocks = lax.dynamic_index_in_dim(block_rows, group_idx, 0, keepdims=False)
    has_cache = my_blocks >= 0
    token_cached = jnp.sum(jnp.where(member & has_cache[None, :], 1, 0), axis=1) > 0
    position = (offset + jnp.where(token_cached, pre_len, 0)).astype(jnp.float32)
    need_blocks, need_requests = compact(block_rows, cache_dev)
    my_requests = lax.dynamic_index_in_dim(need_requests, group_idx, 0, keepdims=False)
    far_cache = fetch_cache(cache_keys, cache_values, need_blocks)
    far_keys, far_values = far_cache[:, 0], far_cache[:, 1]
    far_keys, far_values, slot_weights_later = lax.optimization_barrier(
        (far_keys, far_values, slot_weights)
    )
    query_n = prepare(query_in.reshape(tok_grp, head_count, head_size), query_gain, position)
    key_n = prepare(key_in.reshape(tok_grp, head_count, head_size), key_gain, position)
    keyset = jnp.concatenate(
        [key_n, far_keys.reshape(cache_dev * pre_len, head_count, head_size)], axis=0
    )
    valueset = jnp.concatenate(
        [
            value_in.reshape(tok_grp, head_count, head_size),
            far_values.reshape(cache_dev * pre_len, head_count, head_size),
        ],
        axis=0,
    )
    key_request = jnp.concatenate([segment, jnp.repeat(my_requests, pre_len)])
    allowed = segment[:, None] == key_request[None, :]
    scores = jnp.einsum("qhd,khd->hqk", query_n, keyset, preferred_element_type=jnp.float32) * (
        1.0 / math.sqrt(head_size)
    )
    scores = jnp.where(allowed[None], scores, -1e30)
    peak = jnp.max(scores, axis=-1, keepdims=True)
    expos = jnp.exp(scores - peak)
    weights = (expos / jnp.sum(expos, axis=-1, keepdims=True)).astype(jnp.bfloat16)
    attended = jnp.einsum("hqk,khd->qhd", weights, valueset, preferred_element_type=jnp.float32)
    attended = attended.astype(jnp.bfloat16).reshape(tok_grp, width_q)
    attn_out = sum_heads(jnp.dot(attended, out_proj, preferred_element_type=jnp.float32))
    residual = hidden_in.astype(jnp.float32) + attn_out
    normed = (
        residual
        * lax.rsqrt(jnp.mean(residual * residual, axis=-1, keepdims=True) + 1e-06)
        * norm_gain
    ).astype(jnp.bfloat16)
    slot_total = old_slots.shape[0]
    slot_range = jnp.arange(slot_total, dtype=jnp.int32)
    slot_of = jnp.sum(
        jnp.where(old_slots[None, :] == slot_range[:, None], slot_range[None, :], 0), axis=1
    )
    dense_gates = jnp.sum(
        jnp.where(expert_ids[:, :, None] == old_slots[None, None, :], gate_values[:, :, None], 0.0),
        axis=1,
    )
    high_part = dense_gates.astype(jnp.bfloat16)
    low_part = (dense_gates - high_part.astype(jnp.float32)).astype(jnp.bfloat16)
    lanes = max(64, slot_total)
    gap = ((0, 0), (0, lanes - slot_total))
    codes = jnp.concatenate([jnp.pad(high_part, gap), jnp.pad(low_part, gap)], axis=1)
    spread = spread_weights(slot_weights_later)
    mixture, spread = mix(normed, codes, slot_weights, spread)
    layer_out = (residual + mixture).astype(jnp.bfloat16)
    replica_onehot = new_replicas[:, None] == slot_range[None, :]
    source_slot = jnp.sum(jnp.where(replica_onehot, slot_of[None, :], 0), axis=1)
    replica_shape = (1,) + slot_weights.shape[1:]
    replica_weights = collect_replicas(spread, source_slot, replica_shape)
    return (layer_out, replica_weights)


def solution(mesh):
    in_specs = (
        P(("req", "exp"), None),
        P("req", "exp"),
        P("req", "exp"),
        P("req", "exp"),
        P(),
        P(),
        P("req", None, "exp"),
        P("req", None, "exp"),
        P(),
        P("req", None),
        P("exp", None),
        P(),
        P(("req", "exp"), None),
        P(("req", "exp"), None),
        P(),
        P(),
        P("req", None, None, "exp"),
    )
    out_specs = (P(("req", "exp"), None), P("req", None, None, "exp"))
    return jax.shard_map(body, mesh=mesh, in_specs=in_specs, out_specs=out_specs, check_vma=False)
```

```python
import math

import jax
import jax.numpy as jnp
from jax import lax
from jax.experimental import pallas as pl
from jax.experimental.pallas import tpu as pltpu
from jax.sharding import PartitionSpec as P


def prepare(values, gain, position):
    vector = values.astype(jnp.float32)
    scaled = vector * lax.rsqrt(jnp.mean(vector * vector, axis=-1, keepdims=True) + 1e-06) * gain
    half_size = scaled.shape[-1] // 2
    frequency = 10000.0 ** (-(jnp.arange(half_size, dtype=jnp.float32) * 2.0 / scaled.shape[-1]))
    angles = position[:, None] * frequency[None, :]
    cosine = jnp.cos(angles)[:, None, :]
    sine_part = jnp.sin(angles)[:, None, :]
    lower_half = scaled[..., :half_size]
    upper_half = scaled[..., half_size:]
    rotated = jnp.concatenate(
        [
            lower_half * cosine - upper_half * sine_part,
            upper_half * cosine + lower_half * sine_part,
        ],
        axis=-1,
    )
    return rotated.astype(jnp.bfloat16)


def compact(block_rows, slots_wanted):
    live = block_rows >= 0
    ranks = jnp.cumsum(live.astype(jnp.int32), axis=1) - 1
    request_idx = jnp.arange(block_rows.shape[1], dtype=jnp.int32)[None, :]
    chosen_blocks = []
    chosen_requests = []
    for slot_num in range(slots_wanted):
        picked = live & (ranks == slot_num)
        chosen_blocks.append(jnp.sum(jnp.where(picked, block_rows, 0), axis=1))
        chosen_requests.append(jnp.sum(jnp.where(picked, request_idx, 0), axis=1))
    return (jnp.stack(chosen_blocks, axis=1), jnp.stack(chosen_requests, axis=1))


def experts_kernel(first_slot_ref, tok_ref, weights_ref, out_ref):
    slot_count, _, model_width, _ = weights_ref.shape
    rows = tok_ref[:, :model_width]
    codes = tok_ref[:, model_width:].astype(jnp.float32)
    half_codes = codes.shape[1] // 2
    lane = lax.broadcasted_iota(jnp.int32, codes.shape, 1)
    total = None
    for slot_num in range(slot_count):
        wanted = first_slot_ref[0] + slot_num
        picked = (lane == wanted) | (lane == wanted + half_codes)
        factor = jnp.sum(jnp.where(picked, codes, 0.0), axis=1, keepdims=True)
        gate_act = jnp.dot(rows, weights_ref[slot_num, 0], preferred_element_type=jnp.float32)
        up_act = jnp.dot(rows, weights_ref[slot_num, 1], preferred_element_type=jnp.float32)
        hidden = gate_act / (1.0 + jnp.exp(-gate_act)) * up_act
        hidden = (hidden * factor).astype(jnp.bfloat16)
        part = lax.dot_general(
            hidden,
            weights_ref[slot_num, 2],
            (((1,), (1,)), ((), ())),
            preferred_element_type=jnp.float32,
        )
        total = part if total is None else total + part
    out_ref[...] = total.astype(out_ref.dtype)


def run_experts(first_slot, tokens, slot_weights, block):
    count, ext_width = tokens.shape
    slots_here, mats, width, hidden_size = slot_weights.shape
    return pl.pallas_call(
        experts_kernel,
        out_shape=jax.ShapeDtypeStruct((count, width), jnp.bfloat16),
        grid=(count // block,),
        in_specs=[
            pl.BlockSpec(memory_space=pltpu.SMEM),
            pl.BlockSpec((block, ext_width), lambda i: (i, 0)),
            pl.BlockSpec((slots_here, mats, width, hidden_size), lambda i: (0, 0, 0, 0)),
        ],
        out_specs=pl.BlockSpec((block, width), lambda i: (i, 0)),
        compiler_params=pltpu.CompilerParams(vmem_limit_bytes=40 * 1024 * 1024),
        cost_estimate=pl.CostEstimate(
            flops=2 * count * width * hidden_size * mats * slots_here,
            bytes_accessed=4 * count * width + 2 * slot_weights.size,
            transcendentals=count * hidden_size * slots_here,
        ),
    )(first_slot, tokens, slot_weights)


def turn_pairs(value, step):
    count = lax.axis_size("req")
    return lax.ppermute(value, "req", [(i, (i + 2 * step) % count) for i in range(count)])


def swap(value, mask):
    count = lax.axis_size("req")
    return lax.ppermute(value, "req", [(i, i ^ mask) for i in range(count)])


def after(value, *events):
    return lax.optimization_barrier((value,) + events)[0]


def flip_pair(value):
    count = lax.axis_size("req")
    return lax.ppermute(value, "req", [(i, i ^ 1) for i in range(count)])


def flip_chip(value):
    count = lax.axis_size("exp")
    return lax.ppermute(value, "exp", [(i, i ^ 2) for i in range(count)])


def flip_core(value):
    count = lax.axis_size("exp")
    return lax.ppermute(value, "exp", [(i, i ^ 1) for i in range(count)])


def pick(value, index, axis):
    return lax.dynamic_index_in_dim(value, index, axis, keepdims=False)


def add(first, second):
    return (first.astype(jnp.float32) + second.astype(jnp.float32)).astype(jnp.bfloat16)


def fetch_cache(cache_keys, cache_values, need_blocks):
    me = lax.axis_index("req")
    pair_count = lax.axis_size("req") // 2
    cache_dev = cache_keys.shape[0]
    mine = jnp.stack([cache_keys, cache_values], axis=1)
    column = jnp.stack([mine] + [turn_pairs(mine, step) for step in range(1, pair_count)])
    column = column.reshape((pair_count * cache_dev,) + mine.shape[1:])

    def rows_for(wanted):
        holder = wanted // cache_dev
        back = (me // 2 - holder // 2) % pair_count
        index = back * cache_dev + wanted % cache_dev
        return jnp.stack([pick(column, index[k], 0) for k in range(cache_dev)])

    mine_wanted = pick(need_blocks, me, 0)
    from_pair = flip_pair(rows_for(pick(need_blocks, me ^ 1, 0)))
    here = ((mine_wanted // cache_dev) ^ me) & 1
    return jnp.where((here == 0)[:, None, None, None], rows_for(mine_wanted), from_pair)


def sum_heads(partial_value):
    me = lax.axis_index("exp")
    rows, width = partial_value.shape
    grid = partial_value.reshape(2, 2, rows // 4, width)
    core, chip = me % 2, me // 2
    got = flip_core(pick(grid, 1 - core, 1).astype(jnp.bfloat16))
    level = pick(grid, core, 1) + got.astype(jnp.float32)
    got = flip_chip(pick(level, 1 - chip, 0).astype(jnp.bfloat16))
    return pick(level, chip, 0) + got.astype(jnp.float32)


def spread_tokens(pieces):
    width = pieces[0].shape[1]
    stacked = jnp.stack(pieces)
    cut = stacked.shape[1] // 2
    first, second = stacked[:, :cut], stacked[:, cut:]
    first = jnp.stack([first, flip_pair(first)])
    second = jnp.stack([second, flip_chip(second)])
    first_far, second_far = flip_chip(first), flip_pair(second)
    parts = [first, first_far, second, second_far]
    return jnp.concatenate([part.reshape(-1, width) for part in parts])


def gather_sums(total, piece_count):
    rows, width = total.shape
    cut = rows // (8 * piece_count)
    first, second = total.reshape(2, 2, 2, piece_count, cut, width)
    first = add(first[0], flip_chip(first[1]))
    second = add(second[0], flip_pair(second[1]))
    first = add(first[0], flip_pair(first[1]))
    second = add(second[0], flip_chip(second[1]))
    return jnp.concatenate([first, second], axis=1)


def mix(normed, codes, slot_weights, events):
    pair_count = lax.axis_size("req") // 2
    first_slot = (lax.axis_index("req") * slot_weights.shape[0]).astype(jnp.int32).reshape(1)
    ext = jnp.concatenate([normed, codes], axis=1)
    pieces = [ext] + [turn_pairs(ext, step) for step in range(1, pair_count)]
    events["spread"] = pieces[1:]
    total = None
    for begin in range(0, pair_count, 2):
        here = spread_tokens(pieces[begin : begin + 2])
        events["gathered"] = [here]
        there = flip_core(here)
        far_mixed = run_experts(first_slot, there, slot_weights, 256)
        back = flip_core(far_mixed)
        mixed = run_experts(first_slot, here, slot_weights, 256)
        events["mixed"] = [mixed, far_mixed]
        sums = gather_sums(add(mixed, back), 2)
        for offset in range(2):
            step = begin + offset
            part = sums[offset] if step == 0 else turn_pairs(sums[offset], -step)
            part = part.astype(jnp.float32)
            total = part if total is None else total + part
    return total


def spread_weights(slot_weights, event):
    me = lax.axis_index("req")
    half = lax.axis_size("req") // 2
    spot = me % half
    slots_here = slot_weights.shape[0]
    chunks = slot_weights.reshape(slots_here, half, -1, slot_weights.shape[-1])
    held = [pick(chunks, spot, 1)]
    for mask in range(1, half):
        source = chunks if mask < 3 else after(chunks, event)
        held.append(swap(pick(source, spot ^ mask, 1), mask))
    return jnp.concatenate(held)


def collect_replicas(held, source_slot, slots_here, events):
    me = lax.axis_index("req")
    count = lax.axis_size("req")
    half = count // 2
    spot = me % half
    arrived = {}
    order = [half + mask for mask in range(half)] + list(range(half))
    for place, mask in enumerate(order):
        source = held
        if place < 2 or mask == 1:
            source = after(held, *events["spread"])
        elif place == 2:
            source = after(held, *events["gathered"])
        elif mask:
            source = after(held, *events["mixed"])
        slot = pick(source_slot, me ^ mask, 0)
        index = (spot ^ (slot // slots_here % half)) * slots_here + slot % slots_here
        piece = pick(source, index, 0)
        arrived[mask] = swap(piece, mask) if mask else piece
    same = pick(source_slot, me, 0) // slots_here // half == me // half
    result = jnp.zeros((half,) + held.shape[1:], held.dtype)
    for mask in range(half):
        piece = jnp.where(same, arrived[mask], arrived[half + mask])
        result = lax.dynamic_update_index_in_dim(result, piece, spot ^ mask, 0)
    return result


def body(
    hidden_in,
    query_in,
    key_in,
    value_in,
    query_gain,
    key_gain,
    cache_keys,
    cache_values,
    cache_block,
    request_lengths,
    out_proj,
    norm_gain,
    expert_ids,
    gate_values,
    old_slots,
    new_replicas,
    slot_weights,
):
    req_count = lax.axis_size("req")
    exp_count = lax.axis_size("exp")
    group_idx = lax.axis_index("req")
    tok_grp, width_q = query_in.shape
    tok_dev, model_width = hidden_in.shape
    head_size = query_gain.shape[0]
    head_count = width_q // head_size
    cache_dev = cache_keys.shape[0]
    pre_len = cache_keys.shape[1]
    req_grp = request_lengths.shape[1]
    lengths = request_lengths[0]
    req_ends = jnp.cumsum(lengths)
    starts = req_ends - lengths
    places = jnp.arange(tok_grp, dtype=jnp.int32)
    member = (places[:, None] >= starts[None, :]) & (places[:, None] < req_ends[None, :])
    request_idx = jnp.arange(req_grp, dtype=jnp.int32)
    segment = jnp.sum(jnp.where(member, request_idx[None, :], 0), axis=1)
    offset = places - jnp.sum(jnp.where(member, starts[None, :], 0), axis=1)
    block_rows = cache_block.reshape(req_count, req_grp)
    my_blocks = lax.dynamic_index_in_dim(block_rows, group_idx, 0, keepdims=False)
    has_cache = my_blocks >= 0
    token_cached = jnp.sum(jnp.where(member & has_cache[None, :], 1, 0), axis=1) > 0
    position = (offset + jnp.where(token_cached, pre_len, 0)).astype(jnp.float32)
    need_blocks, need_requests = compact(block_rows, cache_dev)
    my_requests = lax.dynamic_index_in_dim(need_requests, group_idx, 0, keepdims=False)
    far_cache = fetch_cache(cache_keys, cache_values, need_blocks)
    far_keys, far_values = far_cache[:, 0], far_cache[:, 1]
    held = spread_weights(slot_weights, far_cache)
    query_n = prepare(query_in.reshape(tok_grp, head_count, head_size), query_gain, position)
    key_n = prepare(key_in.reshape(tok_grp, head_count, head_size), key_gain, position)
    keyset = jnp.concatenate(
        [key_n, far_keys.reshape(cache_dev * pre_len, head_count, head_size)], axis=0
    )
    valueset = jnp.concatenate(
        [
            value_in.reshape(tok_grp, head_count, head_size),
            far_values.reshape(cache_dev * pre_len, head_count, head_size),
        ],
        axis=0,
    )
    key_request = jnp.concatenate([segment, jnp.repeat(my_requests, pre_len)])
    allowed = segment[:, None] == key_request[None, :]
    scores = jnp.einsum("qhd,khd->hqk", query_n, keyset, preferred_element_type=jnp.float32) * (
        1.0 / math.sqrt(head_size)
    )
    scores = jnp.where(allowed[None], scores, -1e30)
    peak = jnp.max(scores, axis=-1, keepdims=True)
    expos = jnp.exp(scores - peak)
    weights = (expos / jnp.sum(expos, axis=-1, keepdims=True)).astype(jnp.bfloat16)
    attended = jnp.einsum("hqk,khd->qhd", weights, valueset, preferred_element_type=jnp.float32)
    attended = attended.astype(jnp.bfloat16).reshape(tok_grp, width_q)
    attn_out = sum_heads(jnp.dot(attended, out_proj, preferred_element_type=jnp.float32))
    residual = hidden_in.astype(jnp.float32) + attn_out
    normed = (
        residual
        * lax.rsqrt(jnp.mean(residual * residual, axis=-1, keepdims=True) + 1e-06)
        * norm_gain
    ).astype(jnp.bfloat16)
    slot_total = old_slots.shape[0]
    slot_range = jnp.arange(slot_total, dtype=jnp.int32)
    slot_of = jnp.sum(
        jnp.where(old_slots[None, :] == slot_range[:, None], slot_range[None, :], 0), axis=1
    )
    dense_gates = jnp.sum(
        jnp.where(expert_ids[:, :, None] == old_slots[None, None, :], gate_values[:, :, None], 0.0),
        axis=1,
    )
    high_part = dense_gates.astype(jnp.bfloat16)
    low_part = (dense_gates - high_part.astype(jnp.float32)).astype(jnp.bfloat16)
    lanes = max(64, slot_total)
    gap = ((0, 0), (0, lanes - slot_total))
    codes = jnp.concatenate([jnp.pad(high_part, gap), jnp.pad(low_part, gap)], axis=1)
    events = {}
    mixture = mix(normed, codes, slot_weights, events)
    layer_out = (residual + mixture).astype(jnp.bfloat16)
    replica_onehot = new_replicas[:, None] == slot_range[None, :]
    source_slot = jnp.sum(jnp.where(replica_onehot, slot_of[None, :], 0), axis=1)
    replica_weights = collect_replicas(held, source_slot, slot_weights.shape[0], events)
    return (layer_out, replica_weights.reshape((1,) + slot_weights.shape[1:]))


def solution(mesh):
    in_specs = (
        P(("req", "exp"), None),
        P("req", "exp"),
        P("req", "exp"),
        P("req", "exp"),
        P(),
        P(),
        P("req", None, "exp"),
        P("req", None, "exp"),
        P(),
        P("req", None),
        P("exp", None),
        P(),
        P(("req", "exp"), None),
        P(("req", "exp"), None),
        P(),
        P(),
        P("req", None, None, "exp"),
    )
    out_specs = (P(("req", "exp"), None), P("req", None, None, "exp"))
    return jax.shard_map(body, mesh=mesh, in_specs=in_specs, out_specs=out_specs, check_vma=False)
```

```python
import math

import jax
import jax.numpy as jnp
from jax import lax
from jax.experimental import pallas as pl
from jax.experimental.pallas import tpu as pltpu
from jax.sharding import PartitionSpec as P


def prepare(values, gain, position):
    vector = values.astype(jnp.float32)
    scaled = vector * lax.rsqrt(jnp.mean(vector * vector, axis=-1, keepdims=True) + 1e-06) * gain
    half_size = scaled.shape[-1] // 2
    frequency = 10000.0 ** (-(jnp.arange(half_size, dtype=jnp.float32) * 2.0 / scaled.shape[-1]))
    angles = position[:, None] * frequency[None, :]
    cosine = jnp.cos(angles)[:, None, :]
    sine_part = jnp.sin(angles)[:, None, :]
    lower_half = scaled[..., :half_size]
    upper_half = scaled[..., half_size:]
    rotated = jnp.concatenate(
        [
            lower_half * cosine - upper_half * sine_part,
            upper_half * cosine + lower_half * sine_part,
        ],
        axis=-1,
    )
    return rotated.astype(jnp.bfloat16)


def compact(block_rows, slots_wanted):
    live = block_rows >= 0
    ranks = jnp.cumsum(live.astype(jnp.int32), axis=1) - 1
    request_idx = jnp.arange(block_rows.shape[1], dtype=jnp.int32)[None, :]
    chosen_blocks = []
    chosen_requests = []
    for slot_num in range(slots_wanted):
        picked = live & (ranks == slot_num)
        chosen_blocks.append(jnp.sum(jnp.where(picked, block_rows, 0), axis=1))
        chosen_requests.append(jnp.sum(jnp.where(picked, request_idx, 0), axis=1))
    return (jnp.stack(chosen_blocks, axis=1), jnp.stack(chosen_requests, axis=1))


def experts_kernel(first_slot_ref, tok_ref, weights_ref, out_ref):
    slot_count, _, model_width, _ = weights_ref.shape
    rows = tok_ref[:, :model_width]
    codes = tok_ref[:, model_width:].astype(jnp.float32)
    half_codes = codes.shape[1] // 2
    lane = lax.broadcasted_iota(jnp.int32, codes.shape, 1)
    total = None
    for slot_num in range(slot_count):
        wanted = first_slot_ref[0] + slot_num
        picked = (lane == wanted) | (lane == wanted + half_codes)
        factor = jnp.sum(jnp.where(picked, codes, 0.0), axis=1, keepdims=True)
        gate_act = jnp.dot(rows, weights_ref[slot_num, 0], preferred_element_type=jnp.float32)
        up_act = jnp.dot(rows, weights_ref[slot_num, 1], preferred_element_type=jnp.float32)
        hidden = gate_act / (1.0 + jnp.exp(-gate_act)) * up_act
        hidden = (hidden * factor).astype(jnp.bfloat16)
        part = lax.dot_general(
            hidden,
            weights_ref[slot_num, 2],
            (((1,), (1,)), ((), ())),
            preferred_element_type=jnp.float32,
        )
        total = part if total is None else total + part
    out_ref[...] = total.astype(out_ref.dtype)


def run_experts(first_slot, tokens, slot_weights, block):
    count, ext_width = tokens.shape
    slots_here, mats, width, hidden_size = slot_weights.shape
    return pl.pallas_call(
        experts_kernel,
        out_shape=jax.ShapeDtypeStruct((count, width), jnp.bfloat16),
        grid=(count // block,),
        in_specs=[
            pl.BlockSpec(memory_space=pltpu.SMEM),
            pl.BlockSpec((block, ext_width), lambda i: (i, 0)),
            pl.BlockSpec((slots_here, mats, width, hidden_size), lambda i: (0, 0, 0, 0)),
        ],
        out_specs=pl.BlockSpec((block, width), lambda i: (i, 0)),
        compiler_params=pltpu.CompilerParams(vmem_limit_bytes=40 * 1024 * 1024),
        cost_estimate=pl.CostEstimate(
            flops=2 * count * width * hidden_size * mats * slots_here,
            bytes_accessed=4 * count * width + 2 * slot_weights.size,
            transcendentals=count * hidden_size * slots_here,
        ),
    )(first_slot, tokens, slot_weights)


def turn_pairs(value, step):
    count = lax.axis_size("req")
    return lax.ppermute(value, "req", [(i, (i + 2 * step) % count) for i in range(count)])


def swap(value, mask):
    count = lax.axis_size("req")
    return lax.ppermute(value, "req", [(i, i ^ mask) for i in range(count)])


def after(value, *events):
    return lax.optimization_barrier((value,) + events)[0]


def flip_pair(value):
    count = lax.axis_size("req")
    return lax.ppermute(value, "req", [(i, i ^ 1) for i in range(count)])


def flip_chip(value):
    count = lax.axis_size("exp")
    return lax.ppermute(value, "exp", [(i, i ^ 2) for i in range(count)])


def flip_core(value):
    count = lax.axis_size("exp")
    return lax.ppermute(value, "exp", [(i, i ^ 1) for i in range(count)])


def pick(value, index, axis):
    return lax.dynamic_index_in_dim(value, index, axis, keepdims=False)


def add(first, second):
    return (first.astype(jnp.float32) + second.astype(jnp.float32)).astype(jnp.bfloat16)


def fetch_cache(cache_keys, cache_values, need_blocks):
    me = lax.axis_index("req")
    pair_count = lax.axis_size("req") // 2
    cache_dev = cache_keys.shape[0]
    mine = jnp.stack([cache_keys, cache_values], axis=1)
    column = jnp.stack([mine] + [turn_pairs(mine, step) for step in range(1, pair_count)])
    column = column.reshape((pair_count * cache_dev,) + mine.shape[1:])

    def rows_for(wanted):
        holder = wanted // cache_dev
        back = (me // 2 - holder // 2) % pair_count
        index = back * cache_dev + wanted % cache_dev
        return jnp.stack([pick(column, index[k], 0) for k in range(cache_dev)])

    mine_wanted = pick(need_blocks, me, 0)
    from_pair = flip_pair(rows_for(pick(need_blocks, me ^ 1, 0)))
    here = ((mine_wanted // cache_dev) ^ me) & 1
    return jnp.where((here == 0)[:, None, None, None], rows_for(mine_wanted), from_pair)


def sum_heads(partial_value):
    me = lax.axis_index("exp")
    rows, width = partial_value.shape
    grid = partial_value.reshape(2, 2, rows // 4, width)
    core, chip = me % 2, me // 2
    got = flip_core(pick(grid, 1 - core, 1).astype(jnp.bfloat16))
    level = pick(grid, core, 1) + got.astype(jnp.float32)
    got = flip_chip(pick(level, 1 - chip, 0).astype(jnp.bfloat16))
    return pick(level, chip, 0) + got.astype(jnp.float32)


def spread_tokens(pieces):
    width = pieces[0].shape[1]
    stacked = jnp.stack(pieces)
    cut = stacked.shape[1] // 2
    first, second = stacked[:, :cut], stacked[:, cut:]
    first = jnp.stack([first, flip_pair(first)])
    second = jnp.stack([second, flip_chip(second)])
    first_far, second_far = flip_chip(first), flip_pair(second)
    parts = [first, first_far, second, second_far]
    return jnp.concatenate([part.reshape(-1, width) for part in parts])


def gather_sums(total, piece_count):
    rows, width = total.shape
    cut = rows // (8 * piece_count)
    first, second = total.reshape(2, 2, 2, piece_count, cut, width)
    first = add(first[0], flip_chip(first[1]))
    second = add(second[0], flip_pair(second[1]))
    first = add(first[0], flip_pair(first[1]))
    second = add(second[0], flip_chip(second[1]))
    return jnp.concatenate([first, second], axis=1)


def mix(normed, codes, slot_weights, events):
    pair_count = lax.axis_size("req") // 2
    first_slot = (lax.axis_index("req") * slot_weights.shape[0]).astype(jnp.int32).reshape(1)
    ext = jnp.concatenate([normed, codes], axis=1)
    pieces = [ext] + [turn_pairs(ext, step) for step in range(1, pair_count)]
    events["spread"] = pieces[1:]
    total = None
    for begin in range(0, pair_count, 2):
        here = spread_tokens(pieces[begin : begin + 2])
        events["gathered"] = [here]
        there = flip_core(here)
        far_mixed = run_experts(first_slot, there, slot_weights, 256)
        back = flip_core(far_mixed)
        mixed = run_experts(first_slot, here, slot_weights, 256)
        events["mixed"] = [mixed, far_mixed]
        sums = gather_sums(add(mixed, back), 2)
        for offset in range(2):
            step = begin + offset
            part = sums[offset] if step == 0 else turn_pairs(sums[offset], -step)
            part = part.astype(jnp.float32)
            total = part if total is None else total + part
    return total


def spread_weights(slot_weights, event):
    me = lax.axis_index("req")
    half = lax.axis_size("req") // 2
    spot = me % half
    slots_here = slot_weights.shape[0]
    chunks = slot_weights.reshape(slots_here, half, -1, slot_weights.shape[-1])
    held = [pick(chunks, spot, 1)]
    for mask in range(1, half):
        source = chunks if mask < 3 else after(chunks, event)
        held.append(swap(pick(source, spot ^ mask, 1), mask))
    return jnp.concatenate(held)


def copy_kernel(index_ref, source_ref, out_ref):
    out_ref[...] = source_ref[...]


def take_chunks(source, index, part, parts):
    _, rows, width = source.shape
    size = rows // parts
    return pl.pallas_call(
        copy_kernel,
        out_shape=jax.ShapeDtypeStruct((index.shape[0], size, width), source.dtype),
        grid_spec=pltpu.PrefetchScalarGridSpec(
            num_scalar_prefetch=1,
            grid=(index.shape[0],),
            in_specs=[pl.BlockSpec((1, size, width), lambda i, index: (index[i], part, 0))],
            out_specs=pl.BlockSpec((1, size, width), lambda i, index: (i, 0, 0)),
        ),
        cost_estimate=pl.CostEstimate(
            flops=0, bytes_accessed=4 * index.shape[0] * size * width, transcendentals=0
        ),
    )(index, source)


def collect_replicas(held, source_slot, slots_here, events):
    me = lax.axis_index("req")
    count = lax.axis_size("req")
    half = count // 2
    pair_count = count // 2
    side = me % 2
    columns = [[2 * i + k for i in range(pair_count)] for k in range(2)]
    spots = source_slot // slots_here % half
    index = ((me % half) ^ spots) * slots_here + source_slot % slots_here
    halves = source_slot // slots_here // half
    parts = 2
    size, width = held.shape[1] // parts, held.shape[2]
    result = jnp.zeros((half // 2, 2, parts, size, width), held.dtype)
    for part in range(parts):
        source = after(held, *events["spread" if part == 0 else "mixed"])
        outgoing = take_chunks(source, index, part, parts)
        outgoing = outgoing.reshape(pair_count, 2, size, width)
        arrived = lax.all_to_all(
            outgoing, "req", 0, 0, axis_index_groups=columns, tiled=True
        )

        def wanted_by(receiver):
            begin = pick(halves, receiver, 0) * (half // 2)
            where = (begin, receiver % 2, 0, 0)
            return lax.dynamic_slice(arrived, where, (half // 2, 1, size, width))

        swapped = swap(wanted_by(me ^ 1), 1)
        for rows, column in ((wanted_by(me), side), (swapped, 1 - side)):
            where = (0, column, part, 0, 0)
            result = lax.dynamic_update_slice(result, rows[:, :, None], where)
    return result


def body(
    hidden_in,
    query_in,
    key_in,
    value_in,
    query_gain,
    key_gain,
    cache_keys,
    cache_values,
    cache_block,
    request_lengths,
    out_proj,
    norm_gain,
    expert_ids,
    gate_values,
    old_slots,
    new_replicas,
    slot_weights,
):
    req_count = lax.axis_size("req")
    exp_count = lax.axis_size("exp")
    group_idx = lax.axis_index("req")
    tok_grp, width_q = query_in.shape
    tok_dev, model_width = hidden_in.shape
    head_size = query_gain.shape[0]
    head_count = width_q // head_size
    cache_dev = cache_keys.shape[0]
    pre_len = cache_keys.shape[1]
    req_grp = request_lengths.shape[1]
    lengths = request_lengths[0]
    req_ends = jnp.cumsum(lengths)
    starts = req_ends - lengths
    places = jnp.arange(tok_grp, dtype=jnp.int32)
    member = (places[:, None] >= starts[None, :]) & (places[:, None] < req_ends[None, :])
    request_idx = jnp.arange(req_grp, dtype=jnp.int32)
    segment = jnp.sum(jnp.where(member, request_idx[None, :], 0), axis=1)
    offset = places - jnp.sum(jnp.where(member, starts[None, :], 0), axis=1)
    block_rows = cache_block.reshape(req_count, req_grp)
    my_blocks = lax.dynamic_index_in_dim(block_rows, group_idx, 0, keepdims=False)
    has_cache = my_blocks >= 0
    token_cached = jnp.sum(jnp.where(member & has_cache[None, :], 1, 0), axis=1) > 0
    position = (offset + jnp.where(token_cached, pre_len, 0)).astype(jnp.float32)
    need_blocks, need_requests = compact(block_rows, cache_dev)
    my_requests = lax.dynamic_index_in_dim(need_requests, group_idx, 0, keepdims=False)
    far_cache = fetch_cache(cache_keys, cache_values, need_blocks)
    far_keys, far_values = far_cache[:, 0], far_cache[:, 1]
    held = spread_weights(slot_weights, far_cache)
    query_n = prepare(query_in.reshape(tok_grp, head_count, head_size), query_gain, position)
    key_n = prepare(key_in.reshape(tok_grp, head_count, head_size), key_gain, position)
    keyset = jnp.concatenate(
        [key_n, far_keys.reshape(cache_dev * pre_len, head_count, head_size)], axis=0
    )
    valueset = jnp.concatenate(
        [
            value_in.reshape(tok_grp, head_count, head_size),
            far_values.reshape(cache_dev * pre_len, head_count, head_size),
        ],
        axis=0,
    )
    key_request = jnp.concatenate([segment, jnp.repeat(my_requests, pre_len)])
    allowed = segment[:, None] == key_request[None, :]
    scores = jnp.einsum("qhd,khd->hqk", query_n, keyset, preferred_element_type=jnp.float32) * (
        1.0 / math.sqrt(head_size)
    )
    scores = jnp.where(allowed[None], scores, -1e30)
    peak = jnp.max(scores, axis=-1, keepdims=True)
    expos = jnp.exp(scores - peak)
    weights = (expos / jnp.sum(expos, axis=-1, keepdims=True)).astype(jnp.bfloat16)
    attended = jnp.einsum("hqk,khd->qhd", weights, valueset, preferred_element_type=jnp.float32)
    attended = attended.astype(jnp.bfloat16).reshape(tok_grp, width_q)
    attn_out = sum_heads(jnp.dot(attended, out_proj, preferred_element_type=jnp.float32))
    residual = hidden_in.astype(jnp.float32) + attn_out
    normed = (
        residual
        * lax.rsqrt(jnp.mean(residual * residual, axis=-1, keepdims=True) + 1e-06)
        * norm_gain
    ).astype(jnp.bfloat16)
    slot_total = old_slots.shape[0]
    slot_range = jnp.arange(slot_total, dtype=jnp.int32)
    slot_of = jnp.sum(
        jnp.where(old_slots[None, :] == slot_range[:, None], slot_range[None, :], 0), axis=1
    )
    dense_gates = jnp.sum(
        jnp.where(expert_ids[:, :, None] == old_slots[None, None, :], gate_values[:, :, None], 0.0),
        axis=1,
    )
    high_part = dense_gates.astype(jnp.bfloat16)
    low_part = (dense_gates - high_part.astype(jnp.float32)).astype(jnp.bfloat16)
    lanes = max(64, slot_total)
    gap = ((0, 0), (0, lanes - slot_total))
    codes = jnp.concatenate([jnp.pad(high_part, gap), jnp.pad(low_part, gap)], axis=1)
    events = {}
    mixture = mix(normed, codes, slot_weights, events)
    layer_out = (residual + mixture).astype(jnp.bfloat16)
    replica_onehot = new_replicas[:, None] == slot_range[None, :]
    source_slot = jnp.sum(jnp.where(replica_onehot, slot_of[None, :], 0), axis=1)
    replica_weights = collect_replicas(held, source_slot, slot_weights.shape[0], events)
    return (layer_out, replica_weights.reshape((1,) + slot_weights.shape[1:]))


def solution(mesh):
    in_specs = (
        P(("req", "exp"), None),
        P("req", "exp"),
        P("req", "exp"),
        P("req", "exp"),
        P(),
        P(),
        P("req", None, "exp"),
        P("req", None, "exp"),
        P(),
        P("req", None),
        P("exp", None),
        P(),
        P(("req", "exp"), None),
        P(("req", "exp"), None),
        P(),
        P(),
        P("req", None, None, "exp"),
    )
    out_specs = (P(("req", "exp"), None), P("req", None, None, "exp"))
    return jax.shard_map(body, mesh=mesh, in_specs=in_specs, out_specs=out_specs, check_vma=False)
```

```python
import math

import jax
import jax.numpy as jnp
from jax import lax
from jax.experimental import pallas as pl
from jax.experimental.pallas import tpu as pltpu
from jax.sharding import PartitionSpec as P


def prepare(values, gain, position):
    vector = values.astype(jnp.float32)
    scaled = vector * lax.rsqrt(jnp.mean(vector * vector, axis=-1, keepdims=True) + 1e-06) * gain
    half_size = scaled.shape[-1] // 2
    frequency = 10000.0 ** (-(jnp.arange(half_size, dtype=jnp.float32) * 2.0 / scaled.shape[-1]))
    angles = position[:, None] * frequency[None, :]
    cosine = jnp.cos(angles)[:, None, :]
    sine_part = jnp.sin(angles)[:, None, :]
    lower_half = scaled[..., :half_size]
    upper_half = scaled[..., half_size:]
    rotated = jnp.concatenate(
        [
            lower_half * cosine - upper_half * sine_part,
            upper_half * cosine + lower_half * sine_part,
        ],
        axis=-1,
    )
    return rotated.astype(jnp.bfloat16)


def compact(block_rows, slots_wanted):
    live = block_rows >= 0
    ranks = jnp.cumsum(live.astype(jnp.int32), axis=1) - 1
    request_idx = jnp.arange(block_rows.shape[1], dtype=jnp.int32)[None, :]
    chosen_blocks = []
    chosen_requests = []
    for slot_num in range(slots_wanted):
        picked = live & (ranks == slot_num)
        chosen_blocks.append(jnp.sum(jnp.where(picked, block_rows, 0), axis=1))
        chosen_requests.append(jnp.sum(jnp.where(picked, request_idx, 0), axis=1))
    return (jnp.stack(chosen_blocks, axis=1), jnp.stack(chosen_requests, axis=1))


def experts_kernel(first_slot_ref, tok_ref, weights_ref, out_ref):
    slot_count, _, model_width, _ = weights_ref.shape
    rows = tok_ref[:, :model_width]
    codes = tok_ref[:, model_width:].astype(jnp.float32)
    half_codes = codes.shape[1] // 2
    lane = lax.broadcasted_iota(jnp.int32, codes.shape, 1)
    total = None
    for slot_num in range(slot_count):
        wanted = first_slot_ref[0] + slot_num
        picked = (lane == wanted) | (lane == wanted + half_codes)
        factor = jnp.sum(jnp.where(picked, codes, 0.0), axis=1, keepdims=True)
        gate_act = jnp.dot(rows, weights_ref[slot_num, 0], preferred_element_type=jnp.float32)
        up_act = jnp.dot(rows, weights_ref[slot_num, 1], preferred_element_type=jnp.float32)
        hidden = gate_act / (1.0 + jnp.exp(-gate_act)) * up_act
        hidden = (hidden * factor).astype(jnp.bfloat16)
        part = lax.dot_general(
            hidden,
            weights_ref[slot_num, 2],
            (((1,), (1,)), ((), ())),
            preferred_element_type=jnp.float32,
        )
        total = part if total is None else total + part
    out_ref[...] = total.astype(out_ref.dtype)


def run_experts(first_slot, tokens, slot_weights, block):
    count, ext_width = tokens.shape
    slots_here, mats, width, hidden_size = slot_weights.shape
    return pl.pallas_call(
        experts_kernel,
        out_shape=jax.ShapeDtypeStruct((count, width), jnp.bfloat16),
        grid=(count // block,),
        in_specs=[
            pl.BlockSpec(memory_space=pltpu.SMEM),
            pl.BlockSpec((block, ext_width), lambda i: (i, 0)),
            pl.BlockSpec((slots_here, mats, width, hidden_size), lambda i: (0, 0, 0, 0)),
        ],
        out_specs=pl.BlockSpec((block, width), lambda i: (i, 0)),
        compiler_params=pltpu.CompilerParams(vmem_limit_bytes=40 * 1024 * 1024),
        cost_estimate=pl.CostEstimate(
            flops=2 * count * width * hidden_size * mats * slots_here,
            bytes_accessed=4 * count * width + 2 * slot_weights.size,
            transcendentals=count * hidden_size * slots_here,
        ),
    )(first_slot, tokens, slot_weights)


def turn_pairs(value, step):
    count = lax.axis_size("req")
    return lax.ppermute(value, "req", [(i, (i + 2 * step) % count) for i in range(count)])


def swap(value, mask):
    count = lax.axis_size("req")
    return lax.ppermute(value, "req", [(i, i ^ mask) for i in range(count)])


def together(*values):
    return lax.optimization_barrier(values)


def after(value, *events):
    return lax.optimization_barrier((value,) + events)[0]


def flip_pair(value):
    count = lax.axis_size("req")
    return lax.ppermute(value, "req", [(i, i ^ 1) for i in range(count)])


def flip_chip(value):
    count = lax.axis_size("exp")
    return lax.ppermute(value, "exp", [(i, i ^ 2) for i in range(count)])


def flip_core(value):
    count = lax.axis_size("exp")
    return lax.ppermute(value, "exp", [(i, i ^ 1) for i in range(count)])


def pick(value, index, axis):
    return lax.dynamic_index_in_dim(value, index, axis, keepdims=False)


def add(first, second):
    return (first.astype(jnp.float32) + second.astype(jnp.float32)).astype(jnp.bfloat16)


def fetch_cache(cache_keys, cache_values, need_blocks):
    me = lax.axis_index("req")
    pair_count = lax.axis_size("req") // 2
    cache_dev = cache_keys.shape[0]
    mine = jnp.stack([cache_keys, cache_values], axis=1)
    column = jnp.stack([mine] + [turn_pairs(mine, step) for step in range(1, pair_count)])
    column = column.reshape((pair_count * cache_dev,) + mine.shape[1:])

    def rows_for(wanted):
        holder = wanted // cache_dev
        back = (me // 2 - holder // 2) % pair_count
        index = back * cache_dev + wanted % cache_dev
        return jnp.stack([pick(column, index[k], 0) for k in range(cache_dev)])

    mine_wanted = pick(need_blocks, me, 0)
    from_pair = flip_pair(rows_for(pick(need_blocks, me ^ 1, 0)))
    here = ((mine_wanted // cache_dev) ^ me) & 1
    return jnp.where((here == 0)[:, None, None, None], rows_for(mine_wanted), from_pair)


def sum_heads(partial_value):
    me = lax.axis_index("exp")
    rows, width = partial_value.shape
    grid = partial_value.reshape(2, 2, rows // 4, width)
    core, chip = me % 2, me // 2
    got = flip_core(pick(grid, 1 - core, 1).astype(jnp.bfloat16))
    level = pick(grid, core, 1) + got.astype(jnp.float32)
    got = flip_chip(pick(level, 1 - chip, 0).astype(jnp.bfloat16))
    return pick(level, chip, 0) + got.astype(jnp.float32)


def spread_tokens(pieces):
    width = pieces[0].shape[1]
    stacked = jnp.stack(pieces)
    cut = stacked.shape[1] // 2
    first, second = stacked[:, :cut], stacked[:, cut:]
    first = jnp.stack([first, flip_pair(first)])
    second = jnp.stack([second, flip_chip(second)])
    first_far, second_far = flip_chip(first), flip_pair(second)
    parts = [first, first_far, second, second_far]
    return jnp.concatenate([part.reshape(-1, width) for part in parts])


def gather_sums(total, piece_count):
    rows, width = total.shape
    cut = rows // (8 * piece_count)
    first, second = total.reshape(2, 2, 2, piece_count, cut, width)
    first = add(first[0], flip_chip(first[1]))
    second = add(second[0], flip_pair(second[1]))
    first = add(first[0], flip_pair(first[1]))
    second = add(second[0], flip_chip(second[1]))
    return jnp.concatenate([first, second], axis=1)


def mix(normed, codes, slot_weights, outgoing):
    pair_count = lax.axis_size("req") // 2
    first_slot = (lax.axis_index("req") * slot_weights.shape[0]).astype(jnp.int32).reshape(1)
    ext = jnp.concatenate([normed, codes], axis=1)
    pieces = [ext] + [turn_pairs(ext, step) for step in range(1, pair_count)]
    *pieces, outgoing = together(*pieces, outgoing)
    total = None
    for begin in range(0, pair_count, 2):
        here = spread_tokens(pieces[begin : begin + 2])
        there = flip_core(here)
        far_mixed = run_experts(first_slot, there, slot_weights, 256)
        back = flip_core(far_mixed)
        mixed = run_experts(first_slot, here, slot_weights, 256)
        sums = gather_sums(add(mixed, back), 2)
        for offset in range(2):
            step = begin + offset
            part = sums[offset] if step == 0 else turn_pairs(sums[offset], -step)
            part = part.astype(jnp.float32)
            total = part if total is None else total + part
    return total, outgoing, (mixed, far_mixed)


def spread_weights(slot_weights, event):
    me = lax.axis_index("req")
    half = lax.axis_size("req") // 2
    spot = me % half
    slots_here = slot_weights.shape[0]
    chunks = slot_weights.reshape(slots_here, half, -1, slot_weights.shape[-1])
    held = [pick(chunks, spot, 1)]
    for mask in range(1, half):
        source = chunks if mask < 3 else after(chunks, event)
        held.append(swap(pick(source, spot ^ mask, 1), mask))
    return held


def copy_kernel(index_ref, source_ref, out_ref):
    out_ref[...] = source_ref[...]


def take_chunks(source, index, part, parts):
    _, rows, width = source.shape
    size = rows // parts
    return pl.pallas_call(
        copy_kernel,
        out_shape=jax.ShapeDtypeStruct((index.shape[0], size, width), source.dtype),
        grid_spec=pltpu.PrefetchScalarGridSpec(
            num_scalar_prefetch=1,
            grid=(index.shape[0],),
            in_specs=[pl.BlockSpec((1, size, width), lambda i, index: (index[i], part, 0))],
            out_specs=pl.BlockSpec((1, size, width), lambda i, index: (i, 0, 0)),
        ),
        cost_estimate=pl.CostEstimate(
            flops=0, bytes_accessed=4 * index.shape[0] * size * width, transcendentals=0
        ),
    )(index, source)


def chunk_index(source_slot, slots_here):
    half = lax.axis_size("req") // 2
    spots = source_slot // slots_here % half
    return ((lax.axis_index("req") % half) ^ spots) * slots_here + source_slot % slots_here


def collect_replicas(operands, source_slot, slots_here):
    me = lax.axis_index("req")
    count = lax.axis_size("req")
    half = count // 2
    pair_count = count // 2
    side = me % 2
    columns = [[2 * i + k for i in range(pair_count)] for k in range(2)]
    halves = source_slot // slots_here // half
    parts = len(operands)
    _, size, width = operands[0].shape
    result = jnp.zeros((half // 2, 2, parts, size, width), operands[0].dtype)
    for part in range(parts):
        outgoing = operands[part]
        outgoing = outgoing.reshape(pair_count, 2, size, width)
        arrived = lax.all_to_all(
            outgoing, "req", 0, 0, axis_index_groups=columns, tiled=True
        )

        def wanted_by(receiver):
            begin = pick(halves, receiver, 0) * (half // 2)
            where = (begin, receiver % 2, 0, 0)
            return lax.dynamic_slice(arrived, where, (half // 2, 1, size, width))

        swapped = swap(wanted_by(me ^ 1), 1)
        for rows, column in ((wanted_by(me), side), (swapped, 1 - side)):
            where = (0, column, part, 0, 0)
            result = lax.dynamic_update_slice(result, rows[:, :, None], where)
    return result


def body(
    hidden_in,
    query_in,
    key_in,
    value_in,
    query_gain,
    key_gain,
    cache_keys,
    cache_values,
    cache_block,
    request_lengths,
    out_proj,
    norm_gain,
    expert_ids,
    gate_values,
    old_slots,
    new_replicas,
    slot_weights,
):
    req_count = lax.axis_size("req")
    exp_count = lax.axis_size("exp")
    group_idx = lax.axis_index("req")
    tok_grp, width_q = query_in.shape
    tok_dev, model_width = hidden_in.shape
    head_size = query_gain.shape[0]
    head_count = width_q // head_size
    cache_dev = cache_keys.shape[0]
    pre_len = cache_keys.shape[1]
    req_grp = request_lengths.shape[1]
    lengths = request_lengths[0]
    req_ends = jnp.cumsum(lengths)
    starts = req_ends - lengths
    places = jnp.arange(tok_grp, dtype=jnp.int32)
    member = (places[:, None] >= starts[None, :]) & (places[:, None] < req_ends[None, :])
    request_idx = jnp.arange(req_grp, dtype=jnp.int32)
    segment = jnp.sum(jnp.where(member, request_idx[None, :], 0), axis=1)
    offset = places - jnp.sum(jnp.where(member, starts[None, :], 0), axis=1)
    block_rows = cache_block.reshape(req_count, req_grp)
    my_blocks = lax.dynamic_index_in_dim(block_rows, group_idx, 0, keepdims=False)
    has_cache = my_blocks >= 0
    token_cached = jnp.sum(jnp.where(member & has_cache[None, :], 1, 0), axis=1) > 0
    position = (offset + jnp.where(token_cached, pre_len, 0)).astype(jnp.float32)
    need_blocks, need_requests = compact(block_rows, cache_dev)
    my_requests = lax.dynamic_index_in_dim(need_requests, group_idx, 0, keepdims=False)
    far_cache = fetch_cache(cache_keys, cache_values, need_blocks)
    far_keys, far_values = far_cache[:, 0], far_cache[:, 1]
    held = spread_weights(slot_weights, far_cache)
    query_n = prepare(query_in.reshape(tok_grp, head_count, head_size), query_gain, position)
    key_n = prepare(key_in.reshape(tok_grp, head_count, head_size), key_gain, position)
    keyset = jnp.concatenate(
        [key_n, far_keys.reshape(cache_dev * pre_len, head_count, head_size)], axis=0
    )
    valueset = jnp.concatenate(
        [
            value_in.reshape(tok_grp, head_count, head_size),
            far_values.reshape(cache_dev * pre_len, head_count, head_size),
        ],
        axis=0,
    )
    key_request = jnp.concatenate([segment, jnp.repeat(my_requests, pre_len)])
    allowed = segment[:, None] == key_request[None, :]
    scores = jnp.einsum("qhd,khd->hqk", query_n, keyset, preferred_element_type=jnp.float32) * (
        1.0 / math.sqrt(head_size)
    )
    scores = jnp.where(allowed[None], scores, -1e30)
    peak = jnp.max(scores, axis=-1, keepdims=True)
    expos = jnp.exp(scores - peak)
    weights = (expos / jnp.sum(expos, axis=-1, keepdims=True)).astype(jnp.bfloat16)
    attended = jnp.einsum("hqk,khd->qhd", weights, valueset, preferred_element_type=jnp.float32)
    attended = attended.astype(jnp.bfloat16).reshape(tok_grp, width_q)
    attended, *held[1:3] = together(attended, *held[1:3])
    attn_out = sum_heads(jnp.dot(attended, out_proj, preferred_element_type=jnp.float32))
    residual = hidden_in.astype(jnp.float32) + attn_out
    normed = (
        residual
        * lax.rsqrt(jnp.mean(residual * residual, axis=-1, keepdims=True) + 1e-06)
        * norm_gain
    ).astype(jnp.bfloat16)
    slot_total = old_slots.shape[0]
    slot_range = jnp.arange(slot_total, dtype=jnp.int32)
    slot_of = jnp.sum(
        jnp.where(old_slots[None, :] == slot_range[:, None], slot_range[None, :], 0), axis=1
    )
    dense_gates = jnp.sum(
        jnp.where(expert_ids[:, :, None] == old_slots[None, None, :], gate_values[:, :, None], 0.0),
        axis=1,
    )
    high_part = dense_gates.astype(jnp.bfloat16)
    low_part = (dense_gates - high_part.astype(jnp.float32)).astype(jnp.bfloat16)
    lanes = max(64, slot_total)
    gap = ((0, 0), (0, lanes - slot_total))
    codes = jnp.concatenate([jnp.pad(high_part, gap), jnp.pad(low_part, gap)], axis=1)
    replica_onehot = new_replicas[:, None] == slot_range[None, :]
    source_slot = jnp.sum(jnp.where(replica_onehot, slot_of[None, :], 0), axis=1)
    slots_here = slot_weights.shape[0]
    normed, *held[3:] = together(normed, *held[3:])
    held = jnp.concatenate(held)
    index = chunk_index(source_slot, slots_here)
    first_chunks = take_chunks(held, index, 0, 2)
    mixture, first_chunks, mixed = mix(normed, codes, slot_weights, first_chunks)
    layer_out = (residual + mixture).astype(jnp.bfloat16)
    second_chunks = take_chunks(after(held, *mixed), index, 1, 2)
    replica_weights = collect_replicas((first_chunks, second_chunks), source_slot, slots_here)
    return (layer_out, replica_weights.reshape((1,) + slot_weights.shape[1:]))


def solution(mesh):
    in_specs = (
        P(("req", "exp"), None),
        P("req", "exp"),
        P("req", "exp"),
        P("req", "exp"),
        P(),
        P(),
        P("req", None, "exp"),
        P("req", None, "exp"),
        P(),
        P("req", None),
        P("exp", None),
        P(),
        P(("req", "exp"), None),
        P(("req", "exp"), None),
        P(),
        P(),
        P("req", None, None, "exp"),
    )
    out_specs = (P(("req", "exp"), None), P("req", None, None, "exp"))
    return jax.shard_map(body, mesh=mesh, in_specs=in_specs, out_specs=out_specs, check_vma=False)
```

```python
import functools
import math

import jax
import jax.numpy as jnp
from jax import lax
from jax.experimental import pallas as pl
from jax.experimental.pallas import tpu as pltpu
from jax.sharding import PartitionSpec as P


def prepare(values, gain, position):
    vector = values.astype(jnp.float32)
    scaled = vector * lax.rsqrt(jnp.mean(vector * vector, axis=-1, keepdims=True) + 1e-06) * gain
    half_size = scaled.shape[-1] // 2
    frequency = 10000.0 ** (-(jnp.arange(half_size, dtype=jnp.float32) * 2.0 / scaled.shape[-1]))
    angles = position[:, None] * frequency[None, :]
    cosine = jnp.cos(angles)[:, None, :]
    sine_part = jnp.sin(angles)[:, None, :]
    lower_half = scaled[..., :half_size]
    upper_half = scaled[..., half_size:]
    rotated = jnp.concatenate(
        [
            lower_half * cosine - upper_half * sine_part,
            upper_half * cosine + lower_half * sine_part,
        ],
        axis=-1,
    )
    return rotated.astype(jnp.bfloat16)


def compact(block_rows, slots_wanted):
    live = block_rows >= 0
    ranks = jnp.cumsum(live.astype(jnp.int32), axis=1) - 1
    request_idx = jnp.arange(block_rows.shape[1], dtype=jnp.int32)[None, :]
    chosen_blocks = []
    chosen_requests = []
    for slot_num in range(slots_wanted):
        picked = live & (ranks == slot_num)
        chosen_blocks.append(jnp.sum(jnp.where(picked, block_rows, 0), axis=1))
        chosen_requests.append(jnp.sum(jnp.where(picked, request_idx, 0), axis=1))
    return (jnp.stack(chosen_blocks, axis=1), jnp.stack(chosen_requests, axis=1))


def experts_kernel(first_slot_ref, tok_ref, weights_ref, out_ref):
    slot_count, _, model_width, _ = weights_ref.shape
    rows = tok_ref[:, :model_width]
    codes = tok_ref[:, model_width:].astype(jnp.float32)
    half_codes = codes.shape[1] // 2
    lane = lax.broadcasted_iota(jnp.int32, codes.shape, 1)
    total = None
    for slot_num in range(slot_count):
        wanted = first_slot_ref[0] + slot_num
        picked = (lane == wanted) | (lane == wanted + half_codes)
        factor = jnp.sum(jnp.where(picked, codes, 0.0), axis=1, keepdims=True)
        gate_act = jnp.dot(rows, weights_ref[slot_num, 0], preferred_element_type=jnp.float32)
        up_act = jnp.dot(rows, weights_ref[slot_num, 1], preferred_element_type=jnp.float32)
        hidden = gate_act / (1.0 + jnp.exp(-gate_act)) * up_act
        hidden = (hidden * factor).astype(jnp.bfloat16)
        part = lax.dot_general(
            hidden,
            weights_ref[slot_num, 2],
            (((1,), (1,)), ((), ())),
            preferred_element_type=jnp.float32,
        )
        total = part if total is None else total + part
    out_ref[...] = total.astype(out_ref.dtype)


def run_experts(first_slot, tokens, slot_weights, block):
    count, ext_width = tokens.shape
    slots_here, mats, width, hidden_size = slot_weights.shape
    return pl.pallas_call(
        experts_kernel,
        out_shape=jax.ShapeDtypeStruct((count, width), jnp.bfloat16),
        grid=(count // block,),
        in_specs=[
            pl.BlockSpec(memory_space=pltpu.SMEM),
            pl.BlockSpec((block, ext_width), lambda i: (i, 0)),
            pl.BlockSpec((slots_here, mats, width, hidden_size), lambda i: (0, 0, 0, 0)),
        ],
        out_specs=pl.BlockSpec((block, width), lambda i: (i, 0)),
        compiler_params=pltpu.CompilerParams(vmem_limit_bytes=40 * 1024 * 1024),
        cost_estimate=pl.CostEstimate(
            flops=2 * count * width * hidden_size * mats * slots_here,
            bytes_accessed=4 * count * width + 2 * slot_weights.size,
            transcendentals=count * hidden_size * slots_here,
        ),
    )(first_slot, tokens, slot_weights)


def turn_pairs(value, step):
    count = lax.axis_size("req")
    return lax.ppermute(value, "req", [(i, (i + 2 * step) % count) for i in range(count)])


def swap(value, mask):
    count = lax.axis_size("req")
    return lax.ppermute(value, "req", [(i, i ^ mask) for i in range(count)])


def together(*values):
    return lax.optimization_barrier(values)


def after(value, *events):
    return lax.optimization_barrier((value,) + events)[0]


def flip_pair(value):
    count = lax.axis_size("req")
    return lax.ppermute(value, "req", [(i, i ^ 1) for i in range(count)])


def flip_chip(value):
    count = lax.axis_size("exp")
    return lax.ppermute(value, "exp", [(i, i ^ 2) for i in range(count)])


def flip_core(value):
    count = lax.axis_size("exp")
    return lax.ppermute(value, "exp", [(i, i ^ 1) for i in range(count)])


def pick(value, index, axis):
    return lax.dynamic_index_in_dim(value, index, axis, keepdims=False)


def add(first, second):
    return (first.astype(jnp.float32) + second.astype(jnp.float32)).astype(jnp.bfloat16)


def fetch_cache(cache_keys, cache_values, need_blocks):
    me = lax.axis_index("req")
    pair_count = lax.axis_size("req") // 2
    cache_dev = cache_keys.shape[0]
    mine = jnp.stack([cache_keys, cache_values], axis=1)
    column = jnp.stack([mine] + [turn_pairs(mine, step) for step in range(1, pair_count)])
    column = column.reshape((pair_count * cache_dev,) + mine.shape[1:])

    def rows_for(wanted):
        holder = wanted // cache_dev
        back = (me // 2 - holder // 2) % pair_count
        index = back * cache_dev + wanted % cache_dev
        return jnp.stack([pick(column, index[k], 0) for k in range(cache_dev)])

    mine_wanted = pick(need_blocks, me, 0)
    from_pair = flip_pair(rows_for(pick(need_blocks, me ^ 1, 0)))
    here = ((mine_wanted // cache_dev) ^ me) & 1
    wanted = jnp.where((here == 0)[:, None, None, None], rows_for(mine_wanted), from_pair)
    return wanted, column


def sum_heads(partial_value):
    me = lax.axis_index("exp")
    rows, width = partial_value.shape
    grid = partial_value.reshape(2, 2, rows // 4, width)
    core, chip = me % 2, me // 2
    got = flip_core(pick(grid, 1 - core, 1).astype(jnp.bfloat16))
    level = pick(grid, core, 1) + got.astype(jnp.float32)
    got = flip_chip(pick(level, 1 - chip, 0).astype(jnp.bfloat16))
    return pick(level, chip, 0) + got.astype(jnp.float32)


def spread_tokens(pieces):
    width = pieces[0].shape[1]
    stacked = jnp.stack(pieces)
    cut = stacked.shape[1] // 2
    first, second = stacked[:, :cut], stacked[:, cut:]
    first = jnp.stack([first, flip_pair(first)])
    second = jnp.stack([second, flip_chip(second)])
    first_far, second_far = flip_chip(first), flip_pair(second)
    parts = [first, first_far, second, second_far]
    return jnp.concatenate([part.reshape(-1, width) for part in parts])


def gather_sums(total, piece_count):
    rows, width = total.shape
    cut = rows // (8 * piece_count)
    first, second = total.reshape(2, 2, 2, piece_count, cut, width)
    first = add(first[0], flip_chip(first[1]))
    second = add(second[0], flip_pair(second[1]))
    first = add(first[0], flip_pair(first[1]))
    second = add(second[0], flip_chip(second[1]))
    return jnp.concatenate([first, second], axis=1)


def mix(normed, codes, slot_weights, outgoing):
    pair_count = lax.axis_size("req") // 2
    first_slot = (lax.axis_index("req") * slot_weights.shape[0]).astype(jnp.int32).reshape(1)
    ext = jnp.concatenate([normed, codes], axis=1)
    pieces = [ext] + [turn_pairs(ext, step) for step in range(1, pair_count)]
    outgoing = after(outgoing, *pieces[1:])
    *pieces[2:], outgoing = together(*pieces[2:], outgoing)
    total = None
    for begin in range(0, pair_count, 2):
        here = spread_tokens(pieces[begin : begin + 2])
        there = flip_core(here)
        far_mixed = run_experts(first_slot, there, slot_weights, 256)
        back = flip_core(far_mixed)
        mixed = run_experts(first_slot, here, slot_weights, 256)
        sums = gather_sums(add(mixed, back), 2)
        for offset in range(2):
            step = begin + offset
            part = sums[offset] if step == 0 else turn_pairs(sums[offset], -step)
            part = part.astype(jnp.float32)
            total = part if total is None else total + part
    return total, outgoing, (mixed, far_mixed)


def spread_weights(slot_weights, event):
    me = lax.axis_index("req")
    half = lax.axis_size("req") // 2
    spot = me % half
    slots_here = slot_weights.shape[0]
    chunks = slot_weights.reshape(slots_here, half, -1, slot_weights.shape[-1])
    held = [pick(chunks, spot, 1)]
    for mask in range(1, half):
        source = chunks if mask < 3 else after(chunks, event)
        held.append(swap(pick(source, spot ^ mask, 1), mask))
    return held


def pick_kernel(slots_here, begin, size, index_ref, *refs):
    sources, (out_ref, sems) = refs[:-2], refs[-2:]
    count = out_ref.shape[0]

    def start(i, carry):
        holder, slot = index_ref[i] // slots_here, index_ref[i] % slots_here
        for k, source in enumerate(sources):

            @pl.when(holder == k)
            def _():
                rows = source.at[slot, pl.ds(begin, size)]
                pltpu.make_async_copy(rows, out_ref.at[i], sems.at[i]).start()

        return carry

    def finish(i, carry):
        rows = sources[0].at[0, pl.ds(begin, size)]
        pltpu.make_async_copy(rows, out_ref.at[i], sems.at[i]).wait()
        return carry

    lax.fori_loop(0, count, start, 0)
    lax.fori_loop(0, count, finish, 0)


def take_chunks(held, index, begin, size):
    slots_here, _, width = held[0].shape
    count = index.shape[0]
    return pl.pallas_call(
        functools.partial(pick_kernel, slots_here, begin, size),
        out_shape=jax.ShapeDtypeStruct((count, size, width), held[0].dtype),
        in_specs=[pl.BlockSpec(memory_space=pltpu.SMEM)]
        + [pl.BlockSpec(memory_space=pl.ANY)] * len(held),
        out_specs=pl.BlockSpec(memory_space=pl.ANY),
        scratch_shapes=[pltpu.SemaphoreType.DMA((count,))],
        cost_estimate=pl.CostEstimate(
            flops=0, bytes_accessed=4 * count * size * width, transcendentals=0
        ),
    )(index, *held)


def chunk_index(source_slot, slots_here):
    half = lax.axis_size("req") // 2
    spots = source_slot // slots_here % half
    return ((lax.axis_index("req") % half) ^ spots) * slots_here + source_slot % slots_here


def collect_replicas(operands, source_slot, slots_here):
    me = lax.axis_index("req")
    count = lax.axis_size("req")
    half = count // 2
    pair_count = count // 2
    side = me % 2
    columns = [[2 * i + k for i in range(pair_count)] for k in range(2)]
    halves = source_slot // slots_here // half
    width = operands[0].shape[2]
    rows_all = sum(operand.shape[1] for operand in operands)
    result = jnp.zeros((half // 2, 2, rows_all, width), operands[0].dtype)
    first_row = 0
    for outgoing in operands:
        size = outgoing.shape[1]
        outgoing = outgoing.reshape(pair_count, 2, size, width)
        arrived = lax.all_to_all(
            outgoing, "req", 0, 0, axis_index_groups=columns, tiled=True
        )

        def wanted_by(receiver):
            begin = pick(halves, receiver, 0) * (half // 2)
            where = (begin, receiver % 2, 0, 0)
            return lax.dynamic_slice(arrived, where, (half // 2, 1, size, width))

        swapped = swap(wanted_by(me ^ 1), 1)
        for rows, column in ((wanted_by(me), side), (swapped, 1 - side)):
            result = lax.dynamic_update_slice(result, rows, (0, column, first_row, 0))
        first_row += size
    return result


def body(
    hidden_in,
    query_in,
    key_in,
    value_in,
    query_gain,
    key_gain,
    cache_keys,
    cache_values,
    cache_block,
    request_lengths,
    out_proj,
    norm_gain,
    expert_ids,
    gate_values,
    old_slots,
    new_replicas,
    slot_weights,
):
    req_count = lax.axis_size("req")
    exp_count = lax.axis_size("exp")
    group_idx = lax.axis_index("req")
    tok_grp, width_q = query_in.shape
    tok_dev, model_width = hidden_in.shape
    head_size = query_gain.shape[0]
    head_count = width_q // head_size
    cache_dev = cache_keys.shape[0]
    pre_len = cache_keys.shape[1]
    req_grp = request_lengths.shape[1]
    lengths = request_lengths[0]
    req_ends = jnp.cumsum(lengths)
    starts = req_ends - lengths
    places = jnp.arange(tok_grp, dtype=jnp.int32)
    member = (places[:, None] >= starts[None, :]) & (places[:, None] < req_ends[None, :])
    request_idx = jnp.arange(req_grp, dtype=jnp.int32)
    segment = jnp.sum(jnp.where(member, request_idx[None, :], 0), axis=1)
    offset = places - jnp.sum(jnp.where(member, starts[None, :], 0), axis=1)
    block_rows = cache_block.reshape(req_count, req_grp)
    my_blocks = lax.dynamic_index_in_dim(block_rows, group_idx, 0, keepdims=False)
    has_cache = my_blocks >= 0
    token_cached = jnp.sum(jnp.where(member & has_cache[None, :], 1, 0), axis=1) > 0
    position = (offset + jnp.where(token_cached, pre_len, 0)).astype(jnp.float32)
    need_blocks, need_requests = compact(block_rows, cache_dev)
    my_requests = lax.dynamic_index_in_dim(need_requests, group_idx, 0, keepdims=False)
    far_cache, column = fetch_cache(cache_keys, cache_values, need_blocks)
    far_keys, far_values = far_cache[:, 0], far_cache[:, 1]
    held = spread_weights(slot_weights, column)
    query_n = prepare(query_in.reshape(tok_grp, head_count, head_size), query_gain, position)
    key_n = prepare(key_in.reshape(tok_grp, head_count, head_size), key_gain, position)
    keyset = jnp.concatenate(
        [key_n, far_keys.reshape(cache_dev * pre_len, head_count, head_size)], axis=0
    )
    valueset = jnp.concatenate(
        [
            value_in.reshape(tok_grp, head_count, head_size),
            far_values.reshape(cache_dev * pre_len, head_count, head_size),
        ],
        axis=0,
    )
    key_request = jnp.concatenate([segment, jnp.repeat(my_requests, pre_len)])
    allowed = segment[:, None] == key_request[None, :]
    scores = jnp.einsum("qhd,khd->hqk", query_n, keyset, preferred_element_type=jnp.float32) * (
        1.0 / math.sqrt(head_size)
    )
    scores = jnp.where(allowed[None], scores, -1e30)
    peak = jnp.max(scores, axis=-1, keepdims=True)
    expos = jnp.exp(scores - peak)
    weights = (expos / jnp.sum(expos, axis=-1, keepdims=True)).astype(jnp.bfloat16)
    attended = jnp.einsum("hqk,khd->qhd", weights, valueset, preferred_element_type=jnp.float32)
    attended = attended.astype(jnp.bfloat16).reshape(tok_grp, width_q)
    attended, *held[1:3] = together(attended, *held[1:3])
    attn_out = sum_heads(jnp.dot(attended, out_proj, preferred_element_type=jnp.float32))
    residual = hidden_in.astype(jnp.float32) + attn_out
    normed = (
        residual
        * lax.rsqrt(jnp.mean(residual * residual, axis=-1, keepdims=True) + 1e-06)
        * norm_gain
    ).astype(jnp.bfloat16)
    slot_total = old_slots.shape[0]
    slot_range = jnp.arange(slot_total, dtype=jnp.int32)
    slot_of = jnp.sum(
        jnp.where(old_slots[None, :] == slot_range[:, None], slot_range[None, :], 0), axis=1
    )
    dense_gates = jnp.sum(
        jnp.where(expert_ids[:, :, None] == old_slots[None, None, :], gate_values[:, :, None], 0.0),
        axis=1,
    )
    high_part = dense_gates.astype(jnp.bfloat16)
    low_part = (dense_gates - high_part.astype(jnp.float32)).astype(jnp.bfloat16)
    lanes = max(64, slot_total)
    gap = ((0, 0), (0, lanes - slot_total))
    codes = jnp.concatenate([jnp.pad(high_part, gap), jnp.pad(low_part, gap)], axis=1)
    replica_onehot = new_replicas[:, None] == slot_range[None, :]
    source_slot = jnp.sum(jnp.where(replica_onehot, slot_of[None, :], 0), axis=1)
    slots_here = slot_weights.shape[0]
    index = chunk_index(source_slot, slots_here)
    last_size = held[0].shape[1] // 3
    first_size = held[0].shape[1] - last_size
    first_chunks = take_chunks(held, index, 0, first_size)
    second_chunks = take_chunks(held, index, first_size, last_size)
    mixture, first_chunks, mixed = mix(normed, codes, slot_weights, first_chunks)
    layer_out = (residual + mixture).astype(jnp.bfloat16)
    second_chunks = after(second_chunks, *mixed)
    replica_weights = collect_replicas((first_chunks, second_chunks), source_slot, slots_here)
    return (layer_out, replica_weights.reshape((1,) + slot_weights.shape[1:]))


def solution(mesh):
    in_specs = (
        P(("req", "exp"), None),
        P("req", "exp"),
        P("req", "exp"),
        P("req", "exp"),
        P(),
        P(),
        P("req", None, "exp"),
        P("req", None, "exp"),
        P(),
        P("req", None),
        P("exp", None),
        P(),
        P(("req", "exp"), None),
        P(("req", "exp"), None),
        P(),
        P(),
        P("req", None, None, "exp"),
    )
    out_specs = (P(("req", "exp"), None), P("req", None, None, "exp"))
    return jax.shard_map(body, mesh=mesh, in_specs=in_specs, out_specs=out_specs, check_vma=False)
```

```python
import functools
import math

import jax
import jax.numpy as jnp
from jax import lax
from jax.experimental import pallas as pl
from jax.experimental.pallas import tpu as pltpu
from jax.sharding import PartitionSpec as P


def prepare(values, gain, position):
    vector = values.astype(jnp.float32)
    scaled = vector * lax.rsqrt(jnp.mean(vector * vector, axis=-1, keepdims=True) + 1e-06) * gain
    half_size = scaled.shape[-1] // 2
    frequency = 10000.0 ** (-(jnp.arange(half_size, dtype=jnp.float32) * 2.0 / scaled.shape[-1]))
    angles = position[:, None] * frequency[None, :]
    cosine = jnp.cos(angles)[:, None, :]
    sine_part = jnp.sin(angles)[:, None, :]
    lower_half = scaled[..., :half_size]
    upper_half = scaled[..., half_size:]
    rotated = jnp.concatenate(
        [
            lower_half * cosine - upper_half * sine_part,
            upper_half * cosine + lower_half * sine_part,
        ],
        axis=-1,
    )
    return rotated.astype(jnp.bfloat16)


def compact(block_rows, slots_wanted):
    live = block_rows >= 0
    ranks = jnp.cumsum(live.astype(jnp.int32), axis=1) - 1
    request_idx = jnp.arange(block_rows.shape[1], dtype=jnp.int32)[None, :]
    chosen_blocks = []
    chosen_requests = []
    for slot_num in range(slots_wanted):
        picked = live & (ranks == slot_num)
        chosen_blocks.append(jnp.sum(jnp.where(picked, block_rows, 0), axis=1))
        chosen_requests.append(jnp.sum(jnp.where(picked, request_idx, 0), axis=1))
    return (jnp.stack(chosen_blocks, axis=1), jnp.stack(chosen_requests, axis=1))


def experts_kernel(first_slot_ref, tok_ref, weights_ref, out_ref):
    slot_count, _, model_width, _ = weights_ref.shape
    rows = tok_ref[:, :model_width]
    codes = tok_ref[:, model_width:].astype(jnp.float32)
    half_codes = codes.shape[1] // 2
    lane = lax.broadcasted_iota(jnp.int32, codes.shape, 1)
    total = None
    for slot_num in range(slot_count):
        wanted = first_slot_ref[0] + slot_num
        picked = (lane == wanted) | (lane == wanted + half_codes)
        factor = jnp.sum(jnp.where(picked, codes, 0.0), axis=1, keepdims=True)
        gate_act = jnp.dot(rows, weights_ref[slot_num, 0], preferred_element_type=jnp.float32)
        up_act = jnp.dot(rows, weights_ref[slot_num, 1], preferred_element_type=jnp.float32)
        hidden = gate_act / (1.0 + jnp.exp(-gate_act)) * up_act
        hidden = (hidden * factor).astype(jnp.bfloat16)
        part = lax.dot_general(
            hidden,
            weights_ref[slot_num, 2],
            (((1,), (1,)), ((), ())),
            preferred_element_type=jnp.float32,
        )
        total = part if total is None else total + part
    out_ref[...] = total.astype(out_ref.dtype)


def run_experts(first_slot, tokens, slot_weights, block):
    count, ext_width = tokens.shape
    slots_here, mats, width, hidden_size = slot_weights.shape
    return pl.pallas_call(
        experts_kernel,
        out_shape=jax.ShapeDtypeStruct((count, width), jnp.bfloat16),
        grid=(count // block,),
        in_specs=[
            pl.BlockSpec(memory_space=pltpu.SMEM),
            pl.BlockSpec((block, ext_width), lambda i: (i, 0)),
            pl.BlockSpec((slots_here, mats, width, hidden_size), lambda i: (0, 0, 0, 0)),
        ],
        out_specs=pl.BlockSpec((block, width), lambda i: (i, 0)),
        compiler_params=pltpu.CompilerParams(vmem_limit_bytes=40 * 1024 * 1024),
        cost_estimate=pl.CostEstimate(
            flops=2 * count * width * hidden_size * mats * slots_here,
            bytes_accessed=4 * count * width + 2 * slot_weights.size,
            transcendentals=count * hidden_size * slots_here,
        ),
    )(first_slot, tokens, slot_weights)


def turn_pairs(value, step):
    count = lax.axis_size("req")
    return lax.ppermute(value, "req", [(i, (i + 2 * step) % count) for i in range(count)])


def swap(value, mask):
    count = lax.axis_size("req")
    return lax.ppermute(value, "req", [(i, i ^ mask) for i in range(count)])


def together(*values):
    return lax.optimization_barrier(values)


def after(value, *events):
    return lax.optimization_barrier((value,) + events)[0]


def flip_pair(value):
    count = lax.axis_size("req")
    return lax.ppermute(value, "req", [(i, i ^ 1) for i in range(count)])


def flip_chip(value):
    count = lax.axis_size("exp")
    return lax.ppermute(value, "exp", [(i, i ^ 2) for i in range(count)])


def flip_core(value):
    count = lax.axis_size("exp")
    return lax.ppermute(value, "exp", [(i, i ^ 1) for i in range(count)])


def pick(value, index, axis):
    return lax.dynamic_index_in_dim(value, index, axis, keepdims=False)


def add(first, second):
    return (first.astype(jnp.float32) + second.astype(jnp.float32)).astype(jnp.bfloat16)


def fetch_cache(cache_keys, cache_values, need_blocks):
    me = lax.axis_index("req")
    pair_count = lax.axis_size("req") // 2
    cache_dev = cache_keys.shape[0]
    mine = jnp.stack([cache_keys, cache_values], axis=1)
    column = jnp.stack([mine] + [turn_pairs(mine, step) for step in range(1, pair_count)])
    column = column.reshape((pair_count * cache_dev,) + mine.shape[1:])

    def rows_for(wanted):
        holder = wanted // cache_dev
        back = (me // 2 - holder // 2) % pair_count
        index = back * cache_dev + wanted % cache_dev
        return jnp.stack([pick(column, index[k], 0) for k in range(cache_dev)])

    mine_wanted = pick(need_blocks, me, 0)
    from_pair = flip_pair(rows_for(pick(need_blocks, me ^ 1, 0)))
    here = ((mine_wanted // cache_dev) ^ me) & 1
    wanted = jnp.where((here == 0)[:, None, None, None], rows_for(mine_wanted), from_pair)
    return wanted


def sum_heads(partial_value):
    me = lax.axis_index("exp")
    rows, width = partial_value.shape
    grid = partial_value.reshape(2, 2, rows // 4, width)
    core, chip = me % 2, me // 2
    got = flip_core(pick(grid, 1 - core, 1).astype(jnp.bfloat16))
    level = pick(grid, core, 1) + got.astype(jnp.float32)
    got = flip_chip(pick(level, 1 - chip, 0).astype(jnp.bfloat16))
    return pick(level, chip, 0) + got.astype(jnp.float32)


def spread_tokens(pieces):
    width = pieces[0].shape[1]
    stacked = jnp.stack(pieces)
    cut = stacked.shape[1] // 2
    first, second = stacked[:, :cut], stacked[:, cut:]
    first = jnp.stack([first, flip_pair(first)])
    second = jnp.stack([second, flip_chip(second)])
    first_far, second_far = flip_chip(first), flip_pair(second)
    parts = [first, first_far, second, second_far]
    return jnp.concatenate([part.reshape(-1, width) for part in parts])


def gather_sums(total, piece_count):
    rows, width = total.shape
    cut = rows // (8 * piece_count)
    first, second = total.reshape(2, 2, 2, piece_count, cut, width)
    first = add(first[0], flip_chip(first[1]))
    second = add(second[0], flip_pair(second[1]))
    first = add(first[0], flip_pair(first[1]))
    second = add(second[0], flip_chip(second[1]))
    return jnp.concatenate([first, second], axis=1)


def mix(normed, codes, slot_weights, held, pick_first):
    pair_count = lax.axis_size("req") // 2
    first_slot = (lax.axis_index("req") * slot_weights.shape[0]).astype(jnp.int32).reshape(1)
    ext = jnp.concatenate([normed, codes], axis=1)
    pieces = [ext]
    for step in range(1, pair_count):
        source = ext
        if step == 2:
            source, *held[3:] = together(ext, *held[3:])
        pieces.append(turn_pairs(source, step))
    outgoing = pick_first(held)
    outgoing = after(outgoing, *pieces[1:])
    *pieces[2:], outgoing = together(*pieces[2:], outgoing)
    arrived = trade_columns(outgoing)
    total = None
    for begin in range(0, pair_count, 2):
        here = spread_tokens(pieces[begin : begin + 2])
        there = flip_core(here)
        back = flip_core(run_experts(first_slot, there, slot_weights, 256))
        if begin + 2 >= pair_count:
            here, arrived = together(here, arrived)
        mixed = run_experts(first_slot, here, slot_weights, 256)
        sums = gather_sums(add(mixed, back), 2)
        for offset in range(2):
            step = begin + offset
            part = sums[offset] if step == 0 else turn_pairs(sums[offset], -step)
            part = part.astype(jnp.float32)
            total = part if total is None else total + part
    return total, arrived


def spread_weights(slot_weights):
    me = lax.axis_index("req")
    half = lax.axis_size("req") // 2
    spot = me % half
    slots_here = slot_weights.shape[0]
    chunks = slot_weights.reshape(slots_here, half, -1, slot_weights.shape[-1])
    held = [pick(chunks, spot, 1)]
    for mask in range(1, half):
        held.append(swap(pick(chunks, spot ^ mask, 1), mask))
    return held


def pick_kernel(slots_here, index_ref, *refs):
    sources, out_ref = refs[:-1], refs[-1]
    holder = index_ref[pl.program_id(0)] // slots_here
    for k, source in enumerate(sources):

        @pl.when(holder == k)
        def _():
            out_ref[...] = source[...]


def take_chunks(held, index, begin, size):
    slots_here, _, width = held[0].shape
    count = index.shape[0]
    place = begin // size

    def block_of(k):
        def index_map(i, index):
            mine = index[i] // slots_here == k
            return (jnp.where(mine, index[i] % slots_here, 0), place, 0)

        return pl.BlockSpec((1, size, width), index_map)

    return pl.pallas_call(
        functools.partial(pick_kernel, slots_here),
        out_shape=jax.ShapeDtypeStruct((count, size, width), held[0].dtype),
        grid_spec=pltpu.PrefetchScalarGridSpec(
            num_scalar_prefetch=1,
            grid=(count,),
            in_specs=[block_of(k) for k in range(len(held))],
            out_specs=pl.BlockSpec((1, size, width), lambda i, index: (i, 0, 0)),
        ),
        compiler_params=pltpu.CompilerParams(vmem_limit_bytes=24 * 1024 * 1024),
        cost_estimate=pl.CostEstimate(
            flops=0, bytes_accessed=4 * count * size * width, transcendentals=0
        ),
    )(index, *held)


def trade_columns(outgoing):
    pair_count = lax.axis_size("req") // 2
    columns = [[2 * i + k for i in range(pair_count)] for k in range(2)]
    outgoing = outgoing.reshape((pair_count, 2) + outgoing.shape[1:])
    return lax.all_to_all(outgoing, "req", 0, 0, axis_index_groups=columns, tiled=True)


def chunk_index(source_slot, slots_here):
    half = lax.axis_size("req") // 2
    spots = source_slot // slots_here % half
    return ((lax.axis_index("req") % half) ^ spots) * slots_here + source_slot % slots_here


def collect_replicas(arrivals, source_slot, slots_here):
    me = lax.axis_index("req")
    half = lax.axis_size("req") // 2
    side = me % 2
    halves = source_slot // slots_here // half
    width = arrivals[0].shape[3]
    rows_all = sum(arrived.shape[2] for arrived in arrivals)
    result = jnp.zeros((half // 2, 2, rows_all, width), arrivals[0].dtype)
    first_row = 0
    for arrived in arrivals:
        size = arrived.shape[2]

        def wanted_by(receiver):
            begin = pick(halves, receiver, 0) * (half // 2)
            where = (begin, receiver % 2, 0, 0)
            return lax.dynamic_slice(arrived, where, (half // 2, 1, size, width))

        swapped = swap(wanted_by(me ^ 1), 1)
        for rows, column in ((wanted_by(me), side), (swapped, 1 - side)):
            result = lax.dynamic_update_slice(result, rows, (0, column, first_row, 0))
        first_row += size
    return result


def body(
    hidden_in,
    query_in,
    key_in,
    value_in,
    query_gain,
    key_gain,
    cache_keys,
    cache_values,
    cache_block,
    request_lengths,
    out_proj,
    norm_gain,
    expert_ids,
    gate_values,
    old_slots,
    new_replicas,
    slot_weights,
):
    req_count = lax.axis_size("req")
    exp_count = lax.axis_size("exp")
    group_idx = lax.axis_index("req")
    tok_grp, width_q = query_in.shape
    tok_dev, model_width = hidden_in.shape
    head_size = query_gain.shape[0]
    head_count = width_q // head_size
    cache_dev = cache_keys.shape[0]
    pre_len = cache_keys.shape[1]
    req_grp = request_lengths.shape[1]
    lengths = request_lengths[0]
    req_ends = jnp.cumsum(lengths)
    starts = req_ends - lengths
    places = jnp.arange(tok_grp, dtype=jnp.int32)
    member = (places[:, None] >= starts[None, :]) & (places[:, None] < req_ends[None, :])
    request_idx = jnp.arange(req_grp, dtype=jnp.int32)
    segment = jnp.sum(jnp.where(member, request_idx[None, :], 0), axis=1)
    offset = places - jnp.sum(jnp.where(member, starts[None, :], 0), axis=1)
    block_rows = cache_block.reshape(req_count, req_grp)
    my_blocks = lax.dynamic_index_in_dim(block_rows, group_idx, 0, keepdims=False)
    has_cache = my_blocks >= 0
    token_cached = jnp.sum(jnp.where(member & has_cache[None, :], 1, 0), axis=1) > 0
    position = (offset + jnp.where(token_cached, pre_len, 0)).astype(jnp.float32)
    need_blocks, need_requests = compact(block_rows, cache_dev)
    my_requests = lax.dynamic_index_in_dim(need_requests, group_idx, 0, keepdims=False)
    far_cache = fetch_cache(cache_keys, cache_values, need_blocks)
    far_keys, far_values = far_cache[:, 0], far_cache[:, 1]
    held = spread_weights(slot_weights)
    query_n = prepare(query_in.reshape(tok_grp, head_count, head_size), query_gain, position)
    key_n = prepare(key_in.reshape(tok_grp, head_count, head_size), key_gain, position)
    keyset = jnp.concatenate(
        [key_n, far_keys.reshape(cache_dev * pre_len, head_count, head_size)], axis=0
    )
    valueset = jnp.concatenate(
        [
            value_in.reshape(tok_grp, head_count, head_size),
            far_values.reshape(cache_dev * pre_len, head_count, head_size),
        ],
        axis=0,
    )
    key_request = jnp.concatenate([segment, jnp.repeat(my_requests, pre_len)])
    allowed = segment[:, None] == key_request[None, :]
    scores = jnp.einsum("qhd,khd->hqk", query_n, keyset, preferred_element_type=jnp.float32) * (
        1.0 / math.sqrt(head_size)
    )
    scores = jnp.where(allowed[None], scores, -1e30)
    peak = jnp.max(scores, axis=-1, keepdims=True)
    expos = jnp.exp(scores - peak)
    weights = (expos / jnp.sum(expos, axis=-1, keepdims=True)).astype(jnp.bfloat16)
    attended = jnp.einsum("hqk,khd->qhd", weights, valueset, preferred_element_type=jnp.float32)
    attended = attended.astype(jnp.bfloat16).reshape(tok_grp, width_q)
    attended, *held[1:3] = together(attended, *held[1:3])
    attn_out = sum_heads(jnp.dot(attended, out_proj, preferred_element_type=jnp.float32))
    residual = hidden_in.astype(jnp.float32) + attn_out
    normed = (
        residual
        * lax.rsqrt(jnp.mean(residual * residual, axis=-1, keepdims=True) + 1e-06)
        * norm_gain
    ).astype(jnp.bfloat16)
    slot_total = old_slots.shape[0]
    slot_range = jnp.arange(slot_total, dtype=jnp.int32)
    slot_of = jnp.sum(
        jnp.where(old_slots[None, :] == slot_range[:, None], slot_range[None, :], 0), axis=1
    )
    dense_gates = jnp.sum(
        jnp.where(expert_ids[:, :, None] == old_slots[None, None, :], gate_values[:, :, None], 0.0),
        axis=1,
    )
    high_part = dense_gates.astype(jnp.bfloat16)
    low_part = (dense_gates - high_part.astype(jnp.float32)).astype(jnp.bfloat16)
    lanes = max(64, slot_total)
    gap = ((0, 0), (0, lanes - slot_total))
    codes = jnp.concatenate([jnp.pad(high_part, gap), jnp.pad(low_part, gap)], axis=1)
    replica_onehot = new_replicas[:, None] == slot_range[None, :]
    source_slot = jnp.sum(jnp.where(replica_onehot, slot_of[None, :], 0), axis=1)
    slots_here = slot_weights.shape[0]
    index = chunk_index(source_slot, slots_here)
    size = held[0].shape[1] // 2
    mixture, first = mix(
        normed, codes, slot_weights, held, lambda held: take_chunks(held, index, 0, size)
    )
    layer_out = (residual + mixture).astype(jnp.bfloat16)
    second = trade_columns(after(take_chunks(held, index, size, size), first))
    replica_weights = collect_replicas((first, second), source_slot, slots_here)
    return (layer_out, replica_weights.reshape((1,) + slot_weights.shape[1:]))


def solution(mesh):
    in_specs = (
        P(("req", "exp"), None),
        P("req", "exp"),
        P("req", "exp"),
        P("req", "exp"),
        P(),
        P(),
        P("req", None, "exp"),
        P("req", None, "exp"),
        P(),
        P("req", None),
        P("exp", None),
        P(),
        P(("req", "exp"), None),
        P(("req", "exp"), None),
        P(),
        P(),
        P("req", None, None, "exp"),
    )
    out_specs = (P(("req", "exp"), None), P("req", None, None, "exp"))
    return jax.shard_map(body, mesh=mesh, in_specs=in_specs, out_specs=out_specs, check_vma=False)
```

```python
import functools
import math

import jax
import jax.numpy as jnp
from jax import lax
from jax.experimental import pallas as pl
from jax.experimental.pallas import tpu as pltpu
from jax.sharding import PartitionSpec as P


def prepare(values, gain, position):
    vector = values.astype(jnp.float32)
    scaled = vector * lax.rsqrt(jnp.mean(vector * vector, axis=-1, keepdims=True) + 1e-06) * gain
    half_size = scaled.shape[-1] // 2
    frequency = 10000.0 ** (-(jnp.arange(half_size, dtype=jnp.float32) * 2.0 / scaled.shape[-1]))
    angles = position[:, None] * frequency[None, :]
    cosine = jnp.cos(angles)[:, None, :]
    sine_part = jnp.sin(angles)[:, None, :]
    lower_half = scaled[..., :half_size]
    upper_half = scaled[..., half_size:]
    rotated = jnp.concatenate(
        [
            lower_half * cosine - upper_half * sine_part,
            upper_half * cosine + lower_half * sine_part,
        ],
        axis=-1,
    )
    return rotated.astype(jnp.bfloat16)


def compact(block_rows, slots_wanted):
    live = block_rows >= 0
    ranks = jnp.cumsum(live.astype(jnp.int32), axis=1) - 1
    request_idx = jnp.arange(block_rows.shape[1], dtype=jnp.int32)[None, :]
    chosen_blocks = []
    chosen_requests = []
    for slot_num in range(slots_wanted):
        picked = live & (ranks == slot_num)
        chosen_blocks.append(jnp.sum(jnp.where(picked, block_rows, 0), axis=1))
        chosen_requests.append(jnp.sum(jnp.where(picked, request_idx, 0), axis=1))
    return (jnp.stack(chosen_blocks, axis=1), jnp.stack(chosen_requests, axis=1))


def experts_kernel(first_slot_ref, tok_ref, weights_ref, out_ref):
    slot_count, _, model_width, _ = weights_ref.shape
    rows = tok_ref[:, :model_width]
    codes = tok_ref[:, model_width:].astype(jnp.float32)
    half_codes = codes.shape[1] // 2
    lane = lax.broadcasted_iota(jnp.int32, codes.shape, 1)
    total = None
    for slot_num in range(slot_count):
        wanted = first_slot_ref[0] + slot_num
        picked = (lane == wanted) | (lane == wanted + half_codes)
        factor = jnp.sum(jnp.where(picked, codes, 0.0), axis=1, keepdims=True)
        gate_act = jnp.dot(rows, weights_ref[slot_num, 0], preferred_element_type=jnp.float32)
        up_act = jnp.dot(rows, weights_ref[slot_num, 1], preferred_element_type=jnp.float32)
        hidden = gate_act / (1.0 + jnp.exp(-gate_act)) * up_act
        hidden = (hidden * factor).astype(jnp.bfloat16)
        part = lax.dot_general(
            hidden,
            weights_ref[slot_num, 2],
            (((1,), (1,)), ((), ())),
            preferred_element_type=jnp.float32,
        )
        total = part if total is None else total + part
    out_ref[...] = total.astype(out_ref.dtype)


def run_experts(first_slot, tokens, slot_weights, block):
    count, ext_width = tokens.shape
    slots_here, mats, width, hidden_size = slot_weights.shape
    return pl.pallas_call(
        experts_kernel,
        out_shape=jax.ShapeDtypeStruct((count, width), jnp.bfloat16),
        grid=(count // block,),
        in_specs=[
            pl.BlockSpec(memory_space=pltpu.SMEM),
            pl.BlockSpec((block, ext_width), lambda i: (i, 0)),
            pl.BlockSpec((slots_here, mats, width, hidden_size), lambda i: (0, 0, 0, 0)),
        ],
        out_specs=pl.BlockSpec((block, width), lambda i: (i, 0)),
        compiler_params=pltpu.CompilerParams(vmem_limit_bytes=40 * 1024 * 1024),
        cost_estimate=pl.CostEstimate(
            flops=2 * count * width * hidden_size * mats * slots_here,
            bytes_accessed=4 * count * width + 2 * slot_weights.size,
            transcendentals=count * hidden_size * slots_here,
        ),
    )(first_slot, tokens, slot_weights)


def turn_pairs(value, step):
    count = lax.axis_size("req")
    return lax.ppermute(value, "req", [(i, (i + 2 * step) % count) for i in range(count)])


def swap(value, mask):
    count = lax.axis_size("req")
    return lax.ppermute(value, "req", [(i, i ^ mask) for i in range(count)])


def together(*values):
    return lax.optimization_barrier(values)


def after(value, *events):
    return lax.optimization_barrier((value,) + events)[0]


def flip_pair(value):
    count = lax.axis_size("req")
    return lax.ppermute(value, "req", [(i, i ^ 1) for i in range(count)])


def flip_chip(value):
    count = lax.axis_size("exp")
    return lax.ppermute(value, "exp", [(i, i ^ 2) for i in range(count)])


def flip_core(value):
    count = lax.axis_size("exp")
    return lax.ppermute(value, "exp", [(i, i ^ 1) for i in range(count)])


def pick(value, index, axis):
    return lax.dynamic_index_in_dim(value, index, axis, keepdims=False)


def add(first, second):
    return (first.astype(jnp.float32) + second.astype(jnp.float32)).astype(jnp.bfloat16)


def fetch_cache(cache_keys, cache_values, need_blocks):
    me = lax.axis_index("req")
    pair_count = lax.axis_size("req") // 2
    cache_dev = cache_keys.shape[0]
    mine = jnp.stack([cache_keys, cache_values], axis=1)
    column = jnp.stack([mine] + [turn_pairs(mine, step) for step in range(1, pair_count)])
    column = column.reshape((pair_count * cache_dev,) + mine.shape[1:])

    def rows_for(wanted):
        holder = wanted // cache_dev
        back = (me // 2 - holder // 2) % pair_count
        index = back * cache_dev + wanted % cache_dev
        return jnp.stack([pick(column, index[k], 0) for k in range(cache_dev)])

    mine_wanted = pick(need_blocks, me, 0)
    from_pair = flip_pair(rows_for(pick(need_blocks, me ^ 1, 0)))
    here = ((mine_wanted // cache_dev) ^ me) & 1
    wanted = jnp.where((here == 0)[:, None, None, None], rows_for(mine_wanted), from_pair)
    return wanted


def sum_heads(partial_value, events):
    me = lax.axis_index("exp")
    partial_value, *events = together(partial_value, *events)
    rows, width = partial_value.shape
    grid = partial_value.reshape(2, 2, rows // 4, width)
    core, chip = me % 2, me // 2
    got = flip_core(pick(grid, 1 - core, 1).astype(jnp.bfloat16))
    level = pick(grid, core, 1) + got.astype(jnp.float32)
    got = flip_chip(pick(level, 1 - chip, 0).astype(jnp.bfloat16))
    return pick(level, chip, 0) + got.astype(jnp.float32), events


def spread_tokens(pieces):
    width = pieces[0].shape[1]
    stacked = jnp.stack(pieces)
    cut = stacked.shape[1] // 2
    first, second = stacked[:, :cut], stacked[:, cut:]
    first = jnp.stack([first, flip_pair(first)])
    second = jnp.stack([second, flip_chip(second)])
    first_far, second_far = flip_chip(first), flip_pair(second)
    parts = [first, first_far, second, second_far]
    return jnp.concatenate([part.reshape(-1, width) for part in parts])


def gather_sums(total, piece_count):
    rows, width = total.shape
    cut = rows // (8 * piece_count)
    first, second = total.reshape(2, 2, 2, piece_count, cut, width)
    first = add(first[0], flip_chip(first[1]))
    second = add(second[0], flip_pair(second[1]))
    first = add(first[0], flip_pair(first[1]))
    second = add(second[0], flip_chip(second[1]))
    return jnp.concatenate([first, second], axis=1)


def mix(normed, codes, slot_weights, held, pick_first):
    pair_count = lax.axis_size("req") // 2
    first_slot = (lax.axis_index("req") * slot_weights.shape[0]).astype(jnp.int32).reshape(1)
    ext = jnp.concatenate([normed, codes], axis=1)
    pieces = [ext]
    for step in range(1, pair_count):
        source = ext
        if step == 2:
            late = slot_weights.shape[0] + 2
            source, *held[late:] = together(ext, *held[late:])
        pieces.append(turn_pairs(source, step))
    outgoing = pick_first(held)
    outgoing = after(outgoing, *pieces[1:])
    *pieces[2:], outgoing = together(*pieces[2:], outgoing)
    arrived = trade_columns(outgoing)
    total = None
    for begin in range(0, pair_count, 2):
        here = spread_tokens(pieces[begin : begin + 2])
        there = flip_core(here)
        back = flip_core(run_experts(first_slot, there, slot_weights, 256))
        mixed = run_experts(first_slot, here, slot_weights, 256)
        if begin + 2 >= pair_count:
            mixed, arrived = together(mixed, arrived)
        sums = gather_sums(add(mixed, back), 2)
        for offset in range(2):
            step = begin + offset
            part = sums[offset] if step == 0 else turn_pairs(sums[offset], -step)
            part = part.astype(jnp.float32)
            total = part if total is None else total + part
    return total, arrived


def spread_weights(slot_weights):
    me = lax.axis_index("req")
    half = lax.axis_size("req") // 2
    spot = me % half
    slots_here = slot_weights.shape[0]
    chunks = slot_weights.reshape(slots_here, half, -1, slot_weights.shape[-1])
    held = [pick(chunks, spot, 1)]
    near = pick(chunks, spot ^ 1, 1)
    held += [swap(near[k : k + 1], 1) for k in range(slots_here)]
    held += [swap(pick(chunks, spot ^ mask, 1), mask) for mask in range(2, half)]
    return held


def pick_kernel(bounds, index_ref, *refs):
    sources, out_ref = refs[:-1], refs[-1]
    wanted = index_ref[pl.program_id(0)]
    for source, (low, high) in zip(sources, bounds):

        @pl.when((wanted >= low) & (wanted < high))
        def _():
            out_ref[...] = source[...]


def take_chunks(held, index, begin, size):
    width = held[0].shape[2]
    count = index.shape[0]
    place = begin // size
    bounds, low = [], 0
    for part in held:
        bounds.append((low, low + part.shape[0]))
        low += part.shape[0]

    def block_of(low, high):
        def index_map(i, index):
            mine = (index[i] >= low) & (index[i] < high)
            return (jnp.where(mine, index[i] - low, 0), place, 0)

        return pl.BlockSpec((1, size, width), index_map)

    return pl.pallas_call(
        functools.partial(pick_kernel, bounds),
        out_shape=jax.ShapeDtypeStruct((count, size, width), held[0].dtype),
        grid_spec=pltpu.PrefetchScalarGridSpec(
            num_scalar_prefetch=1,
            grid=(count,),
            in_specs=[block_of(*bound) for bound in bounds],
            out_specs=pl.BlockSpec((1, size, width), lambda i, index: (i, 0, 0)),
        ),
        compiler_params=pltpu.CompilerParams(vmem_limit_bytes=24 * 1024 * 1024),
        cost_estimate=pl.CostEstimate(
            flops=0, bytes_accessed=4 * count * size * width, transcendentals=0
        ),
    )(index, *held)


def trade_columns(outgoing):
    pair_count = lax.axis_size("req") // 2
    columns = [[2 * i + k for i in range(pair_count)] for k in range(2)]
    outgoing = outgoing.reshape((pair_count, 2) + outgoing.shape[1:])
    return lax.all_to_all(outgoing, "req", 0, 0, axis_index_groups=columns, tiled=True)


def chunk_index(source_slot, slots_here):
    half = lax.axis_size("req") // 2
    spots = source_slot // slots_here % half
    return ((lax.axis_index("req") % half) ^ spots) * slots_here + source_slot % slots_here


def collect_replicas(arrivals, source_slot, slots_here):
    me = lax.axis_index("req")
    half = lax.axis_size("req") // 2
    side = me % 2
    halves = source_slot // slots_here // half
    width = arrivals[0].shape[3]
    rows_all = sum(arrived.shape[2] for arrived in arrivals)
    result = jnp.zeros((half // 2, 2, rows_all, width), arrivals[0].dtype)
    first_row = 0
    for arrived in arrivals:
        size = arrived.shape[2]

        def wanted_by(receiver):
            begin = pick(halves, receiver, 0) * (half // 2)
            where = (begin, receiver % 2, 0, 0)
            return lax.dynamic_slice(arrived, where, (half // 2, 1, size, width))

        swapped = swap(wanted_by(me ^ 1), 1)
        for rows, column in ((wanted_by(me), side), (swapped, 1 - side)):
            result = lax.dynamic_update_slice(result, rows, (0, column, first_row, 0))
        first_row += size
    return result


def body(
    hidden_in,
    query_in,
    key_in,
    value_in,
    query_gain,
    key_gain,
    cache_keys,
    cache_values,
    cache_block,
    request_lengths,
    out_proj,
    norm_gain,
    expert_ids,
    gate_values,
    old_slots,
    new_replicas,
    slot_weights,
):
    req_count = lax.axis_size("req")
    exp_count = lax.axis_size("exp")
    group_idx = lax.axis_index("req")
    tok_grp, width_q = query_in.shape
    tok_dev, model_width = hidden_in.shape
    head_size = query_gain.shape[0]
    head_count = width_q // head_size
    cache_dev = cache_keys.shape[0]
    pre_len = cache_keys.shape[1]
    req_grp = request_lengths.shape[1]
    lengths = request_lengths[0]
    req_ends = jnp.cumsum(lengths)
    starts = req_ends - lengths
    places = jnp.arange(tok_grp, dtype=jnp.int32)
    member = (places[:, None] >= starts[None, :]) & (places[:, None] < req_ends[None, :])
    request_idx = jnp.arange(req_grp, dtype=jnp.int32)
    segment = jnp.sum(jnp.where(member, request_idx[None, :], 0), axis=1)
    offset = places - jnp.sum(jnp.where(member, starts[None, :], 0), axis=1)
    block_rows = cache_block.reshape(req_count, req_grp)
    my_blocks = lax.dynamic_index_in_dim(block_rows, group_idx, 0, keepdims=False)
    has_cache = my_blocks >= 0
    token_cached = jnp.sum(jnp.where(member & has_cache[None, :], 1, 0), axis=1) > 0
    position = (offset + jnp.where(token_cached, pre_len, 0)).astype(jnp.float32)
    need_blocks, need_requests = compact(block_rows, cache_dev)
    my_requests = lax.dynamic_index_in_dim(need_requests, group_idx, 0, keepdims=False)
    far_cache = fetch_cache(cache_keys, cache_values, need_blocks)
    far_keys, far_values = far_cache[:, 0], far_cache[:, 1]
    held = spread_weights(slot_weights)
    query_n = prepare(query_in.reshape(tok_grp, head_count, head_size), query_gain, position)
    key_n = prepare(key_in.reshape(tok_grp, head_count, head_size), key_gain, position)
    keyset = jnp.concatenate(
        [key_n, far_keys.reshape(cache_dev * pre_len, head_count, head_size)], axis=0
    )
    valueset = jnp.concatenate(
        [
            value_in.reshape(tok_grp, head_count, head_size),
            far_values.reshape(cache_dev * pre_len, head_count, head_size),
        ],
        axis=0,
    )
    key_request = jnp.concatenate([segment, jnp.repeat(my_requests, pre_len)])
    allowed = segment[:, None] == key_request[None, :]
    scores = jnp.einsum("qhd,khd->hqk", query_n, keyset, preferred_element_type=jnp.float32) * (
        1.0 / math.sqrt(head_size)
    )
    scores = jnp.where(allowed[None], scores, -1e30)
    peak = jnp.max(scores, axis=-1, keepdims=True)
    expos = jnp.exp(scores - peak)
    weights = (expos / jnp.sum(expos, axis=-1, keepdims=True)).astype(jnp.bfloat16)
    attended = jnp.einsum("hqk,khd->qhd", weights, valueset, preferred_element_type=jnp.float32)
    attended = attended.astype(jnp.bfloat16).reshape(tok_grp, width_q)
    near = slot_weights.shape[0]
    attended, held[1], held[near + 1] = together(attended, held[1], held[near + 1])
    attn_out, held[2 : near + 1] = sum_heads(
        jnp.dot(attended, out_proj, preferred_element_type=jnp.float32), held[2 : near + 1]
    )
    residual = hidden_in.astype(jnp.float32) + attn_out
    normed = (
        residual
        * lax.rsqrt(jnp.mean(residual * residual, axis=-1, keepdims=True) + 1e-06)
        * norm_gain
    ).astype(jnp.bfloat16)
    slot_total = old_slots.shape[0]
    slot_range = jnp.arange(slot_total, dtype=jnp.int32)
    slot_of = jnp.sum(
        jnp.where(old_slots[None, :] == slot_range[:, None], slot_range[None, :], 0), axis=1
    )
    dense_gates = jnp.sum(
        jnp.where(expert_ids[:, :, None] == old_slots[None, None, :], gate_values[:, :, None], 0.0),
        axis=1,
    )
    high_part = dense_gates.astype(jnp.bfloat16)
    low_part = (dense_gates - high_part.astype(jnp.float32)).astype(jnp.bfloat16)
    lanes = max(64, slot_total)
    gap = ((0, 0), (0, lanes - slot_total))
    codes = jnp.concatenate([jnp.pad(high_part, gap), jnp.pad(low_part, gap)], axis=1)
    replica_onehot = new_replicas[:, None] == slot_range[None, :]
    source_slot = jnp.sum(jnp.where(replica_onehot, slot_of[None, :], 0), axis=1)
    slots_here = slot_weights.shape[0]
    index = chunk_index(source_slot, slots_here)
    last = held[0].shape[1] // 3
    size = held[0].shape[1] - last
    mixture, first = mix(
        normed, codes, slot_weights, held, lambda held: take_chunks(held, index, 0, size)
    )
    layer_out = (residual + mixture).astype(jnp.bfloat16)
    second = trade_columns(after(take_chunks(held, index, size, last), first))
    replica_weights = collect_replicas((first, second), source_slot, slots_here)
    return (layer_out, replica_weights.reshape((1,) + slot_weights.shape[1:]))


def solution(mesh):
    in_specs = (
        P(("req", "exp"), None),
        P("req", "exp"),
        P("req", "exp"),
        P("req", "exp"),
        P(),
        P(),
        P("req", None, "exp"),
        P("req", None, "exp"),
        P(),
        P("req", None),
        P("exp", None),
        P(),
        P(("req", "exp"), None),
        P(("req", "exp"), None),
        P(),
        P(),
        P("req", None, None, "exp"),
    )
    out_specs = (P(("req", "exp"), None), P("req", None, None, "exp"))
    return jax.shard_map(body, mesh=mesh, in_specs=in_specs, out_specs=out_specs, check_vma=False)
```

```python
import functools
import math

import jax
import jax.numpy as jnp
from jax import lax
from jax.experimental import pallas as pl
from jax.experimental.pallas import tpu as pltpu
from jax.sharding import PartitionSpec as P


def prepare(values, gain, position):
    vector = values.astype(jnp.float32)
    scaled = vector * lax.rsqrt(jnp.mean(vector * vector, axis=-1, keepdims=True) + 1e-06) * gain
    half_size = scaled.shape[-1] // 2
    frequency = 10000.0 ** (-(jnp.arange(half_size, dtype=jnp.float32) * 2.0 / scaled.shape[-1]))
    angles = position[:, None] * frequency[None, :]
    cosine = jnp.cos(angles)[:, None, :]
    sine_part = jnp.sin(angles)[:, None, :]
    lower_half = scaled[..., :half_size]
    upper_half = scaled[..., half_size:]
    rotated = jnp.concatenate(
        [
            lower_half * cosine - upper_half * sine_part,
            upper_half * cosine + lower_half * sine_part,
        ],
        axis=-1,
    )
    return rotated.astype(jnp.bfloat16)


def compact(block_rows, slots_wanted):
    live = block_rows >= 0
    ranks = jnp.cumsum(live.astype(jnp.int32), axis=1) - 1
    request_idx = jnp.arange(block_rows.shape[1], dtype=jnp.int32)[None, :]
    chosen_blocks = []
    chosen_requests = []
    for slot_num in range(slots_wanted):
        picked = live & (ranks == slot_num)
        chosen_blocks.append(jnp.sum(jnp.where(picked, block_rows, 0), axis=1))
        chosen_requests.append(jnp.sum(jnp.where(picked, request_idx, 0), axis=1))
    return (jnp.stack(chosen_blocks, axis=1), jnp.stack(chosen_requests, axis=1))


def experts_kernel(first_slot_ref, tok_ref, weights_ref, out_ref):
    slot_count, _, model_width, _ = weights_ref.shape
    rows = tok_ref[:, :model_width]
    codes = tok_ref[:, model_width:].astype(jnp.float32)
    half_codes = codes.shape[1] // 2
    lane = lax.broadcasted_iota(jnp.int32, codes.shape, 1)
    total = None
    for slot_num in range(slot_count):
        wanted = first_slot_ref[0] + slot_num
        picked = (lane == wanted) | (lane == wanted + half_codes)
        factor = jnp.sum(jnp.where(picked, codes, 0.0), axis=1, keepdims=True)
        gate_act = jnp.dot(rows, weights_ref[slot_num, 0], preferred_element_type=jnp.float32)
        up_act = jnp.dot(rows, weights_ref[slot_num, 1], preferred_element_type=jnp.float32)
        hidden = gate_act / (1.0 + jnp.exp(-gate_act)) * up_act
        hidden = (hidden * factor).astype(jnp.bfloat16)
        part = lax.dot_general(
            hidden,
            weights_ref[slot_num, 2],
            (((1,), (1,)), ((), ())),
            preferred_element_type=jnp.float32,
        )
        total = part if total is None else total + part
    out_ref[...] = total.astype(out_ref.dtype)


def run_experts(first_slot, tokens, slot_weights, block):
    count, ext_width = tokens.shape
    slots_here, mats, width, hidden_size = slot_weights.shape
    return pl.pallas_call(
        experts_kernel,
        out_shape=jax.ShapeDtypeStruct((count, width), jnp.bfloat16),
        grid=(count // block,),
        in_specs=[
            pl.BlockSpec(memory_space=pltpu.SMEM),
            pl.BlockSpec((block, ext_width), lambda i: (i, 0)),
            pl.BlockSpec((slots_here, mats, width, hidden_size), lambda i: (0, 0, 0, 0)),
        ],
        out_specs=pl.BlockSpec((block, width), lambda i: (i, 0)),
        compiler_params=pltpu.CompilerParams(vmem_limit_bytes=40 * 1024 * 1024),
        cost_estimate=pl.CostEstimate(
            flops=2 * count * width * hidden_size * mats * slots_here,
            bytes_accessed=4 * count * width + 2 * slot_weights.size,
            transcendentals=count * hidden_size * slots_here,
        ),
    )(first_slot, tokens, slot_weights)


def turn_pairs(value, step):
    count = lax.axis_size("req")
    return lax.ppermute(value, "req", [(i, (i + 2 * step) % count) for i in range(count)])


def swap(value, mask):
    count = lax.axis_size("req")
    return lax.ppermute(value, "req", [(i, i ^ mask) for i in range(count)])


def together(*values):
    return lax.optimization_barrier(values)


def after(value, *events):
    return lax.optimization_barrier((value,) + events)[0]


def flip_pair(value):
    count = lax.axis_size("req")
    return lax.ppermute(value, "req", [(i, i ^ 1) for i in range(count)])


def flip_chip(value):
    count = lax.axis_size("exp")
    return lax.ppermute(value, "exp", [(i, i ^ 2) for i in range(count)])


def flip_core(value):
    count = lax.axis_size("exp")
    return lax.ppermute(value, "exp", [(i, i ^ 1) for i in range(count)])


def pick(value, index, axis):
    return lax.dynamic_index_in_dim(value, index, axis, keepdims=False)


def add(first, second):
    return (first.astype(jnp.float32) + second.astype(jnp.float32)).astype(jnp.bfloat16)


def fetch_cache(cache_keys, cache_values, need_blocks):
    me = lax.axis_index("req")
    pair_count = lax.axis_size("req") // 2
    cache_dev = cache_keys.shape[0]
    mine = jnp.stack([cache_keys, cache_values], axis=1)
    column = jnp.stack([mine] + [turn_pairs(mine, step) for step in range(1, pair_count)])
    column = column.reshape((pair_count * cache_dev,) + mine.shape[1:])

    def rows_for(wanted):
        holder = wanted // cache_dev
        back = (me // 2 - holder // 2) % pair_count
        index = back * cache_dev + wanted % cache_dev
        return jnp.stack([pick(column, index[k], 0) for k in range(cache_dev)])

    mine_wanted = pick(need_blocks, me, 0)
    from_pair = flip_pair(rows_for(pick(need_blocks, me ^ 1, 0)))
    here = ((mine_wanted // cache_dev) ^ me) & 1
    wanted = jnp.where((here == 0)[:, None, None, None], rows_for(mine_wanted), from_pair)
    return wanted


def sum_heads(partial_value):
    me = lax.axis_index("exp")
    rows, width = partial_value.shape
    grid = partial_value.reshape(2, 2, rows // 4, width)
    core, chip = me % 2, me // 2
    got = flip_core(pick(grid, 1 - core, 1).astype(jnp.bfloat16))
    level = pick(grid, core, 1) + got.astype(jnp.float32)
    got = flip_chip(pick(level, 1 - chip, 0).astype(jnp.bfloat16))
    total = pick(level, chip, 0) + got.astype(jnp.float32)
    return total


def spread_tokens(pieces):
    width = pieces[0].shape[1]
    stacked = jnp.stack(pieces)
    cut = stacked.shape[1] // 2
    first, second = stacked[:, :cut], stacked[:, cut:]
    first = jnp.stack([first, flip_pair(first)])
    second = jnp.stack([second, flip_chip(second)])
    first_far, second_far = flip_chip(first), flip_pair(second)
    parts = [first, first_far, second, second_far]
    return jnp.concatenate([part.reshape(-1, width) for part in parts])


def gather_sums(total, piece_count):
    rows, width = total.shape
    cut = rows // (8 * piece_count)
    first, second = total.reshape(2, 2, 2, piece_count, cut, width)
    first = add(first[0], flip_chip(first[1]))
    second = add(second[0], flip_pair(second[1]))
    first = add(first[0], flip_pair(first[1]))
    second = add(second[0], flip_chip(second[1]))
    return jnp.concatenate([first, second], axis=1)


def mix(normed, codes, slot_weights, held, pick_first):
    pair_count = lax.axis_size("req") // 2
    first_slot = (lax.axis_index("req") * slot_weights.shape[0]).astype(jnp.int32).reshape(1)
    ext = jnp.concatenate([normed, codes], axis=1)
    pieces = [ext]
    for step in range(1, pair_count):
        source = ext
        if step == 2:
            source, *held = together(ext, *held)
        pieces.append(turn_pairs(source, step))
    outgoing = pick_first(held)
    pieces = list(together(*pieces))
    outgoing = after(outgoing, pieces[1])
    *pieces[2:], outgoing = together(*pieces[2:], outgoing)
    arrived = trade_columns(outgoing)
    total = None
    for begin in range(0, pair_count, 2):
        here = spread_tokens(pieces[begin : begin + 2])
        there = flip_core(here)
        back = flip_core(run_experts(first_slot, there, slot_weights, 256))
        mixed = run_experts(first_slot, here, slot_weights, 256)
        if begin + 2 >= pair_count:
            mixed, arrived = together(mixed, arrived)
        sums = gather_sums(add(mixed, back), 2)
        for offset in range(2):
            step = begin + offset
            part = sums[offset] if step == 0 else turn_pairs(sums[offset], -step)
            part = part.astype(jnp.float32)
            total = part if total is None else total + part
    return total, arrived


def spread_weights(slot_weights, event):
    me = lax.axis_index("req")
    half = lax.axis_size("req") // 2
    spot = me % half
    slots_here = slot_weights.shape[0]
    chunks = slot_weights.reshape(slots_here, half, -1, slot_weights.shape[-1])
    held = [pick(chunks, spot, 1)]
    near = pick(chunks, spot ^ 1, 1)
    later = after(near, event)
    for slot in range(slots_here):
        source = near if slot == 0 else later
        held.append(swap(source[slot : slot + 1], 1))
    held += [swap(pick(chunks, spot ^ mask, 1), mask) for mask in range(2, half)]
    return held


def pick_kernel(bounds, index_ref, *refs):
    sources, out_ref = refs[:-1], refs[-1]
    wanted = index_ref[pl.program_id(0)]
    for source, (low, high) in zip(sources, bounds):

        @pl.when((wanted >= low) & (wanted < high))
        def _():
            out_ref[...] = source[...]


def take_chunks(held, index, begin, size):
    width = held[0].shape[2]
    count = index.shape[0]
    place = begin // size
    bounds, low = [], 0
    for part in held:
        bounds.append((low, low + part.shape[0]))
        low += part.shape[0]

    def block_of(low, high):
        def index_map(i, index):
            mine = (index[i] >= low) & (index[i] < high)
            return (jnp.where(mine, index[i] - low, 0), place, 0)

        return pl.BlockSpec((1, size, width), index_map)

    return pl.pallas_call(
        functools.partial(pick_kernel, bounds),
        out_shape=jax.ShapeDtypeStruct((count, size, width), held[0].dtype),
        grid_spec=pltpu.PrefetchScalarGridSpec(
            num_scalar_prefetch=1,
            grid=(count,),
            in_specs=[block_of(*bound) for bound in bounds],
            out_specs=pl.BlockSpec((1, size, width), lambda i, index: (i, 0, 0)),
        ),
        compiler_params=pltpu.CompilerParams(vmem_limit_bytes=24 * 1024 * 1024),
        cost_estimate=pl.CostEstimate(
            flops=0, bytes_accessed=4 * count * size * width, transcendentals=0
        ),
    )(index, *held)


def trade_columns(outgoing):
    pair_count = lax.axis_size("req") // 2
    columns = [[2 * i + k for i in range(pair_count)] for k in range(2)]
    outgoing = outgoing.reshape((pair_count, 2) + outgoing.shape[1:])
    return lax.all_to_all(outgoing, "req", 0, 0, axis_index_groups=columns, tiled=True)


def chunk_index(source_slot, slots_here):
    half = lax.axis_size("req") // 2
    spots = source_slot // slots_here % half
    return ((lax.axis_index("req") % half) ^ spots) * slots_here + source_slot % slots_here


def collect_replicas(arrivals, source_slot, slots_here):
    me = lax.axis_index("req")
    half = lax.axis_size("req") // 2
    side = me % 2
    halves = source_slot // slots_here // half
    width = arrivals[0].shape[3]
    rows_all = sum(arrived.shape[2] for arrived in arrivals)
    result = jnp.zeros((half // 2, 2, rows_all, width), arrivals[0].dtype)
    first_row = 0
    for arrived in arrivals:
        size = arrived.shape[2]

        def wanted_by(receiver):
            begin = pick(halves, receiver, 0) * (half // 2)
            where = (begin, receiver % 2, 0, 0)
            return lax.dynamic_slice(arrived, where, (half // 2, 1, size, width))

        swapped = swap(wanted_by(me ^ 1), 1)
        for rows, column in ((wanted_by(me), side), (swapped, 1 - side)):
            result = lax.dynamic_update_slice(result, rows, (0, column, first_row, 0))
        first_row += size
    return result


def body(
    hidden_in,
    query_in,
    key_in,
    value_in,
    query_gain,
    key_gain,
    cache_keys,
    cache_values,
    cache_block,
    request_lengths,
    out_proj,
    norm_gain,
    expert_ids,
    gate_values,
    old_slots,
    new_replicas,
    slot_weights,
):
    req_count = lax.axis_size("req")
    exp_count = lax.axis_size("exp")
    group_idx = lax.axis_index("req")
    tok_grp, width_q = query_in.shape
    tok_dev, model_width = hidden_in.shape
    head_size = query_gain.shape[0]
    head_count = width_q // head_size
    cache_dev = cache_keys.shape[0]
    pre_len = cache_keys.shape[1]
    req_grp = request_lengths.shape[1]
    lengths = request_lengths[0]
    req_ends = jnp.cumsum(lengths)
    starts = req_ends - lengths
    places = jnp.arange(tok_grp, dtype=jnp.int32)
    member = (places[:, None] >= starts[None, :]) & (places[:, None] < req_ends[None, :])
    request_idx = jnp.arange(req_grp, dtype=jnp.int32)
    segment = jnp.sum(jnp.where(member, request_idx[None, :], 0), axis=1)
    offset = places - jnp.sum(jnp.where(member, starts[None, :], 0), axis=1)
    block_rows = cache_block.reshape(req_count, req_grp)
    my_blocks = lax.dynamic_index_in_dim(block_rows, group_idx, 0, keepdims=False)
    has_cache = my_blocks >= 0
    token_cached = jnp.sum(jnp.where(member & has_cache[None, :], 1, 0), axis=1) > 0
    position = (offset + jnp.where(token_cached, pre_len, 0)).astype(jnp.float32)
    need_blocks, need_requests = compact(block_rows, cache_dev)
    my_requests = lax.dynamic_index_in_dim(need_requests, group_idx, 0, keepdims=False)
    far_cache = fetch_cache(cache_keys, cache_values, need_blocks)
    far_keys, far_values = far_cache[:, 0], far_cache[:, 1]
    held = spread_weights(slot_weights, far_cache)
    query_n = prepare(query_in.reshape(tok_grp, head_count, head_size), query_gain, position)
    key_n = prepare(key_in.reshape(tok_grp, head_count, head_size), key_gain, position)
    keyset = jnp.concatenate(
        [key_n, far_keys.reshape(cache_dev * pre_len, head_count, head_size)], axis=0
    )
    valueset = jnp.concatenate(
        [
            value_in.reshape(tok_grp, head_count, head_size),
            far_values.reshape(cache_dev * pre_len, head_count, head_size),
        ],
        axis=0,
    )
    key_request = jnp.concatenate([segment, jnp.repeat(my_requests, pre_len)])
    allowed = segment[:, None] == key_request[None, :]
    scores = jnp.einsum("qhd,khd->hqk", query_n, keyset, preferred_element_type=jnp.float32) * (
        1.0 / math.sqrt(head_size)
    )
    scores = jnp.where(allowed[None], scores, -1e30)
    peak = jnp.max(scores, axis=-1, keepdims=True)
    expos = jnp.exp(scores - peak)
    weights = (expos / jnp.sum(expos, axis=-1, keepdims=True)).astype(jnp.bfloat16)
    attended = jnp.einsum("hqk,khd->qhd", weights, valueset, preferred_element_type=jnp.float32)
    attended = attended.astype(jnp.bfloat16).reshape(tok_grp, width_q)
    near = slot_weights.shape[0]
    attended, held[1], held[near + 1] = together(attended, held[1], held[near + 1])
    attn_out = sum_heads(jnp.dot(attended, out_proj, preferred_element_type=jnp.float32))
    residual = hidden_in.astype(jnp.float32) + attn_out
    normed = (
        residual
        * lax.rsqrt(jnp.mean(residual * residual, axis=-1, keepdims=True) + 1e-06)
        * norm_gain
    ).astype(jnp.bfloat16)
    slot_total = old_slots.shape[0]
    slot_range = jnp.arange(slot_total, dtype=jnp.int32)
    slot_of = jnp.sum(
        jnp.where(old_slots[None, :] == slot_range[:, None], slot_range[None, :], 0), axis=1
    )
    dense_gates = jnp.sum(
        jnp.where(expert_ids[:, :, None] == old_slots[None, None, :], gate_values[:, :, None], 0.0),
        axis=1,
    )
    high_part = dense_gates.astype(jnp.bfloat16)
    low_part = (dense_gates - high_part.astype(jnp.float32)).astype(jnp.bfloat16)
    lanes = max(64, slot_total)
    gap = ((0, 0), (0, lanes - slot_total))
    codes = jnp.concatenate([jnp.pad(high_part, gap), jnp.pad(low_part, gap)], axis=1)
    replica_onehot = new_replicas[:, None] == slot_range[None, :]
    source_slot = jnp.sum(jnp.where(replica_onehot, slot_of[None, :], 0), axis=1)
    slots_here = slot_weights.shape[0]
    index = chunk_index(source_slot, slots_here)
    last = held[0].shape[1] // 3
    size = held[0].shape[1] - last
    mixture, first = mix(
        normed, codes, slot_weights, held, lambda held: take_chunks(held, index, 0, size)
    )
    layer_out = (residual + mixture).astype(jnp.bfloat16)
    second = trade_columns(after(take_chunks(held, index, size, last), first))
    replica_weights = collect_replicas((first, second), source_slot, slots_here)
    return (layer_out, replica_weights.reshape((1,) + slot_weights.shape[1:]))


def solution(mesh):
    in_specs = (
        P(("req", "exp"), None),
        P("req", "exp"),
        P("req", "exp"),
        P("req", "exp"),
        P(),
        P(),
        P("req", None, "exp"),
        P("req", None, "exp"),
        P(),
        P("req", None),
        P("exp", None),
        P(),
        P(("req", "exp"), None),
        P(("req", "exp"), None),
        P(),
        P(),
        P("req", None, None, "exp"),
    )
    out_specs = (P(("req", "exp"), None), P("req", None, None, "exp"))
    return jax.shard_map(body, mesh=mesh, in_specs=in_specs, out_specs=out_specs, check_vma=False)
```

```python
import functools
import math

import jax
import jax.numpy as jnp
from jax import lax
from jax.experimental import pallas as pl
from jax.experimental.pallas import tpu as pltpu
from jax.sharding import PartitionSpec as P


def prepare(values, gain, position):
    vector = values.astype(jnp.float32)
    scaled = vector * lax.rsqrt(jnp.mean(vector * vector, axis=-1, keepdims=True) + 1e-06) * gain
    half_size = scaled.shape[-1] // 2
    frequency = 10000.0 ** (-(jnp.arange(half_size, dtype=jnp.float32) * 2.0 / scaled.shape[-1]))
    angles = position[:, None] * frequency[None, :]
    cosine = jnp.cos(angles)[:, None, :]
    sine_part = jnp.sin(angles)[:, None, :]
    lower_half = scaled[..., :half_size]
    upper_half = scaled[..., half_size:]
    rotated = jnp.concatenate(
        [
            lower_half * cosine - upper_half * sine_part,
            upper_half * cosine + lower_half * sine_part,
        ],
        axis=-1,
    )
    return rotated.astype(jnp.bfloat16)


def compact(block_rows, slots_wanted):
    live = block_rows >= 0
    ranks = jnp.cumsum(live.astype(jnp.int32), axis=1) - 1
    request_idx = jnp.arange(block_rows.shape[1], dtype=jnp.int32)[None, :]
    chosen_blocks = []
    chosen_requests = []
    for slot_num in range(slots_wanted):
        picked = live & (ranks == slot_num)
        chosen_blocks.append(jnp.sum(jnp.where(picked, block_rows, 0), axis=1))
        chosen_requests.append(jnp.sum(jnp.where(picked, request_idx, 0), axis=1))
    return (jnp.stack(chosen_blocks, axis=1), jnp.stack(chosen_requests, axis=1))


def experts_kernel(first_slot_ref, tok_ref, weights_ref, out_ref):
    slot_count, _, model_width, _ = weights_ref.shape
    rows = tok_ref[:, :model_width]
    codes = tok_ref[:, model_width:].astype(jnp.float32)
    half_codes = codes.shape[1] // 2
    lane = lax.broadcasted_iota(jnp.int32, codes.shape, 1)
    total = None
    for slot_num in range(slot_count):
        wanted = first_slot_ref[0] + slot_num
        picked = (lane == wanted) | (lane == wanted + half_codes)
        factor = jnp.sum(jnp.where(picked, codes, 0.0), axis=1, keepdims=True)
        gate_act = jnp.dot(rows, weights_ref[slot_num, 0], preferred_element_type=jnp.float32)
        up_act = jnp.dot(rows, weights_ref[slot_num, 1], preferred_element_type=jnp.float32)
        hidden = gate_act / (1.0 + jnp.exp(-gate_act)) * up_act
        hidden = (hidden * factor).astype(jnp.bfloat16)
        part = lax.dot_general(
            hidden,
            weights_ref[slot_num, 2],
            (((1,), (1,)), ((), ())),
            preferred_element_type=jnp.float32,
        )
        total = part if total is None else total + part
    out_ref[...] = total.astype(out_ref.dtype)


def run_experts(first_slot, tokens, slot_weights, block):
    count, ext_width = tokens.shape
    slots_here, mats, width, hidden_size = slot_weights.shape
    return pl.pallas_call(
        experts_kernel,
        out_shape=jax.ShapeDtypeStruct((count, width), jnp.bfloat16),
        grid=(count // block,),
        in_specs=[
            pl.BlockSpec(memory_space=pltpu.SMEM),
            pl.BlockSpec((block, ext_width), lambda i: (i, 0)),
            pl.BlockSpec((slots_here, mats, width, hidden_size), lambda i: (0, 0, 0, 0)),
        ],
        out_specs=pl.BlockSpec((block, width), lambda i: (i, 0)),
        compiler_params=pltpu.CompilerParams(vmem_limit_bytes=40 * 1024 * 1024),
        cost_estimate=pl.CostEstimate(
            flops=2 * count * width * hidden_size * mats * slots_here,
            bytes_accessed=4 * count * width + 2 * slot_weights.size,
            transcendentals=count * hidden_size * slots_here,
        ),
    )(first_slot, tokens, slot_weights)


def turn_pairs(value, step):
    count = lax.axis_size("req")
    return lax.ppermute(value, "req", [(i, (i + 2 * step) % count) for i in range(count)])


def swap(value, mask):
    count = lax.axis_size("req")
    return lax.ppermute(value, "req", [(i, i ^ mask) for i in range(count)])


def together(*values):
    return lax.optimization_barrier(values)


def after(value, *events):
    return lax.optimization_barrier((value,) + events)[0]


def flip_pair(value):
    count = lax.axis_size("req")
    return lax.ppermute(value, "req", [(i, i ^ 1) for i in range(count)])


def flip_chip(value):
    count = lax.axis_size("exp")
    return lax.ppermute(value, "exp", [(i, i ^ 2) for i in range(count)])


def flip_core(value):
    count = lax.axis_size("exp")
    return lax.ppermute(value, "exp", [(i, i ^ 1) for i in range(count)])


def pick(value, index, axis):
    return lax.dynamic_index_in_dim(value, index, axis, keepdims=False)


def add(first, second):
    return (first.astype(jnp.float32) + second.astype(jnp.float32)).astype(jnp.bfloat16)


def fetch_cache(cache_keys, cache_values, need_blocks):
    me = lax.axis_index("req")
    pair_count = lax.axis_size("req") // 2
    cache_dev = cache_keys.shape[0]
    mine = jnp.stack([cache_keys, cache_values], axis=1)
    column = jnp.stack([mine] + [turn_pairs(mine, step) for step in range(1, pair_count)])
    column = column.reshape((pair_count * cache_dev,) + mine.shape[1:])

    def rows_for(wanted):
        holder = wanted // cache_dev
        back = (me // 2 - holder // 2) % pair_count
        index = back * cache_dev + wanted % cache_dev
        return jnp.stack([pick(column, index[k], 0) for k in range(cache_dev)])

    mine_wanted = pick(need_blocks, me, 0)
    from_pair = flip_pair(rows_for(pick(need_blocks, me ^ 1, 0)))
    here = ((mine_wanted // cache_dev) ^ me) & 1
    wanted = jnp.where((here == 0)[:, None, None, None], rows_for(mine_wanted), from_pair)
    return wanted


def sum_heads(partial_value):
    me = lax.axis_index("exp")
    rows, width = partial_value.shape
    grid = partial_value.reshape(2, 2, rows // 4, width)
    core, chip = me % 2, me // 2
    got = flip_core(pick(grid, 1 - core, 1).astype(jnp.bfloat16))
    level = pick(grid, core, 1) + got.astype(jnp.float32)
    got = flip_chip(pick(level, 1 - chip, 0).astype(jnp.bfloat16))
    return pick(level, chip, 0) + got.astype(jnp.float32)


def spread_tokens(pieces):
    width = pieces[0].shape[1]
    stacked = jnp.stack(pieces)
    cut = stacked.shape[1] // 2
    first, second = stacked[:, :cut], stacked[:, cut:]
    first = jnp.stack([first, flip_pair(first)])
    second = jnp.stack([second, flip_chip(second)])
    first_far, second_far = flip_chip(first), flip_pair(second)
    parts = [first, first_far, second, second_far]
    return jnp.concatenate([part.reshape(-1, width) for part in parts])


def gather_sums(total, piece_count):
    rows, width = total.shape
    cut = rows // (8 * piece_count)
    first, second = total.reshape(2, 2, 2, piece_count, cut, width)
    first = add(first[0], flip_chip(first[1]))
    second = add(second[0], flip_pair(second[1]))
    first = add(first[0], flip_pair(first[1]))
    second = add(second[0], flip_chip(second[1]))
    return jnp.concatenate([first, second], axis=1)


def mix(normed, codes, slot_weights, held, pick_first):
    pair_count = lax.axis_size("req") // 2
    first_slot = (lax.axis_index("req") * slot_weights.shape[0]).astype(jnp.int32).reshape(1)
    ext = jnp.concatenate([normed, codes], axis=1)
    pieces = [ext]
    for step in range(1, pair_count):
        source = ext
        if step == 2:
            source, *held[3:] = together(ext, *held[3:])
        pieces.append(turn_pairs(source, step))
    outgoing = pick_first(held)
    outgoing = after(outgoing, *pieces[1:])
    *pieces[2:], outgoing = together(*pieces[2:], outgoing)
    arrived = trade_columns(outgoing)
    total, ready = None, []
    for begin in range(0, pair_count, 2):
        here = spread_tokens(pieces[begin : begin + 2])
        there = flip_core(here)
        if begin + 2 >= pair_count:
            there, arrived = together(there, arrived)
        back = flip_core(run_experts(first_slot, there, slot_weights, 256))
        mixed = run_experts(first_slot, here, slot_weights, 256)
        sums = gather_sums(add(mixed, back), 2)
        ready.append(sums)
        for offset in range(2):
            step = begin + offset
            part = sums[offset] if step == 0 else turn_pairs(sums[offset], -step)
            part = part.astype(jnp.float32)
            total = part if total is None else total + part
    return total, arrived, ready


def spread_weights(slot_weights):
    me = lax.axis_index("req")
    half = lax.axis_size("req") // 2
    spot = me % half
    slots_here = slot_weights.shape[0]
    chunks = slot_weights.reshape(slots_here, half, -1, slot_weights.shape[-1])
    held = [pick(chunks, spot, 1)]
    for mask in range(1, half):
        held.append(swap(pick(chunks, spot ^ mask, 1), mask))
    return held


def pick_kernel(slots_here, index_ref, *refs):
    sources, out_ref = refs[:-1], refs[-1]
    holder = index_ref[pl.program_id(0)] // slots_here
    for k, source in enumerate(sources):

        @pl.when(holder == k)
        def _():
            out_ref[...] = source[...]


def take_chunks(held, index, begin, size):
    slots_here, _, width = held[0].shape
    count = index.shape[0]
    place = begin // size

    def block_of(k):
        def index_map(i, index):
            mine = index[i] // slots_here == k
            return (jnp.where(mine, index[i] % slots_here, 0), place, 0)

        return pl.BlockSpec((1, size, width), index_map)

    return pl.pallas_call(
        functools.partial(pick_kernel, slots_here),
        out_shape=jax.ShapeDtypeStruct((count, size, width), held[0].dtype),
        grid_spec=pltpu.PrefetchScalarGridSpec(
            num_scalar_prefetch=1,
            grid=(count,),
            in_specs=[block_of(k) for k in range(len(held))],
            out_specs=pl.BlockSpec((1, size, width), lambda i, index: (i, 0, 0)),
        ),
        compiler_params=pltpu.CompilerParams(vmem_limit_bytes=24 * 1024 * 1024),
        cost_estimate=pl.CostEstimate(
            flops=0, bytes_accessed=4 * count * size * width, transcendentals=0
        ),
    )(index, *held)


def trade_columns(outgoing):
    pair_count = lax.axis_size("req") // 2
    columns = [[2 * i + k for i in range(pair_count)] for k in range(2)]
    outgoing = outgoing.reshape((pair_count, 2) + outgoing.shape[1:])
    return lax.all_to_all(outgoing, "req", 0, 0, axis_index_groups=columns, tiled=True)


def chunk_index(source_slot, slots_here):
    half = lax.axis_size("req") // 2
    spots = source_slot // slots_here % half
    return ((lax.axis_index("req") % half) ^ spots) * slots_here + source_slot % slots_here


def collect_replicas(arrivals, source_slot, slots_here):
    me = lax.axis_index("req")
    half = lax.axis_size("req") // 2
    side = me % 2
    halves = source_slot // slots_here // half
    width = arrivals[0].shape[3]
    rows_all = sum(arrived.shape[2] for arrived in arrivals)
    result = jnp.zeros((half // 2, 2, rows_all, width), arrivals[0].dtype)
    first_row = 0
    for arrived in arrivals:
        size = arrived.shape[2]

        def wanted_by(receiver):
            begin = pick(halves, receiver, 0) * (half // 2)
            where = (begin, receiver % 2, 0, 0)
            return lax.dynamic_slice(arrived, where, (half // 2, 1, size, width))

        swapped = swap(wanted_by(me ^ 1), 1)
        for rows, column in ((wanted_by(me), side), (swapped, 1 - side)):
            result = lax.dynamic_update_slice(result, rows, (0, column, first_row, 0))
        first_row += size
    return result


def body(
    hidden_in,
    query_in,
    key_in,
    value_in,
    query_gain,
    key_gain,
    cache_keys,
    cache_values,
    cache_block,
    request_lengths,
    out_proj,
    norm_gain,
    expert_ids,
    gate_values,
    old_slots,
    new_replicas,
    slot_weights,
):
    req_count = lax.axis_size("req")
    exp_count = lax.axis_size("exp")
    group_idx = lax.axis_index("req")
    tok_grp, width_q = query_in.shape
    tok_dev, model_width = hidden_in.shape
    head_size = query_gain.shape[0]
    head_count = width_q // head_size
    cache_dev = cache_keys.shape[0]
    pre_len = cache_keys.shape[1]
    req_grp = request_lengths.shape[1]
    lengths = request_lengths[0]
    req_ends = jnp.cumsum(lengths)
    starts = req_ends - lengths
    places = jnp.arange(tok_grp, dtype=jnp.int32)
    member = (places[:, None] >= starts[None, :]) & (places[:, None] < req_ends[None, :])
    request_idx = jnp.arange(req_grp, dtype=jnp.int32)
    segment = jnp.sum(jnp.where(member, request_idx[None, :], 0), axis=1)
    offset = places - jnp.sum(jnp.where(member, starts[None, :], 0), axis=1)
    block_rows = cache_block.reshape(req_count, req_grp)
    my_blocks = lax.dynamic_index_in_dim(block_rows, group_idx, 0, keepdims=False)
    has_cache = my_blocks >= 0
    token_cached = jnp.sum(jnp.where(member & has_cache[None, :], 1, 0), axis=1) > 0
    position = (offset + jnp.where(token_cached, pre_len, 0)).astype(jnp.float32)
    need_blocks, need_requests = compact(block_rows, cache_dev)
    my_requests = lax.dynamic_index_in_dim(need_requests, group_idx, 0, keepdims=False)
    far_cache = fetch_cache(cache_keys, cache_values, need_blocks)
    far_keys, far_values = far_cache[:, 0], far_cache[:, 1]
    held = spread_weights(slot_weights)
    query_n = prepare(query_in.reshape(tok_grp, head_count, head_size), query_gain, position)
    key_n = prepare(key_in.reshape(tok_grp, head_count, head_size), key_gain, position)
    keyset = jnp.concatenate(
        [key_n, far_keys.reshape(cache_dev * pre_len, head_count, head_size)], axis=0
    )
    valueset = jnp.concatenate(
        [
            value_in.reshape(tok_grp, head_count, head_size),
            far_values.reshape(cache_dev * pre_len, head_count, head_size),
        ],
        axis=0,
    )
    key_request = jnp.concatenate([segment, jnp.repeat(my_requests, pre_len)])
    allowed = segment[:, None] == key_request[None, :]
    scores = jnp.einsum("qhd,khd->hqk", query_n, keyset, preferred_element_type=jnp.float32) * (
        1.0 / math.sqrt(head_size)
    )
    scores = jnp.where(allowed[None], scores, -1e30)
    peak = jnp.max(scores, axis=-1, keepdims=True)
    expos = jnp.exp(scores - peak)
    weights = (expos / jnp.sum(expos, axis=-1, keepdims=True)).astype(jnp.bfloat16)
    attended = jnp.einsum("hqk,khd->qhd", weights, valueset, preferred_element_type=jnp.float32)
    attended = attended.astype(jnp.bfloat16).reshape(tok_grp, width_q)
    attended, *held[1:3] = together(attended, *held[1:3])
    attn_out = sum_heads(jnp.dot(attended, out_proj, preferred_element_type=jnp.float32))
    residual = hidden_in.astype(jnp.float32) + attn_out
    normed = (
        residual
        * lax.rsqrt(jnp.mean(residual * residual, axis=-1, keepdims=True) + 1e-06)
        * norm_gain
    ).astype(jnp.bfloat16)
    slot_total = old_slots.shape[0]
    slot_range = jnp.arange(slot_total, dtype=jnp.int32)
    slot_of = jnp.sum(
        jnp.where(old_slots[None, :] == slot_range[:, None], slot_range[None, :], 0), axis=1
    )
    dense_gates = jnp.sum(
        jnp.where(expert_ids[:, :, None] == old_slots[None, None, :], gate_values[:, :, None], 0.0),
        axis=1,
    )
    high_part = dense_gates.astype(jnp.bfloat16)
    low_part = (dense_gates - high_part.astype(jnp.float32)).astype(jnp.bfloat16)
    lanes = max(64, slot_total)
    gap = ((0, 0), (0, lanes - slot_total))
    codes = jnp.concatenate([jnp.pad(high_part, gap), jnp.pad(low_part, gap)], axis=1)
    replica_onehot = new_replicas[:, None] == slot_range[None, :]
    source_slot = jnp.sum(jnp.where(replica_onehot, slot_of[None, :], 0), axis=1)
    slots_here = slot_weights.shape[0]
    index = chunk_index(source_slot, slots_here)
    size = held[0].shape[1] // 2
    mixture, first, ready = mix(
        normed, codes, slot_weights, held, lambda held: take_chunks(held, index, 0, size)
    )
    layer_out = (residual + mixture).astype(jnp.bfloat16)
    second = trade_columns(after(take_chunks(held, index, size, size), first))
    second = after(second, *ready)
    replica_weights = collect_replicas((first, second), source_slot, slots_here)
    return (layer_out, replica_weights.reshape((1,) + slot_weights.shape[1:]))


def solution(mesh):
    in_specs = (
        P(("req", "exp"), None),
        P("req", "exp"),
        P("req", "exp"),
        P("req", "exp"),
        P(),
        P(),
        P("req", None, "exp"),
        P("req", None, "exp"),
        P(),
        P("req", None),
        P("exp", None),
        P(),
        P(("req", "exp"), None),
        P(("req", "exp"), None),
        P(),
        P(),
        P("req", None, None, "exp"),
    )
    out_specs = (P(("req", "exp"), None), P("req", None, None, "exp"))
    return jax.shard_map(body, mesh=mesh, in_specs=in_specs, out_specs=out_specs, check_vma=False)
```

```python
import functools
import math

import jax
import jax.numpy as jnp
from jax import lax
from jax.experimental import pallas as pl
from jax.experimental.pallas import tpu as pltpu
from jax.sharding import PartitionSpec as P


def prepare(values, gain, position):
    vector = values.astype(jnp.float32)
    scaled = vector * lax.rsqrt(jnp.mean(vector * vector, axis=-1, keepdims=True) + 1e-06) * gain
    half_size = scaled.shape[-1] // 2
    frequency = 10000.0 ** (-(jnp.arange(half_size, dtype=jnp.float32) * 2.0 / scaled.shape[-1]))
    angles = position[:, None] * frequency[None, :]
    cosine = jnp.cos(angles)[:, None, :]
    sine_part = jnp.sin(angles)[:, None, :]
    lower_half = scaled[..., :half_size]
    upper_half = scaled[..., half_size:]
    rotated = jnp.concatenate(
        [
            lower_half * cosine - upper_half * sine_part,
            upper_half * cosine + lower_half * sine_part,
        ],
        axis=-1,
    )
    return rotated.astype(jnp.bfloat16)


def compact(block_rows, slots_wanted):
    live = block_rows >= 0
    ranks = jnp.cumsum(live.astype(jnp.int32), axis=1) - 1
    request_idx = jnp.arange(block_rows.shape[1], dtype=jnp.int32)[None, :]
    chosen_blocks = []
    chosen_requests = []
    for slot_num in range(slots_wanted):
        picked = live & (ranks == slot_num)
        chosen_blocks.append(jnp.sum(jnp.where(picked, block_rows, 0), axis=1))
        chosen_requests.append(jnp.sum(jnp.where(picked, request_idx, 0), axis=1))
    return (jnp.stack(chosen_blocks, axis=1), jnp.stack(chosen_requests, axis=1))


def experts_kernel(first_slot_ref, tok_ref, weights_ref, out_ref):
    slot_count, _, model_width, _ = weights_ref.shape
    rows = tok_ref[:, :model_width]
    codes = tok_ref[:, model_width:].astype(jnp.float32)
    half_codes = codes.shape[1] // 2
    lane = lax.broadcasted_iota(jnp.int32, codes.shape, 1)
    total = None
    for slot_num in range(slot_count):
        wanted = first_slot_ref[0] + slot_num
        picked = (lane == wanted) | (lane == wanted + half_codes)
        factor = jnp.sum(jnp.where(picked, codes, 0.0), axis=1, keepdims=True)
        gate_act = jnp.dot(rows, weights_ref[slot_num, 0], preferred_element_type=jnp.float32)
        up_act = jnp.dot(rows, weights_ref[slot_num, 1], preferred_element_type=jnp.float32)
        hidden = gate_act / (1.0 + jnp.exp(-gate_act)) * up_act
        hidden = (hidden * factor).astype(jnp.bfloat16)
        part = lax.dot_general(
            hidden,
            weights_ref[slot_num, 2],
            (((1,), (1,)), ((), ())),
            preferred_element_type=jnp.float32,
        )
        total = part if total is None else total + part
    out_ref[...] = total.astype(out_ref.dtype)


def run_experts(first_slot, tokens, slot_weights, block):
    count, ext_width = tokens.shape
    slots_here, mats, width, hidden_size = slot_weights.shape
    return pl.pallas_call(
        experts_kernel,
        out_shape=jax.ShapeDtypeStruct((count, width), jnp.bfloat16),
        grid=(count // block,),
        in_specs=[
            pl.BlockSpec(memory_space=pltpu.SMEM),
            pl.BlockSpec((block, ext_width), lambda i: (i, 0)),
            pl.BlockSpec((slots_here, mats, width, hidden_size), lambda i: (0, 0, 0, 0)),
        ],
        out_specs=pl.BlockSpec((block, width), lambda i: (i, 0)),
        compiler_params=pltpu.CompilerParams(vmem_limit_bytes=40 * 1024 * 1024),
        cost_estimate=pl.CostEstimate(
            flops=2 * count * width * hidden_size * mats * slots_here,
            bytes_accessed=4 * count * width + 2 * slot_weights.size,
            transcendentals=count * hidden_size * slots_here,
        ),
    )(first_slot, tokens, slot_weights)


def turn_pairs(value, step):
    count = lax.axis_size("req")
    return lax.ppermute(value, "req", [(i, (i + 2 * step) % count) for i in range(count)])


def swap(value, mask):
    count = lax.axis_size("req")
    return lax.ppermute(value, "req", [(i, i ^ mask) for i in range(count)])


def together(*values):
    return lax.optimization_barrier(values)


def after(value, *events):
    return lax.optimization_barrier((value,) + events)[0]


def flip_pair(value):
    count = lax.axis_size("req")
    return lax.ppermute(value, "req", [(i, i ^ 1) for i in range(count)])


def flip_chip(value):
    count = lax.axis_size("exp")
    return lax.ppermute(value, "exp", [(i, i ^ 2) for i in range(count)])


def flip_core(value):
    count = lax.axis_size("exp")
    return lax.ppermute(value, "exp", [(i, i ^ 1) for i in range(count)])


def pick(value, index, axis):
    return lax.dynamic_index_in_dim(value, index, axis, keepdims=False)


def add(first, second):
    return (first.astype(jnp.float32) + second.astype(jnp.float32)).astype(jnp.bfloat16)


def fetch_cache(cache_keys, cache_values, need_blocks):
    me = lax.axis_index("req")
    pair_count = lax.axis_size("req") // 2
    cache_dev = cache_keys.shape[0]
    mine = jnp.stack([cache_keys, cache_values], axis=1)
    column = jnp.stack([mine] + [turn_pairs(mine, step) for step in range(1, pair_count)])
    column = column.reshape((pair_count * cache_dev,) + mine.shape[1:])

    def rows_for(wanted):
        holder = wanted // cache_dev
        back = (me // 2 - holder // 2) % pair_count
        index = back * cache_dev + wanted % cache_dev
        return jnp.stack([pick(column, index[k], 0) for k in range(cache_dev)])

    mine_wanted = pick(need_blocks, me, 0)
    from_pair = flip_pair(rows_for(pick(need_blocks, me ^ 1, 0)))
    here = ((mine_wanted // cache_dev) ^ me) & 1
    wanted = jnp.where((here == 0)[:, None, None, None], rows_for(mine_wanted), from_pair)
    return wanted


def sum_heads(partial_value):
    me = lax.axis_index("exp")
    rows, width = partial_value.shape
    grid = partial_value.reshape(2, 2, rows // 4, width)
    core, chip = me % 2, me // 2
    got = flip_core(pick(grid, 1 - core, 1).astype(jnp.bfloat16))
    level = pick(grid, core, 1) + got.astype(jnp.float32)
    got = flip_chip(pick(level, 1 - chip, 0).astype(jnp.bfloat16))
    return pick(level, chip, 0) + got.astype(jnp.float32)


def spread_tokens(pieces):
    width = pieces[0].shape[1]
    stacked = jnp.stack(pieces)
    cut = stacked.shape[1] // 2
    first, second = stacked[:, :cut], stacked[:, cut:]
    first = jnp.stack([first, flip_pair(first)])
    second = jnp.stack([second, flip_chip(second)])
    first_far, second_far = flip_chip(first), flip_pair(second)
    parts = [first, first_far, second, second_far]
    return jnp.concatenate([part.reshape(-1, width) for part in parts])


def gather_sums(total, piece_count):
    rows, width = total.shape
    cut = rows // (8 * piece_count)
    first, second = total.reshape(2, 2, 2, piece_count, cut, width)
    first = add(first[0], flip_chip(first[1]))
    second = add(second[0], flip_pair(second[1]))
    first = add(first[0], flip_pair(first[1]))
    second = add(second[0], flip_chip(second[1]))
    return jnp.concatenate([first, second], axis=1)


def mix(normed, codes, slot_weights, held, pick_first):
    pair_count = lax.axis_size("req") // 2
    first_slot = (lax.axis_index("req") * slot_weights.shape[0]).astype(jnp.int32).reshape(1)
    ext = jnp.concatenate([normed, codes], axis=1)
    pieces = [ext]
    for step in range(1, pair_count):
        source = ext
        if step == 2:
            source, *held[3:] = together(ext, *held[3:])
        pieces.append(turn_pairs(source, step))
    outgoing = pick_first(held)
    outgoing = after(outgoing, *pieces[1:])
    *pieces, outgoing = together(*pieces, outgoing)
    arrived = trade_columns(outgoing)
    total = None
    for begin in range(0, pair_count, 2):
        here = spread_tokens(pieces[begin : begin + 2])
        there = flip_core(here)
        back = flip_core(run_experts(first_slot, there, slot_weights, 256))
        if begin + 2 >= pair_count:
            here, arrived = together(here, arrived)
        mixed = run_experts(first_slot, here, slot_weights, 256)
        sums = gather_sums(add(mixed, back), 2)
        for offset in range(2):
            step = begin + offset
            part = sums[offset] if step == 0 else turn_pairs(sums[offset], -step)
            part = part.astype(jnp.float32)
            total = part if total is None else total + part
    return total, arrived, mixed


def spread_weights(slot_weights):
    me = lax.axis_index("req")
    half = lax.axis_size("req") // 2
    spot = me % half
    slots_here = slot_weights.shape[0]
    chunks = slot_weights.reshape(slots_here, half, -1, slot_weights.shape[-1])
    held = [pick(chunks, spot, 1)]
    for mask in range(1, half):
        held.append(swap(pick(chunks, spot ^ mask, 1), mask))
    return held


def pick_kernel(slots_here, index_ref, *refs):
    sources, out_ref = refs[:-1], refs[-1]
    holder = index_ref[pl.program_id(0)] // slots_here
    for k, source in enumerate(sources):

        @pl.when(holder == k)
        def _():
            out_ref[...] = source[...]


def take_chunks(held, index, begin, size):
    slots_here, _, width = held[0].shape
    count = index.shape[0]
    place = begin // size

    def block_of(k):
        def index_map(i, index):
            mine = index[i] // slots_here == k
            return (jnp.where(mine, index[i] % slots_here, 0), place, 0)

        return pl.BlockSpec((1, size, width), index_map)

    return pl.pallas_call(
        functools.partial(pick_kernel, slots_here),
        out_shape=jax.ShapeDtypeStruct((count, size, width), held[0].dtype),
        grid_spec=pltpu.PrefetchScalarGridSpec(
            num_scalar_prefetch=1,
            grid=(count,),
            in_specs=[block_of(k) for k in range(len(held))],
            out_specs=pl.BlockSpec((1, size, width), lambda i, index: (i, 0, 0)),
        ),
        compiler_params=pltpu.CompilerParams(vmem_limit_bytes=24 * 1024 * 1024),
        cost_estimate=pl.CostEstimate(
            flops=0, bytes_accessed=4 * count * size * width, transcendentals=0
        ),
    )(index, *held)


def trade_columns(outgoing):
    pair_count = lax.axis_size("req") // 2
    columns = [[2 * i + k for i in range(pair_count)] for k in range(2)]
    outgoing = outgoing.reshape((pair_count, 2) + outgoing.shape[1:])
    return lax.all_to_all(outgoing, "req", 0, 0, axis_index_groups=columns, tiled=True)


def chunk_index(source_slot, slots_here):
    half = lax.axis_size("req") // 2
    spots = source_slot // slots_here % half
    return ((lax.axis_index("req") % half) ^ spots) * slots_here + source_slot % slots_here


def collect_replicas(arrivals, source_slot, slots_here):
    me = lax.axis_index("req")
    half = lax.axis_size("req") // 2
    side = me % 2
    halves = source_slot // slots_here // half
    width = arrivals[0].shape[3]
    rows_all = sum(arrived.shape[2] for arrived in arrivals)
    result = jnp.zeros((half // 2, 2, rows_all, width), arrivals[0].dtype)
    first_row = 0
    for arrived in arrivals:
        size = arrived.shape[2]

        def wanted_by(receiver):
            begin = pick(halves, receiver, 0) * (half // 2)
            where = (begin, receiver % 2, 0, 0)
            return lax.dynamic_slice(arrived, where, (half // 2, 1, size, width))

        swapped = swap(wanted_by(me ^ 1), 1)
        for rows, column in ((wanted_by(me), side), (swapped, 1 - side)):
            result = lax.dynamic_update_slice(result, rows, (0, column, first_row, 0))
        first_row += size
    return result


def body(
    hidden_in,
    query_in,
    key_in,
    value_in,
    query_gain,
    key_gain,
    cache_keys,
    cache_values,
    cache_block,
    request_lengths,
    out_proj,
    norm_gain,
    expert_ids,
    gate_values,
    old_slots,
    new_replicas,
    slot_weights,
):
    req_count = lax.axis_size("req")
    exp_count = lax.axis_size("exp")
    group_idx = lax.axis_index("req")
    tok_grp, width_q = query_in.shape
    tok_dev, model_width = hidden_in.shape
    head_size = query_gain.shape[0]
    head_count = width_q // head_size
    cache_dev = cache_keys.shape[0]
    pre_len = cache_keys.shape[1]
    req_grp = request_lengths.shape[1]
    lengths = request_lengths[0]
    req_ends = jnp.cumsum(lengths)
    starts = req_ends - lengths
    places = jnp.arange(tok_grp, dtype=jnp.int32)
    member = (places[:, None] >= starts[None, :]) & (places[:, None] < req_ends[None, :])
    request_idx = jnp.arange(req_grp, dtype=jnp.int32)
    segment = jnp.sum(jnp.where(member, request_idx[None, :], 0), axis=1)
    offset = places - jnp.sum(jnp.where(member, starts[None, :], 0), axis=1)
    block_rows = cache_block.reshape(req_count, req_grp)
    my_blocks = lax.dynamic_index_in_dim(block_rows, group_idx, 0, keepdims=False)
    has_cache = my_blocks >= 0
    token_cached = jnp.sum(jnp.where(member & has_cache[None, :], 1, 0), axis=1) > 0
    position = (offset + jnp.where(token_cached, pre_len, 0)).astype(jnp.float32)
    need_blocks, need_requests = compact(block_rows, cache_dev)
    my_requests = lax.dynamic_index_in_dim(need_requests, group_idx, 0, keepdims=False)
    far_cache = fetch_cache(cache_keys, cache_values, need_blocks)
    far_keys, far_values = far_cache[:, 0], far_cache[:, 1]
    held = spread_weights(slot_weights)
    query_n = prepare(query_in.reshape(tok_grp, head_count, head_size), query_gain, position)
    key_n = prepare(key_in.reshape(tok_grp, head_count, head_size), key_gain, position)
    keyset = jnp.concatenate(
        [key_n, far_keys.reshape(cache_dev * pre_len, head_count, head_size)], axis=0
    )
    valueset = jnp.concatenate(
        [
            value_in.reshape(tok_grp, head_count, head_size),
            far_values.reshape(cache_dev * pre_len, head_count, head_size),
        ],
        axis=0,
    )
    key_request = jnp.concatenate([segment, jnp.repeat(my_requests, pre_len)])
    allowed = segment[:, None] == key_request[None, :]
    scores = jnp.einsum("qhd,khd->hqk", query_n, keyset, preferred_element_type=jnp.float32) * (
        1.0 / math.sqrt(head_size)
    )
    scores = jnp.where(allowed[None], scores, -1e30)
    peak = jnp.max(scores, axis=-1, keepdims=True)
    expos = jnp.exp(scores - peak)
    weights = (expos / jnp.sum(expos, axis=-1, keepdims=True)).astype(jnp.bfloat16)
    attended = jnp.einsum("hqk,khd->qhd", weights, valueset, preferred_element_type=jnp.float32)
    attended = attended.astype(jnp.bfloat16).reshape(tok_grp, width_q)
    attended, *held[1:3] = together(attended, *held[1:3])
    attn_out = sum_heads(jnp.dot(attended, out_proj, preferred_element_type=jnp.float32))
    residual = hidden_in.astype(jnp.float32) + attn_out
    normed = (
        residual
        * lax.rsqrt(jnp.mean(residual * residual, axis=-1, keepdims=True) + 1e-06)
        * norm_gain
    ).astype(jnp.bfloat16)
    slot_total = old_slots.shape[0]
    slot_range = jnp.arange(slot_total, dtype=jnp.int32)
    slot_of = jnp.sum(
        jnp.where(old_slots[None, :] == slot_range[:, None], slot_range[None, :], 0), axis=1
    )
    dense_gates = jnp.sum(
        jnp.where(expert_ids[:, :, None] == old_slots[None, None, :], gate_values[:, :, None], 0.0),
        axis=1,
    )
    high_part = dense_gates.astype(jnp.bfloat16)
    low_part = (dense_gates - high_part.astype(jnp.float32)).astype(jnp.bfloat16)
    lanes = max(64, slot_total)
    gap = ((0, 0), (0, lanes - slot_total))
    codes = jnp.concatenate([jnp.pad(high_part, gap), jnp.pad(low_part, gap)], axis=1)
    replica_onehot = new_replicas[:, None] == slot_range[None, :]
    source_slot = jnp.sum(jnp.where(replica_onehot, slot_of[None, :], 0), axis=1)
    slots_here = slot_weights.shape[0]
    index = chunk_index(source_slot, slots_here)
    last = held[0].shape[1] // 3
    size = held[0].shape[1] - last
    mixture, first, mixed = mix(
        normed, codes, slot_weights, held, lambda held: take_chunks(held, index, 0, size)
    )
    layer_out = (residual + mixture).astype(jnp.bfloat16)
    second = trade_columns(after(take_chunks(held, index, size, last), first))
    first = after(first, mixed)
    replica_weights = collect_replicas((first, second), source_slot, slots_here)
    return (layer_out, replica_weights.reshape((1,) + slot_weights.shape[1:]))


def solution(mesh):
    in_specs = (
        P(("req", "exp"), None),
        P("req", "exp"),
        P("req", "exp"),
        P("req", "exp"),
        P(),
        P(),
        P("req", None, "exp"),
        P("req", None, "exp"),
        P(),
        P("req", None),
        P("exp", None),
        P(),
        P(("req", "exp"), None),
        P(("req", "exp"), None),
        P(),
        P(),
        P("req", None, None, "exp"),
    )
    out_specs = (P(("req", "exp"), None), P("req", None, None, "exp"))
    return jax.shard_map(body, mesh=mesh, in_specs=in_specs, out_specs=out_specs, check_vma=False)
```

```python
import functools
import math

import jax
import jax.numpy as jnp
from jax import lax
from jax.experimental import pallas as pl
from jax.experimental.pallas import tpu as pltpu
from jax.sharding import PartitionSpec as P


def prepare(values, gain, position):
    vector = values.astype(jnp.float32)
    scaled = vector * lax.rsqrt(jnp.mean(vector * vector, axis=-1, keepdims=True) + 1e-06) * gain
    half_size = scaled.shape[-1] // 2
    frequency = 10000.0 ** (-(jnp.arange(half_size, dtype=jnp.float32) * 2.0 / scaled.shape[-1]))
    angles = position[:, None] * frequency[None, :]
    cosine = jnp.cos(angles)[:, None, :]
    sine_part = jnp.sin(angles)[:, None, :]
    lower_half = scaled[..., :half_size]
    upper_half = scaled[..., half_size:]
    rotated = jnp.concatenate(
        [
            lower_half * cosine - upper_half * sine_part,
            upper_half * cosine + lower_half * sine_part,
        ],
        axis=-1,
    )
    return rotated.astype(jnp.bfloat16)


def compact(block_rows, slots_wanted):
    live = block_rows >= 0
    ranks = jnp.cumsum(live.astype(jnp.int32), axis=1) - 1
    request_idx = jnp.arange(block_rows.shape[1], dtype=jnp.int32)[None, :]
    chosen_blocks = []
    chosen_requests = []
    for slot_num in range(slots_wanted):
        picked = live & (ranks == slot_num)
        chosen_blocks.append(jnp.sum(jnp.where(picked, block_rows, 0), axis=1))
        chosen_requests.append(jnp.sum(jnp.where(picked, request_idx, 0), axis=1))
    return (jnp.stack(chosen_blocks, axis=1), jnp.stack(chosen_requests, axis=1))


def experts_kernel(first_slot_ref, tok_ref, weights_ref, out_ref):
    slot_count, _, model_width, _ = weights_ref.shape
    rows = tok_ref[:, :model_width]
    codes = tok_ref[:, model_width:].astype(jnp.float32)
    half_codes = codes.shape[1] // 2
    lane = lax.broadcasted_iota(jnp.int32, codes.shape, 1)
    total = None
    for slot_num in range(slot_count):
        wanted = first_slot_ref[0] + slot_num
        picked = (lane == wanted) | (lane == wanted + half_codes)
        factor = jnp.sum(jnp.where(picked, codes, 0.0), axis=1, keepdims=True)
        gate_act = jnp.dot(rows, weights_ref[slot_num, 0], preferred_element_type=jnp.float32)
        up_act = jnp.dot(rows, weights_ref[slot_num, 1], preferred_element_type=jnp.float32)
        hidden = gate_act / (1.0 + jnp.exp(-gate_act)) * up_act
        hidden = (hidden * factor).astype(jnp.bfloat16)
        part = lax.dot_general(
            hidden,
            weights_ref[slot_num, 2],
            (((1,), (1,)), ((), ())),
            preferred_element_type=jnp.float32,
        )
        total = part if total is None else total + part
    out_ref[...] = total.astype(out_ref.dtype)


def run_experts(first_slot, tokens, slot_weights, block):
    count, ext_width = tokens.shape
    slots_here, mats, width, hidden_size = slot_weights.shape
    return pl.pallas_call(
        experts_kernel,
        out_shape=jax.ShapeDtypeStruct((count, width), jnp.bfloat16),
        grid=(count // block,),
        in_specs=[
            pl.BlockSpec(memory_space=pltpu.SMEM),
            pl.BlockSpec((block, ext_width), lambda i: (i, 0)),
            pl.BlockSpec((slots_here, mats, width, hidden_size), lambda i: (0, 0, 0, 0)),
        ],
        out_specs=pl.BlockSpec((block, width), lambda i: (i, 0)),
        compiler_params=pltpu.CompilerParams(vmem_limit_bytes=40 * 1024 * 1024),
        cost_estimate=pl.CostEstimate(
            flops=2 * count * width * hidden_size * mats * slots_here,
            bytes_accessed=4 * count * width + 2 * slot_weights.size,
            transcendentals=count * hidden_size * slots_here,
        ),
    )(first_slot, tokens, slot_weights)


def turn_pairs(value, step):
    count = lax.axis_size("req")
    return lax.ppermute(value, "req", [(i, (i + 2 * step) % count) for i in range(count)])


def swap(value, mask):
    count = lax.axis_size("req")
    return lax.ppermute(value, "req", [(i, i ^ mask) for i in range(count)])


def together(*values):
    return lax.optimization_barrier(values)


def after(value, *events):
    return lax.optimization_barrier((value,) + events)[0]


def flip_pair(value):
    count = lax.axis_size("req")
    return lax.ppermute(value, "req", [(i, i ^ 1) for i in range(count)])


def flip_chip(value):
    count = lax.axis_size("exp")
    return lax.ppermute(value, "exp", [(i, i ^ 2) for i in range(count)])


def flip_core(value):
    count = lax.axis_size("exp")
    return lax.ppermute(value, "exp", [(i, i ^ 1) for i in range(count)])


def pick(value, index, axis):
    return lax.dynamic_index_in_dim(value, index, axis, keepdims=False)


def add(first, second):
    return (first.astype(jnp.float32) + second.astype(jnp.float32)).astype(jnp.bfloat16)


def fetch_cache(cache_keys, cache_values, need_blocks):
    me = lax.axis_index("req")
    pair_count = lax.axis_size("req") // 2
    cache_dev = cache_keys.shape[0]
    mine = jnp.stack([cache_keys, cache_values], axis=1)
    column = jnp.stack([mine] + [turn_pairs(mine, step) for step in range(1, pair_count)])
    column = column.reshape((pair_count * cache_dev,) + mine.shape[1:])

    def rows_for(wanted):
        holder = wanted // cache_dev
        back = (me // 2 - holder // 2) % pair_count
        index = back * cache_dev + wanted % cache_dev
        return jnp.stack([pick(column, index[k], 0) for k in range(cache_dev)])

    mine_wanted = pick(need_blocks, me, 0)
    from_pair = flip_pair(rows_for(pick(need_blocks, me ^ 1, 0)))
    here = ((mine_wanted // cache_dev) ^ me) & 1
    wanted = jnp.where((here == 0)[:, None, None, None], rows_for(mine_wanted), from_pair)
    return wanted


def sum_heads(partial_value):
    me = lax.axis_index("exp")
    rows, width = partial_value.shape
    grid = partial_value.reshape(2, 2, rows // 4, width)
    core, chip = me % 2, me // 2
    got = flip_core(pick(grid, 1 - core, 1).astype(jnp.bfloat16))
    level = pick(grid, core, 1) + got.astype(jnp.float32)
    got = flip_chip(pick(level, 1 - chip, 0).astype(jnp.bfloat16))
    return pick(level, chip, 0) + got.astype(jnp.float32)


def spread_tokens(pieces):
    width = pieces[0].shape[1]
    stacked = jnp.stack(pieces)
    cut = stacked.shape[1] // 2
    first, second = stacked[:, :cut], stacked[:, cut:]
    first = jnp.stack([first, flip_pair(first)])
    second = jnp.stack([second, flip_chip(second)])
    first_far, second_far = flip_chip(first), flip_pair(second)
    parts = [first, first_far, second, second_far]
    return jnp.concatenate([part.reshape(-1, width) for part in parts])


def gather_sums(total, piece_count):
    rows, width = total.shape
    cut = rows // (8 * piece_count)
    first, second = total.reshape(2, 2, 2, piece_count, cut, width)
    first = add(first[0], flip_chip(first[1]))
    second = add(second[0], flip_pair(second[1]))
    first = add(first[0], flip_pair(first[1]))
    second = add(second[0], flip_chip(second[1]))
    return jnp.concatenate([first, second], axis=1)


def mix(normed, codes, slot_weights, held, pick_first):
    pair_count = lax.axis_size("req") // 2
    first_slot = (lax.axis_index("req") * slot_weights.shape[0]).astype(jnp.int32).reshape(1)
    ext = jnp.concatenate([normed, codes], axis=1)
    pieces = [ext]
    for step in range(1, pair_count):
        source = ext
        if step == 2:
            source, *held[3:] = together(ext, *held[3:])
        pieces.append(turn_pairs(source, step))
    outgoing = pick_first(held)
    outgoing = after(outgoing, *pieces[1:])
    *pieces[2:], outgoing = together(*pieces[2:], outgoing)
    arrived = trade_columns(outgoing)
    total = None
    for begin in range(0, pair_count, 2):
        here = spread_tokens(pieces[begin : begin + 2])
        there = flip_core(here)
        back = flip_core(run_experts(first_slot, there, slot_weights, 256))
        if begin + 2 >= pair_count:
            here, arrived = together(here, arrived)
        mixed = run_experts(first_slot, here, slot_weights, 256)
        sums = gather_sums(add(mixed, back), 2)
        for offset in range(2):
            step = begin + offset
            part = sums[offset] if step == 0 else turn_pairs(sums[offset], -step)
            part = part.astype(jnp.float32)
            total = part if total is None else total + part
    return total, arrived, mixed


def spread_weights(slot_weights):
    me = lax.axis_index("req")
    half = lax.axis_size("req") // 2
    spot = me % half
    slots_here = slot_weights.shape[0]
    chunks = slot_weights.reshape(slots_here, half, -1, slot_weights.shape[-1])
    held = [pick(chunks, spot, 1)]
    for mask in range(1, half):
        held.append(swap(pick(chunks, spot ^ mask, 1), mask))
    return held


def pick_kernel(slots_here, index_ref, *refs):
    sources, out_ref = refs[:-1], refs[-1]
    holder = index_ref[pl.program_id(0)] // slots_here
    for k, source in enumerate(sources):

        @pl.when(holder == k)
        def _():
            out_ref[...] = source[...]


def take_chunks(held, index, begin, size):
    slots_here, _, width = held[0].shape
    count = index.shape[0]
    place = begin // size

    def block_of(k):
        def index_map(i, index):
            mine = index[i] // slots_here == k
            return (jnp.where(mine, index[i] % slots_here, 0), place, 0)

        return pl.BlockSpec((1, size, width), index_map)

    return pl.pallas_call(
        functools.partial(pick_kernel, slots_here),
        out_shape=jax.ShapeDtypeStruct((count, size, width), held[0].dtype),
        grid_spec=pltpu.PrefetchScalarGridSpec(
            num_scalar_prefetch=1,
            grid=(count,),
            in_specs=[block_of(k) for k in range(len(held))],
            out_specs=pl.BlockSpec((1, size, width), lambda i, index: (i, 0, 0)),
        ),
        compiler_params=pltpu.CompilerParams(vmem_limit_bytes=24 * 1024 * 1024),
        cost_estimate=pl.CostEstimate(
            flops=0, bytes_accessed=4 * count * size * width, transcendentals=0
        ),
    )(index, *held)


def trade_columns(outgoing):
    pair_count = lax.axis_size("req") // 2
    columns = [[2 * i + k for i in range(pair_count)] for k in range(2)]
    outgoing = outgoing.reshape((pair_count, 2) + outgoing.shape[1:])
    return lax.all_to_all(outgoing, "req", 0, 0, axis_index_groups=columns, tiled=True)


def chunk_index(source_slot, slots_here):
    half = lax.axis_size("req") // 2
    spots = source_slot // slots_here % half
    return ((lax.axis_index("req") % half) ^ spots) * slots_here + source_slot % slots_here


def collect_replicas(arrivals, source_slot, slots_here):
    me = lax.axis_index("req")
    half = lax.axis_size("req") // 2
    side = me % 2
    halves = source_slot // slots_here // half
    width = arrivals[0].shape[3]
    rows_all = sum(arrived.shape[2] for arrived in arrivals)
    result = jnp.zeros((half // 2, 2, rows_all, width), arrivals[0].dtype)
    first_row = 0
    for arrived in arrivals:
        size = arrived.shape[2]

        def wanted_by(receiver):
            begin = pick(halves, receiver, 0) * (half // 2)
            where = (begin, receiver % 2, 0, 0)
            return lax.dynamic_slice(arrived, where, (half // 2, 1, size, width))

        swapped = swap(wanted_by(me ^ 1), 1)
        for rows, column in ((wanted_by(me), side), (swapped, 1 - side)):
            result = lax.dynamic_update_slice(result, rows, (0, column, first_row, 0))
        first_row += size
    return result


def body(
    hidden_in,
    query_in,
    key_in,
    value_in,
    query_gain,
    key_gain,
    cache_keys,
    cache_values,
    cache_block,
    request_lengths,
    out_proj,
    norm_gain,
    expert_ids,
    gate_values,
    old_slots,
    new_replicas,
    slot_weights,
):
    req_count = lax.axis_size("req")
    exp_count = lax.axis_size("exp")
    group_idx = lax.axis_index("req")
    tok_grp, width_q = query_in.shape
    tok_dev, model_width = hidden_in.shape
    head_size = query_gain.shape[0]
    head_count = width_q // head_size
    cache_dev = cache_keys.shape[0]
    pre_len = cache_keys.shape[1]
    req_grp = request_lengths.shape[1]
    lengths = request_lengths[0]
    req_ends = jnp.cumsum(lengths)
    starts = req_ends - lengths
    places = jnp.arange(tok_grp, dtype=jnp.int32)
    member = (places[:, None] >= starts[None, :]) & (places[:, None] < req_ends[None, :])
    request_idx = jnp.arange(req_grp, dtype=jnp.int32)
    segment = jnp.sum(jnp.where(member, request_idx[None, :], 0), axis=1)
    offset = places - jnp.sum(jnp.where(member, starts[None, :], 0), axis=1)
    block_rows = cache_block.reshape(req_count, req_grp)
    my_blocks = lax.dynamic_index_in_dim(block_rows, group_idx, 0, keepdims=False)
    has_cache = my_blocks >= 0
    token_cached = jnp.sum(jnp.where(member & has_cache[None, :], 1, 0), axis=1) > 0
    position = (offset + jnp.where(token_cached, pre_len, 0)).astype(jnp.float32)
    need_blocks, need_requests = compact(block_rows, cache_dev)
    my_requests = lax.dynamic_index_in_dim(need_requests, group_idx, 0, keepdims=False)
    far_cache = fetch_cache(cache_keys, cache_values, need_blocks)
    far_keys, far_values = far_cache[:, 0], far_cache[:, 1]
    held = spread_weights(slot_weights)
    query_n = prepare(query_in.reshape(tok_grp, head_count, head_size), query_gain, position)
    key_n = prepare(key_in.reshape(tok_grp, head_count, head_size), key_gain, position)
    keyset = jnp.concatenate(
        [key_n, far_keys.reshape(cache_dev * pre_len, head_count, head_size)], axis=0
    )
    valueset = jnp.concatenate(
        [
            value_in.reshape(tok_grp, head_count, head_size),
            far_values.reshape(cache_dev * pre_len, head_count, head_size),
        ],
        axis=0,
    )
    key_request = jnp.concatenate([segment, jnp.repeat(my_requests, pre_len)])
    allowed = segment[:, None] == key_request[None, :]
    scores = jnp.einsum("qhd,khd->hqk", query_n, keyset, preferred_element_type=jnp.float32) * (
        1.0 / math.sqrt(head_size)
    )
    scores = jnp.where(allowed[None], scores, -1e30)
    peak = jnp.max(scores, axis=-1, keepdims=True)
    expos = jnp.exp(scores - peak)
    weights = (expos / jnp.sum(expos, axis=-1, keepdims=True)).astype(jnp.bfloat16)
    attended = jnp.einsum("hqk,khd->qhd", weights, valueset, preferred_element_type=jnp.float32)
    attended = attended.astype(jnp.bfloat16).reshape(tok_grp, width_q)
    attended, *held[1:3] = together(attended, *held[1:3])
    attn_out = sum_heads(jnp.dot(attended, out_proj, preferred_element_type=jnp.float32))
    residual = hidden_in.astype(jnp.float32) + attn_out
    normed = (
        residual
        * lax.rsqrt(jnp.mean(residual * residual, axis=-1, keepdims=True) + 1e-06)
        * norm_gain
    ).astype(jnp.bfloat16)
    slot_total = old_slots.shape[0]
    slot_range = jnp.arange(slot_total, dtype=jnp.int32)
    slot_of = jnp.sum(
        jnp.where(old_slots[None, :] == slot_range[:, None], slot_range[None, :], 0), axis=1
    )
    dense_gates = jnp.sum(
        jnp.where(expert_ids[:, :, None] == old_slots[None, None, :], gate_values[:, :, None], 0.0),
        axis=1,
    )
    high_part = dense_gates.astype(jnp.bfloat16)
    low_part = (dense_gates - high_part.astype(jnp.float32)).astype(jnp.bfloat16)
    lanes = max(64, slot_total)
    gap = ((0, 0), (0, lanes - slot_total))
    codes = jnp.concatenate([jnp.pad(high_part, gap), jnp.pad(low_part, gap)], axis=1)
    replica_onehot = new_replicas[:, None] == slot_range[None, :]
    source_slot = jnp.sum(jnp.where(replica_onehot, slot_of[None, :], 0), axis=1)
    slots_here = slot_weights.shape[0]
    index = chunk_index(source_slot, slots_here)
    size = held[0].shape[1] // 2
    mixture, first, mixed = mix(
        normed, codes, slot_weights, held, lambda held: take_chunks(held, index, 0, size)
    )
    layer_out = (residual + mixture).astype(jnp.bfloat16)
    second = trade_columns(after(take_chunks(held, index, size, size), first))
    first = after(first, mixed)
    replica_weights = collect_replicas((first, second), source_slot, slots_here)
    return (layer_out, replica_weights.reshape((1,) + slot_weights.shape[1:]))


def solution(mesh):
    in_specs = (
        P(("req", "exp"), None),
        P("req", "exp"),
        P("req", "exp"),
        P("req", "exp"),
        P(),
        P(),
        P("req", None, "exp"),
        P("req", None, "exp"),
        P(),
        P("req", None),
        P("exp", None),
        P(),
        P(("req", "exp"), None),
        P(("req", "exp"), None),
        P(),
        P(),
        P("req", None, None, "exp"),
    )
    out_specs = (P(("req", "exp"), None), P("req", None, None, "exp"))
    return jax.shard_map(body, mesh=mesh, in_specs=in_specs, out_specs=out_specs, check_vma=False)
```

```python
import functools
import math

import jax
import jax.numpy as jnp
from jax import lax
from jax.experimental import pallas as pl
from jax.experimental.pallas import tpu as pltpu
from jax.sharding import PartitionSpec as P


def prepare(values, gain, position):
    vector = values.astype(jnp.float32)
    scaled = vector * lax.rsqrt(jnp.mean(vector * vector, axis=-1, keepdims=True) + 1e-06) * gain
    half_size = scaled.shape[-1] // 2
    frequency = 10000.0 ** (-(jnp.arange(half_size, dtype=jnp.float32) * 2.0 / scaled.shape[-1]))
    angles = position[:, None] * frequency[None, :]
    cosine = jnp.cos(angles)[:, None, :]
    sine_part = jnp.sin(angles)[:, None, :]
    lower_half = scaled[..., :half_size]
    upper_half = scaled[..., half_size:]
    rotated = jnp.concatenate(
        [
            lower_half * cosine - upper_half * sine_part,
            upper_half * cosine + lower_half * sine_part,
        ],
        axis=-1,
    )
    return rotated.astype(jnp.bfloat16)


def compact(block_rows, slots_wanted):
    live = block_rows >= 0
    ranks = jnp.cumsum(live.astype(jnp.int32), axis=1) - 1
    request_idx = jnp.arange(block_rows.shape[1], dtype=jnp.int32)[None, :]
    chosen_blocks = []
    chosen_requests = []
    for slot_num in range(slots_wanted):
        picked = live & (ranks == slot_num)
        chosen_blocks.append(jnp.sum(jnp.where(picked, block_rows, 0), axis=1))
        chosen_requests.append(jnp.sum(jnp.where(picked, request_idx, 0), axis=1))
    return (jnp.stack(chosen_blocks, axis=1), jnp.stack(chosen_requests, axis=1))


def experts_kernel(first_slot_ref, tok_ref, weights_ref, out_ref):
    slot_count, _, model_width, _ = weights_ref.shape
    rows = tok_ref[:, :model_width]
    codes = tok_ref[:, model_width:].astype(jnp.float32)
    half_codes = codes.shape[1] // 2
    lane = lax.broadcasted_iota(jnp.int32, codes.shape, 1)
    total = None
    for slot_num in range(slot_count):
        wanted = first_slot_ref[0] + slot_num
        picked = (lane == wanted) | (lane == wanted + half_codes)
        factor = jnp.sum(jnp.where(picked, codes, 0.0), axis=1, keepdims=True)
        gate_act = jnp.dot(rows, weights_ref[slot_num, 0], preferred_element_type=jnp.float32)
        up_act = jnp.dot(rows, weights_ref[slot_num, 1], preferred_element_type=jnp.float32)
        hidden = gate_act / (1.0 + jnp.exp(-gate_act)) * up_act
        hidden = (hidden * factor).astype(jnp.bfloat16)
        part = lax.dot_general(
            hidden,
            weights_ref[slot_num, 2],
            (((1,), (1,)), ((), ())),
            preferred_element_type=jnp.float32,
        )
        total = part if total is None else total + part
    out_ref[...] = total.astype(out_ref.dtype)


def run_experts(first_slot, tokens, slot_weights, block):
    count, ext_width = tokens.shape
    slots_here, mats, width, hidden_size = slot_weights.shape
    return pl.pallas_call(
        experts_kernel,
        out_shape=jax.ShapeDtypeStruct((count, width), jnp.bfloat16),
        grid=(count // block,),
        in_specs=[
            pl.BlockSpec(memory_space=pltpu.SMEM),
            pl.BlockSpec((block, ext_width), lambda i: (i, 0)),
            pl.BlockSpec((slots_here, mats, width, hidden_size), lambda i: (0, 0, 0, 0)),
        ],
        out_specs=pl.BlockSpec((block, width), lambda i: (i, 0)),
        compiler_params=pltpu.CompilerParams(vmem_limit_bytes=40 * 1024 * 1024),
        cost_estimate=pl.CostEstimate(
            flops=2 * count * width * hidden_size * mats * slots_here,
            bytes_accessed=4 * count * width + 2 * slot_weights.size,
            transcendentals=count * hidden_size * slots_here,
        ),
    )(first_slot, tokens, slot_weights)


def turn_pairs(value, step):
    count = lax.axis_size("req")
    return lax.ppermute(value, "req", [(i, (i + 2 * step) % count) for i in range(count)])


def swap(value, mask):
    count = lax.axis_size("req")
    return lax.ppermute(value, "req", [(i, i ^ mask) for i in range(count)])


def together(*values):
    return lax.optimization_barrier(values)


def after(value, *events):
    return lax.optimization_barrier((value,) + events)[0]


def flip_pair(value):
    count = lax.axis_size("req")
    return lax.ppermute(value, "req", [(i, i ^ 1) for i in range(count)])


def flip_chip(value):
    count = lax.axis_size("exp")
    return lax.ppermute(value, "exp", [(i, i ^ 2) for i in range(count)])


def flip_core(value):
    count = lax.axis_size("exp")
    return lax.ppermute(value, "exp", [(i, i ^ 1) for i in range(count)])


def pick(value, index, axis):
    return lax.dynamic_index_in_dim(value, index, axis, keepdims=False)


def add(first, second):
    return (first.astype(jnp.float32) + second.astype(jnp.float32)).astype(jnp.bfloat16)


def fetch_cache(cache_keys, cache_values, need_blocks):
    me = lax.axis_index("req")
    pair_count = lax.axis_size("req") // 2
    cache_dev = cache_keys.shape[0]
    mine = jnp.stack([cache_keys, cache_values], axis=1)
    column = jnp.stack([mine] + [turn_pairs(mine, step) for step in range(1, pair_count)])
    column = column.reshape((pair_count * cache_dev,) + mine.shape[1:])

    def rows_for(wanted):
        holder = wanted // cache_dev
        back = (me // 2 - holder // 2) % pair_count
        index = back * cache_dev + wanted % cache_dev
        return jnp.stack([pick(column, index[k], 0) for k in range(cache_dev)])

    mine_wanted = pick(need_blocks, me, 0)
    from_pair = flip_pair(rows_for(pick(need_blocks, me ^ 1, 0)))
    here = ((mine_wanted // cache_dev) ^ me) & 1
    wanted = jnp.where((here == 0)[:, None, None, None], rows_for(mine_wanted), from_pair)
    return wanted


def sum_heads(partial_value):
    me = lax.axis_index("exp")
    rows, width = partial_value.shape
    grid = partial_value.reshape(2, 2, rows // 4, width)
    core, chip = me % 2, me // 2
    got = flip_core(pick(grid, 1 - core, 1).astype(jnp.bfloat16))
    level = pick(grid, core, 1) + got.astype(jnp.float32)
    got = flip_chip(pick(level, 1 - chip, 0).astype(jnp.bfloat16))
    return pick(level, chip, 0) + got.astype(jnp.float32)


def spread_tokens(pieces):
    width = pieces[0].shape[1]
    stacked = jnp.stack(pieces)
    cut = stacked.shape[1] // 2
    first, second = stacked[:, :cut], stacked[:, cut:]
    first = jnp.stack([first, flip_pair(first)])
    second = jnp.stack([second, flip_chip(second)])
    first_far, second_far = flip_chip(first), flip_pair(second)
    parts = [first, first_far, second, second_far]
    return jnp.concatenate([part.reshape(-1, width) for part in parts])


def gather_sums(total, piece_count):
    rows, width = total.shape
    cut = rows // (8 * piece_count)
    first, second = total.reshape(2, 2, 2, piece_count, cut, width)
    first = add(first[0], flip_chip(first[1]))
    second = add(second[0], flip_pair(second[1]))
    first = add(first[0], flip_pair(first[1]))
    second = add(second[0], flip_chip(second[1]))
    return jnp.concatenate([first, second], axis=1)


def mix(normed, codes, slot_weights, held, pick_first):
    pair_count = lax.axis_size("req") // 2
    first_slot = (lax.axis_index("req") * slot_weights.shape[0]).astype(jnp.int32).reshape(1)
    ext = jnp.concatenate([normed, codes], axis=1)
    pieces = [ext]
    for step in range(1, pair_count):
        source = ext
        if step == 2:
            source, *held[3:] = together(ext, *held[3:])
        pieces.append(turn_pairs(source, step))
    outgoing = pick_first(held)
    outgoing = after(outgoing, *pieces[1:])
    *pieces[2:], outgoing = together(*pieces[2:], outgoing)
    arrived = trade_columns(outgoing)
    total, ready = None, []
    for begin in range(0, pair_count, 2):
        here = spread_tokens(pieces[begin : begin + 2])
        there = flip_core(here)
        back = flip_core(run_experts(first_slot, there, slot_weights, 256))
        if begin + 2 >= pair_count:
            here, arrived = together(here, arrived)
        mixed = run_experts(first_slot, here, slot_weights, 256)
        sums = gather_sums(add(mixed, back), 2)
        ready.append(sums)
        for offset in range(2):
            step = begin + offset
            part = sums[offset] if step == 0 else turn_pairs(sums[offset], -step)
            part = part.astype(jnp.float32)
            total = part if total is None else total + part
    return total, arrived, ready


def spread_weights(slot_weights):
    me = lax.axis_index("req")
    half = lax.axis_size("req") // 2
    spot = me % half
    slots_here = slot_weights.shape[0]
    chunks = slot_weights.reshape(slots_here, half, -1, slot_weights.shape[-1])
    held = [pick(chunks, spot, 1)]
    for mask in range(1, half):
        held.append(swap(pick(chunks, spot ^ mask, 1), mask))
    return held


def pick_kernel(slots_here, index_ref, *refs):
    sources, out_ref = refs[:-1], refs[-1]
    holder = index_ref[pl.program_id(0)] // slots_here
    for k, source in enumerate(sources):

        @pl.when(holder == k)
        def _():
            out_ref[...] = source[...]


def take_chunks(held, index, begin, size):
    slots_here, _, width = held[0].shape
    count = index.shape[0]
    place = begin // size

    def block_of(k):
        def index_map(i, index):
            mine = index[i] // slots_here == k
            return (jnp.where(mine, index[i] % slots_here, 0), place, 0)

        return pl.BlockSpec((1, size, width), index_map)

    return pl.pallas_call(
        functools.partial(pick_kernel, slots_here),
        out_shape=jax.ShapeDtypeStruct((count, size, width), held[0].dtype),
        grid_spec=pltpu.PrefetchScalarGridSpec(
            num_scalar_prefetch=1,
            grid=(count,),
            in_specs=[block_of(k) for k in range(len(held))],
            out_specs=pl.BlockSpec((1, size, width), lambda i, index: (i, 0, 0)),
        ),
        compiler_params=pltpu.CompilerParams(vmem_limit_bytes=24 * 1024 * 1024),
        cost_estimate=pl.CostEstimate(
            flops=0, bytes_accessed=4 * count * size * width, transcendentals=0
        ),
    )(index, *held)


def trade_columns(outgoing):
    pair_count = lax.axis_size("req") // 2
    columns = [[2 * i + k for i in range(pair_count)] for k in range(2)]
    outgoing = outgoing.reshape((pair_count, 2) + outgoing.shape[1:])
    return lax.all_to_all(outgoing, "req", 0, 0, axis_index_groups=columns, tiled=True)


def chunk_index(source_slot, slots_here):
    half = lax.axis_size("req") // 2
    spots = source_slot // slots_here % half
    return ((lax.axis_index("req") % half) ^ spots) * slots_here + source_slot % slots_here


def collect_replicas(arrivals, source_slot, slots_here):
    me = lax.axis_index("req")
    half = lax.axis_size("req") // 2
    side = me % 2
    halves = source_slot // slots_here // half
    width = arrivals[0].shape[3]
    rows_all = sum(arrived.shape[2] for arrived in arrivals)
    result = jnp.zeros((half // 2, 2, rows_all, width), arrivals[0].dtype)
    first_row = 0
    for arrived in arrivals:
        size = arrived.shape[2]

        def wanted_by(receiver):
            begin = pick(halves, receiver, 0) * (half // 2)
            where = (begin, receiver % 2, 0, 0)
            return lax.dynamic_slice(arrived, where, (half // 2, 1, size, width))

        swapped = swap(wanted_by(me ^ 1), 1)
        for rows, column in ((wanted_by(me), side), (swapped, 1 - side)):
            result = lax.dynamic_update_slice(result, rows, (0, column, first_row, 0))
        first_row += size
    return result


def body(
    hidden_in,
    query_in,
    key_in,
    value_in,
    query_gain,
    key_gain,
    cache_keys,
    cache_values,
    cache_block,
    request_lengths,
    out_proj,
    norm_gain,
    expert_ids,
    gate_values,
    old_slots,
    new_replicas,
    slot_weights,
):
    req_count = lax.axis_size("req")
    exp_count = lax.axis_size("exp")
    group_idx = lax.axis_index("req")
    tok_grp, width_q = query_in.shape
    tok_dev, model_width = hidden_in.shape
    head_size = query_gain.shape[0]
    head_count = width_q // head_size
    cache_dev = cache_keys.shape[0]
    pre_len = cache_keys.shape[1]
    req_grp = request_lengths.shape[1]
    lengths = request_lengths[0]
    req_ends = jnp.cumsum(lengths)
    starts = req_ends - lengths
    places = jnp.arange(tok_grp, dtype=jnp.int32)
    member = (places[:, None] >= starts[None, :]) & (places[:, None] < req_ends[None, :])
    request_idx = jnp.arange(req_grp, dtype=jnp.int32)
    segment = jnp.sum(jnp.where(member, request_idx[None, :], 0), axis=1)
    offset = places - jnp.sum(jnp.where(member, starts[None, :], 0), axis=1)
    block_rows = cache_block.reshape(req_count, req_grp)
    my_blocks = lax.dynamic_index_in_dim(block_rows, group_idx, 0, keepdims=False)
    has_cache = my_blocks >= 0
    token_cached = jnp.sum(jnp.where(member & has_cache[None, :], 1, 0), axis=1) > 0
    position = (offset + jnp.where(token_cached, pre_len, 0)).astype(jnp.float32)
    need_blocks, need_requests = compact(block_rows, cache_dev)
    my_requests = lax.dynamic_index_in_dim(need_requests, group_idx, 0, keepdims=False)
    far_cache = fetch_cache(cache_keys, cache_values, need_blocks)
    far_keys, far_values = far_cache[:, 0], far_cache[:, 1]
    held = spread_weights(slot_weights)
    query_n = prepare(query_in.reshape(tok_grp, head_count, head_size), query_gain, position)
    key_n = prepare(key_in.reshape(tok_grp, head_count, head_size), key_gain, position)
    keyset = jnp.concatenate(
        [key_n, far_keys.reshape(cache_dev * pre_len, head_count, head_size)], axis=0
    )
    valueset = jnp.concatenate(
        [
            value_in.reshape(tok_grp, head_count, head_size),
            far_values.reshape(cache_dev * pre_len, head_count, head_size),
        ],
        axis=0,
    )
    key_request = jnp.concatenate([segment, jnp.repeat(my_requests, pre_len)])
    allowed = segment[:, None] == key_request[None, :]
    scores = jnp.einsum("qhd,khd->hqk", query_n, keyset, preferred_element_type=jnp.float32) * (
        1.0 / math.sqrt(head_size)
    )
    scores = jnp.where(allowed[None], scores, -1e30)
    peak = jnp.max(scores, axis=-1, keepdims=True)
    expos = jnp.exp(scores - peak)
    weights = (expos / jnp.sum(expos, axis=-1, keepdims=True)).astype(jnp.bfloat16)
    attended = jnp.einsum("hqk,khd->qhd", weights, valueset, preferred_element_type=jnp.float32)
    attended = attended.astype(jnp.bfloat16).reshape(tok_grp, width_q)
    attended, *held[1:3] = together(attended, *held[1:3])
    attn_out = sum_heads(jnp.dot(attended, out_proj, preferred_element_type=jnp.float32))
    residual = hidden_in.astype(jnp.float32) + attn_out
    normed = (
        residual
        * lax.rsqrt(jnp.mean(residual * residual, axis=-1, keepdims=True) + 1e-06)
        * norm_gain
    ).astype(jnp.bfloat16)
    slot_total = old_slots.shape[0]
    slot_range = jnp.arange(slot_total, dtype=jnp.int32)
    slot_of = jnp.sum(
        jnp.where(old_slots[None, :] == slot_range[:, None], slot_range[None, :], 0), axis=1
    )
    dense_gates = jnp.sum(
        jnp.where(expert_ids[:, :, None] == old_slots[None, None, :], gate_values[:, :, None], 0.0),
        axis=1,
    )
    high_part = dense_gates.astype(jnp.bfloat16)
    low_part = (dense_gates - high_part.astype(jnp.float32)).astype(jnp.bfloat16)
    lanes = max(64, slot_total)
    gap = ((0, 0), (0, lanes - slot_total))
    codes = jnp.concatenate([jnp.pad(high_part, gap), jnp.pad(low_part, gap)], axis=1)
    replica_onehot = new_replicas[:, None] == slot_range[None, :]
    source_slot = jnp.sum(jnp.where(replica_onehot, slot_of[None, :], 0), axis=1)
    slots_here = slot_weights.shape[0]
    index = chunk_index(source_slot, slots_here)
    size = held[0].shape[1] // 2
    mixture, first, ready = mix(
        normed, codes, slot_weights, held, lambda held: take_chunks(held, index, 0, size)
    )
    layer_out = (residual + mixture).astype(jnp.bfloat16)
    second = trade_columns(after(take_chunks(held, index, size, size), first))
    first = after(first, *ready)
    replica_weights = collect_replicas((first, second), source_slot, slots_here)
    return (layer_out, replica_weights.reshape((1,) + slot_weights.shape[1:]))


def solution(mesh):
    in_specs = (
        P(("req", "exp"), None),
        P("req", "exp"),
        P("req", "exp"),
        P("req", "exp"),
        P(),
        P(),
        P("req", None, "exp"),
        P("req", None, "exp"),
        P(),
        P("req", None),
        P("exp", None),
        P(),
        P(("req", "exp"), None),
        P(("req", "exp"), None),
        P(),
        P(),
        P("req", None, None, "exp"),
    )
    out_specs = (P(("req", "exp"), None), P("req", None, None, "exp"))
    return jax.shard_map(body, mesh=mesh, in_specs=in_specs, out_specs=out_specs, check_vma=False)
```

```python
import functools
import math

import jax
import jax.numpy as jnp
from jax import lax
from jax.experimental import pallas as pl
from jax.experimental.pallas import tpu as pltpu
from jax.sharding import PartitionSpec as P


def prepare(values, gain, position):
    vector = values.astype(jnp.float32)
    scaled = vector * lax.rsqrt(jnp.mean(vector * vector, axis=-1, keepdims=True) + 1e-06) * gain
    half_size = scaled.shape[-1] // 2
    frequency = 10000.0 ** (-(jnp.arange(half_size, dtype=jnp.float32) * 2.0 / scaled.shape[-1]))
    angles = position[:, None] * frequency[None, :]
    cosine = jnp.cos(angles)[:, None, :]
    sine_part = jnp.sin(angles)[:, None, :]
    lower_half = scaled[..., :half_size]
    upper_half = scaled[..., half_size:]
    rotated = jnp.concatenate(
        [
            lower_half * cosine - upper_half * sine_part,
            upper_half * cosine + lower_half * sine_part,
        ],
        axis=-1,
    )
    return rotated.astype(jnp.bfloat16)


def compact(block_rows, slots_wanted):
    live = block_rows >= 0
    ranks = jnp.cumsum(live.astype(jnp.int32), axis=1) - 1
    request_idx = jnp.arange(block_rows.shape[1], dtype=jnp.int32)[None, :]
    chosen_blocks = []
    chosen_requests = []
    for slot_num in range(slots_wanted):
        picked = live & (ranks == slot_num)
        chosen_blocks.append(jnp.sum(jnp.where(picked, block_rows, 0), axis=1))
        chosen_requests.append(jnp.sum(jnp.where(picked, request_idx, 0), axis=1))
    return (jnp.stack(chosen_blocks, axis=1), jnp.stack(chosen_requests, axis=1))


def experts_kernel(first_slot_ref, tok_ref, weights_ref, out_ref):
    slot_count, _, model_width, _ = weights_ref.shape
    rows = tok_ref[:, :model_width]
    codes = tok_ref[:, model_width:].astype(jnp.float32)
    half_codes = codes.shape[1] // 2
    lane = lax.broadcasted_iota(jnp.int32, codes.shape, 1)
    total = None
    for slot_num in range(slot_count):
        wanted = first_slot_ref[0] + slot_num
        picked = (lane == wanted) | (lane == wanted + half_codes)
        factor = jnp.sum(jnp.where(picked, codes, 0.0), axis=1, keepdims=True)
        gate_act = jnp.dot(rows, weights_ref[slot_num, 0], preferred_element_type=jnp.float32)
        up_act = jnp.dot(rows, weights_ref[slot_num, 1], preferred_element_type=jnp.float32)
        hidden = gate_act / (1.0 + jnp.exp(-gate_act)) * up_act
        hidden = (hidden * factor).astype(jnp.bfloat16)
        part = lax.dot_general(
            hidden,
            weights_ref[slot_num, 2],
            (((1,), (1,)), ((), ())),
            preferred_element_type=jnp.float32,
        )
        total = part if total is None else total + part
    out_ref[...] = total.astype(out_ref.dtype)


def run_experts(first_slot, tokens, slot_weights, block):
    count, ext_width = tokens.shape
    slots_here, mats, width, hidden_size = slot_weights.shape
    return pl.pallas_call(
        experts_kernel,
        out_shape=jax.ShapeDtypeStruct((count, width), jnp.bfloat16),
        grid=(count // block,),
        in_specs=[
            pl.BlockSpec(memory_space=pltpu.SMEM),
            pl.BlockSpec((block, ext_width), lambda i: (i, 0)),
            pl.BlockSpec((slots_here, mats, width, hidden_size), lambda i: (0, 0, 0, 0)),
        ],
        out_specs=pl.BlockSpec((block, width), lambda i: (i, 0)),
        compiler_params=pltpu.CompilerParams(vmem_limit_bytes=40 * 1024 * 1024),
        cost_estimate=pl.CostEstimate(
            flops=2 * count * width * hidden_size * mats * slots_here,
            bytes_accessed=4 * count * width + 2 * slot_weights.size,
            transcendentals=count * hidden_size * slots_here,
        ),
    )(first_slot, tokens, slot_weights)


def turn_pairs(value, step):
    count = lax.axis_size("req")
    return lax.ppermute(value, "req", [(i, (i + 2 * step) % count) for i in range(count)])


def swap(value, mask):
    count = lax.axis_size("req")
    return lax.ppermute(value, "req", [(i, i ^ mask) for i in range(count)])


def together(*values):
    return lax.optimization_barrier(values)


def after(value, *events):
    return lax.optimization_barrier((value,) + events)[0]


def flip_pair(value):
    count = lax.axis_size("req")
    return lax.ppermute(value, "req", [(i, i ^ 1) for i in range(count)])


def flip_chip(value):
    count = lax.axis_size("exp")
    return lax.ppermute(value, "exp", [(i, i ^ 2) for i in range(count)])


def flip_core(value):
    count = lax.axis_size("exp")
    return lax.ppermute(value, "exp", [(i, i ^ 1) for i in range(count)])


def pick(value, index, axis):
    return lax.dynamic_index_in_dim(value, index, axis, keepdims=False)


def add(first, second):
    return (first.astype(jnp.float32) + second.astype(jnp.float32)).astype(jnp.bfloat16)


def fetch_cache(cache_keys, cache_values, need_blocks):
    me = lax.axis_index("req")
    pair_count = lax.axis_size("req") // 2
    cache_dev = cache_keys.shape[0]
    mine = jnp.stack([cache_keys, cache_values], axis=1)
    column = jnp.stack([mine] + [turn_pairs(mine, step) for step in range(1, pair_count)])
    column = column.reshape((pair_count * cache_dev,) + mine.shape[1:])

    def rows_for(wanted):
        holder = wanted // cache_dev
        back = (me // 2 - holder // 2) % pair_count
        index = back * cache_dev + wanted % cache_dev
        return jnp.stack([pick(column, index[k], 0) for k in range(cache_dev)])

    mine_wanted = pick(need_blocks, me, 0)
    from_pair = flip_pair(rows_for(pick(need_blocks, me ^ 1, 0)))
    here = ((mine_wanted // cache_dev) ^ me) & 1
    wanted = jnp.where((here == 0)[:, None, None, None], rows_for(mine_wanted), from_pair)
    return wanted


def sum_heads(partial_value):
    me = lax.axis_index("exp")
    rows, width = partial_value.shape
    grid = partial_value.reshape(2, 2, rows // 4, width)
    core, chip = me % 2, me // 2
    got = flip_core(pick(grid, 1 - core, 1).astype(jnp.bfloat16))
    level = pick(grid, core, 1) + got.astype(jnp.float32)
    got = flip_chip(pick(level, 1 - chip, 0).astype(jnp.bfloat16))
    return pick(level, chip, 0) + got.astype(jnp.float32)


def spread_tokens(pieces):
    width = pieces[0].shape[1]
    stacked = jnp.stack(pieces)
    cut = stacked.shape[1] // 2
    first, second = stacked[:, :cut], stacked[:, cut:]
    first = jnp.stack([first, flip_pair(first)])
    second = jnp.stack([second, flip_chip(second)])
    first_far, second_far = flip_chip(first), flip_pair(second)
    parts = [first, first_far, second, second_far]
    return jnp.concatenate([part.reshape(-1, width) for part in parts])


def gather_sums(total, piece_count):
    rows, width = total.shape
    cut = rows // (8 * piece_count)
    first, second = total.reshape(2, 2, 2, piece_count, cut, width)
    first = add(first[0], flip_chip(first[1]))
    second = add(second[0], flip_pair(second[1]))
    first = add(first[0], flip_pair(first[1]))
    second = add(second[0], flip_chip(second[1]))
    return jnp.concatenate([first, second], axis=1)


def mix(normed, codes, slot_weights, held, pick_first):
    pair_count = lax.axis_size("req") // 2
    first_slot = (lax.axis_index("req") * slot_weights.shape[0]).astype(jnp.int32).reshape(1)
    ext = jnp.concatenate([normed, codes], axis=1)
    pieces = [ext]
    for step in range(1, pair_count):
        source = ext
        if step == 2:
            source, *held[3:] = together(ext, *held[3:])
        pieces.append(turn_pairs(source, step))
    outgoing = pick_first(held)
    outgoing = after(outgoing, *pieces[1:])
    *pieces[2:], outgoing = together(*pieces[2:], outgoing)
    arrived = trade_columns(outgoing)
    total = None
    for begin in range(0, pair_count, 2):
        here = spread_tokens(pieces[begin : begin + 2])
        there = flip_core(here)
        back = flip_core(run_experts(first_slot, there, slot_weights, 256))
        if begin + 2 >= pair_count:
            here, arrived = together(here, arrived)
        mixed = run_experts(first_slot, here, slot_weights, 256)
        sums = gather_sums(add(mixed, back), 2)
        for offset in range(2):
            step = begin + offset
            part = sums[offset] if step == 0 else turn_pairs(sums[offset], -step)
            part = part.astype(jnp.float32)
            total = part if total is None else total + part
    return total, arrived, mixed


def spread_weights(slot_weights):
    me = lax.axis_index("req")
    half = lax.axis_size("req") // 2
    spot = me % half
    slots_here = slot_weights.shape[0]
    chunks = slot_weights.reshape(slots_here, half, -1, slot_weights.shape[-1])
    held = [pick(chunks, spot, 1)]
    for mask in range(1, half):
        held.append(swap(pick(chunks, spot ^ mask, 1), mask))
    return held


def pick_kernel(slots_here, index_ref, *refs):
    sources, out_ref = refs[:-1], refs[-1]
    holder = index_ref[pl.program_id(0)] // slots_here
    for k, source in enumerate(sources):

        @pl.when(holder == k)
        def _():
            out_ref[...] = source[...]


def take_chunks(held, index, begin, size):
    slots_here, _, width = held[0].shape
    count = index.shape[0]
    place = begin // size

    def block_of(k):
        def index_map(i, index):
            mine = index[i] // slots_here == k
            return (jnp.where(mine, index[i] % slots_here, 0), place, 0)

        return pl.BlockSpec((1, size, width), index_map)

    return pl.pallas_call(
        functools.partial(pick_kernel, slots_here),
        out_shape=jax.ShapeDtypeStruct((count, size, width), held[0].dtype),
        grid_spec=pltpu.PrefetchScalarGridSpec(
            num_scalar_prefetch=1,
            grid=(count,),
            in_specs=[block_of(k) for k in range(len(held))],
            out_specs=pl.BlockSpec((1, size, width), lambda i, index: (i, 0, 0)),
        ),
        compiler_params=pltpu.CompilerParams(vmem_limit_bytes=24 * 1024 * 1024),
        cost_estimate=pl.CostEstimate(
            flops=0, bytes_accessed=4 * count * size * width, transcendentals=0
        ),
    )(index, *held)


def trade_columns(outgoing):
    pair_count = lax.axis_size("req") // 2
    columns = [[2 * i + k for i in range(pair_count)] for k in range(2)]
    outgoing = outgoing.reshape((pair_count, 2) + outgoing.shape[1:])
    return lax.all_to_all(outgoing, "req", 0, 0, axis_index_groups=columns, tiled=True)


def chunk_index(source_slot, slots_here):
    half = lax.axis_size("req") // 2
    spots = source_slot // slots_here % half
    return ((lax.axis_index("req") % half) ^ spots) * slots_here + source_slot % slots_here


def collect_replicas(arrivals, source_slot, slots_here):
    me = lax.axis_index("req")
    half = lax.axis_size("req") // 2
    side = me % 2
    halves = source_slot // slots_here // half
    width = arrivals[0].shape[3]
    rows_all = sum(arrived.shape[2] for arrived in arrivals)
    result = jnp.zeros((half // 2, 2, rows_all, width), arrivals[0].dtype)
    first_row = 0
    for arrived in arrivals:
        size = arrived.shape[2]

        def wanted_by(receiver):
            begin = pick(halves, receiver, 0) * (half // 2)
            where = (begin, receiver % 2, 0, 0)
            return lax.dynamic_slice(arrived, where, (half // 2, 1, size, width))

        swapped = swap(wanted_by(me ^ 1), 1)
        for rows, column in ((wanted_by(me), side), (swapped, 1 - side)):
            result = lax.dynamic_update_slice(result, rows, (0, column, first_row, 0))
        first_row += size
    return result


def body(
    hidden_in,
    query_in,
    key_in,
    value_in,
    query_gain,
    key_gain,
    cache_keys,
    cache_values,
    cache_block,
    request_lengths,
    out_proj,
    norm_gain,
    expert_ids,
    gate_values,
    old_slots,
    new_replicas,
    slot_weights,
):
    req_count = lax.axis_size("req")
    exp_count = lax.axis_size("exp")
    group_idx = lax.axis_index("req")
    tok_grp, width_q = query_in.shape
    tok_dev, model_width = hidden_in.shape
    head_size = query_gain.shape[0]
    head_count = width_q // head_size
    cache_dev = cache_keys.shape[0]
    pre_len = cache_keys.shape[1]
    req_grp = request_lengths.shape[1]
    lengths = request_lengths[0]
    req_ends = jnp.cumsum(lengths)
    starts = req_ends - lengths
    places = jnp.arange(tok_grp, dtype=jnp.int32)
    member = (places[:, None] >= starts[None, :]) & (places[:, None] < req_ends[None, :])
    request_idx = jnp.arange(req_grp, dtype=jnp.int32)
    segment = jnp.sum(jnp.where(member, request_idx[None, :], 0), axis=1)
    offset = places - jnp.sum(jnp.where(member, starts[None, :], 0), axis=1)
    block_rows = cache_block.reshape(req_count, req_grp)
    my_blocks = lax.dynamic_index_in_dim(block_rows, group_idx, 0, keepdims=False)
    has_cache = my_blocks >= 0
    token_cached = jnp.sum(jnp.where(member & has_cache[None, :], 1, 0), axis=1) > 0
    position = (offset + jnp.where(token_cached, pre_len, 0)).astype(jnp.float32)
    need_blocks, need_requests = compact(block_rows, cache_dev)
    my_requests = lax.dynamic_index_in_dim(need_requests, group_idx, 0, keepdims=False)
    far_cache = fetch_cache(cache_keys, cache_values, need_blocks)
    far_keys, far_values = far_cache[:, 0], far_cache[:, 1]
    held = spread_weights(slot_weights)
    query_n = prepare(query_in.reshape(tok_grp, head_count, head_size), query_gain, position)
    key_n = prepare(key_in.reshape(tok_grp, head_count, head_size), key_gain, position)
    keyset = jnp.concatenate(
        [key_n, far_keys.reshape(cache_dev * pre_len, head_count, head_size)], axis=0
    )
    valueset = jnp.concatenate(
        [
            value_in.reshape(tok_grp, head_count, head_size),
            far_values.reshape(cache_dev * pre_len, head_count, head_size),
        ],
        axis=0,
    )
    key_request = jnp.concatenate([segment, jnp.repeat(my_requests, pre_len)])
    allowed = segment[:, None] == key_request[None, :]
    scores = jnp.einsum("qhd,khd->hqk", query_n, keyset, preferred_element_type=jnp.float32) * (
        1.0 / math.sqrt(head_size)
    )
    scores = jnp.where(allowed[None], scores, -1e30)
    peak = jnp.max(scores, axis=-1, keepdims=True)
    expos = jnp.exp(scores - peak)
    weights = (expos / jnp.sum(expos, axis=-1, keepdims=True)).astype(jnp.bfloat16)
    attended = jnp.einsum("hqk,khd->qhd", weights, valueset, preferred_element_type=jnp.float32)
    attended = attended.astype(jnp.bfloat16).reshape(tok_grp, width_q)
    attended, *held[1:3] = together(attended, *held[1:3])
    attn_out = sum_heads(jnp.dot(attended, out_proj, preferred_element_type=jnp.float32))
    residual = hidden_in.astype(jnp.float32) + attn_out
    normed = (
        residual
        * lax.rsqrt(jnp.mean(residual * residual, axis=-1, keepdims=True) + 1e-06)
        * norm_gain
    ).astype(jnp.bfloat16)
    slot_total = old_slots.shape[0]
    slot_range = jnp.arange(slot_total, dtype=jnp.int32)
    slot_of = jnp.sum(
        jnp.where(old_slots[None, :] == slot_range[:, None], slot_range[None, :], 0), axis=1
    )
    dense_gates = jnp.sum(
        jnp.where(expert_ids[:, :, None] == old_slots[None, None, :], gate_values[:, :, None], 0.0),
        axis=1,
    )
    high_part = dense_gates.astype(jnp.bfloat16)
    low_part = (dense_gates - high_part.astype(jnp.float32)).astype(jnp.bfloat16)
    lanes = max(64, slot_total)
    gap = ((0, 0), (0, lanes - slot_total))
    codes = jnp.concatenate([jnp.pad(high_part, gap), jnp.pad(low_part, gap)], axis=1)
    replica_onehot = new_replicas[:, None] == slot_range[None, :]
    source_slot = jnp.sum(jnp.where(replica_onehot, slot_of[None, :], 0), axis=1)
    slots_here = slot_weights.shape[0]
    index = chunk_index(source_slot, slots_here)
    size = held[0].shape[1] // 2
    normed, *held[3:] = together(normed, *held[3:])
    mixture, first, mixed = mix(
        normed, codes, slot_weights, held, lambda held: take_chunks(held, index, 0, size)
    )
    layer_out = (residual + mixture).astype(jnp.bfloat16)
    second = trade_columns(after(take_chunks(held, index, size, size), first))
    first = after(first, mixed)
    replica_weights = collect_replicas((first, second), source_slot, slots_here)
    return (layer_out, replica_weights.reshape((1,) + slot_weights.shape[1:]))


def solution(mesh):
    in_specs = (
        P(("req", "exp"), None),
        P("req", "exp"),
        P("req", "exp"),
        P("req", "exp"),
        P(),
        P(),
        P("req", None, "exp"),
        P("req", None, "exp"),
        P(),
        P("req", None),
        P("exp", None),
        P(),
        P(("req", "exp"), None),
        P(("req", "exp"), None),
        P(),
        P(),
        P("req", None, None, "exp"),
    )
    out_specs = (P(("req", "exp"), None), P("req", None, None, "exp"))
    return jax.shard_map(body, mesh=mesh, in_specs=in_specs, out_specs=out_specs, check_vma=False)
```
